32 devices in a mesh: batch: 2 (over core), seq: 4 (over y, x), head: 4 (over z).
Axes of the slice: x: 2, y: 2, z: 4, core: 2. Of those that a mesh axis runs over, the one named last changes fastest.
Arguments:
- tokens: bfloat16 [4096, 1024], P(('batch', 'seq', 'head')), may hold values from -6 to 6
- doc_ids: int32 [4096], P(('batch', 'seq')), may hold values from 0 to 2, as said below
- norm_gain: float32 [1024], replicated, may hold values from 0.1 to 1.9
- w_query: bfloat16 [1024, 1024], P(None, 'head'), may hold values from -0.1875 to 0.1875
- w_key: bfloat16 [1024, 2048], P(None, 'head'), may hold values from -0.1875 to 0.1875
- w_value: bfloat16 [1024, 2048], P(None, 'head'), may hold values from -0.1875 to 0.1875
- w_beta: bfloat16 [1024, 16], P(None, 'head'), may hold values from -0.1875 to 0.1875
- w_decay: bfloat16 [1024, 8], P(None, 'head'), may hold values from -0.1875 to 0.1875
- w_outgate: bfloat16 [1024, 1024], P(None, 'head'), may hold values from -0.1875 to 0.1875
- conv_query: bfloat16 [4, 1024], P(None, 'head'), may hold values from -3 to 3
- conv_key: bfloat16 [4, 2048], P(None, 'head'), may hold values from -1 to 1
- conv_value: bfloat16 [4, 2048], P(None, 'head'), may hold values from -3 to 3
- decay_log: float32 [8], P('head'), may hold values from -15 to -3
- out_gain: float32 [1024], P('head'), may hold values from 0.1 to 1.9
- w_out: bfloat16 [1024, 1024], P('head'), may hold values from -0.1875 to 0.1875
- mlp_gain: float32 [1024], replicated, may hold values from 0.1 to 1.9
- w_gate: bfloat16 [1024, 2816], replicated, may hold values from -0.1875 to 0.1875
- w_up: bfloat16 [1024, 2816], replicated, may hold values from -0.1875 to 0.1875
- w_down: bfloat16 [2816, 1024], replicated, may hold values from -0.109375 to 0.109375
- cotangent: bfloat16 [4096, 1024], P(('batch', 'seq', 'head')), may hold values from -6 to 6
Outputs:
- block_out: bfloat16 [4096, 1024], P(('batch', 'seq', 'head'))
- grad_tokens: float32 [4096, 1024], P(('batch', 'seq', 'head'))
- grad_norm_gain: float32 [1024], P(('batch', 'seq', 'head'))
- grad_w_query: float32 [1024, 1024], P(('batch', 'seq'), 'head')
- grad_w_key: float32 [1024, 2048], P(('batch', 'seq'), 'head')
- grad_w_value: float32 [1024, 2048], P(('batch', 'seq'), 'head')
- grad_w_beta: float32 [1024, 16], P(('batch', 'seq'), 'head')
- grad_w_decay: float32 [1024, 8], P(('batch', 'seq'), 'head')
- grad_w_outgate: float32 [1024, 1024], P(('batch', 'seq'), 'head')
- grad_conv_query: float32 [4, 1024], P(None, 'head')
- grad_conv_key: float32 [4, 2048], P(None, 'head')
- grad_conv_value: float32 [4, 2048], P(None, 'head')
- grad_decay_log: float32 [8], P('head')
- grad_out_gain: float32 [1024], P('head')
- grad_w_out: float32 [1024, 1024], P('head', ('batch', 'seq'))
- grad_mlp_gain: float32 [1024], P(('batch', 'seq', 'head'))
- grad_w_gate: float32 [1024, 2816], P(('batch', 'seq', 'head'))
- grad_w_up: float32 [1024, 2816], P(('batch', 'seq', 'head'))
- grad_w_down: float32 [2816, 1024], P(None, ('batch', 'seq', 'head'))
The draws below stay inside these ranges and needn't reach their ends.
Inputs may be any that keep to these rules, and one draw needn't show every extreme that they name: `doc_ids`: each stream of 2048 tokens (one index of batch) is packed: its ids start at 0 and never fall, and one of its documents covers tokens on every segment of the stream.
All inputs are finite; a program needn't handle non-finite values.
Results may differ from the reference program's by a relative error of at most 0.015.
Values may be sent and summed in bfloat16 or wider, within the bound.
No kernel may reach another device: no remote copies, remote signals or barrier semaphores. Data moves between devices by JAX's collectives and lax.ppermute only.
A program may use at most 192 MiB of HBM per device.

```python
import jax
import jax.numpy as jnp
from jax import lax

D = 1024
HEAD_TOTAL = 8
DK = 128
NH = 2
FF = 2816
TAPS = 4
SCAN_BLOCK_STEPS = 64
TOK_SEG = 512
STREAM = 2048
TOKENS = 4096


def draw_doc_ids(key, part):
    key = jax.random.fold_in(key, 7)
    first_key, last_key = jax.random.split(key)
    stream_count = TOKENS // STREAM
    starts = jax.random.randint(first_key, (stream_count, 1), 1, TOK_SEG)
    ends = STREAM - jax.random.randint(last_key, (stream_count, 1), 1, TOK_SEG)
    place = jnp.arange(STREAM, dtype=jnp.int32)[None, :]
    document_index = (place >= starts).astype(jnp.int32) + (place >= ends).astype(jnp.int32)
    return document_index.reshape(TOKENS)


def draw_conv_key(key, part):
    key = jax.random.fold_in(key, 11)
    tap_key, scale_key = jax.random.split(key)
    columns = HEAD_TOTAL * NH * DK
    taps = jnp.clip(0.5 * jax.random.normal(tap_key, (TAPS, columns), jnp.float32), -1.0, 1.0)
    column_scale = jnp.exp(jax.random.uniform(scale_key, (1, columns), jnp.float32, -6.9, 0.0))
    return (taps * column_scale).astype(jnp.bfloat16)


def block_levels(rng, shape, shards, smallest, top_value):
    def one(dim, blocks):
        steps = jax.random.uniform(jax.random.fold_in(jax.random.fold_in(rng, 6), dim), (blocks,), jnp.float32, smallest / len(shards), top_value / len(shards))
        return jnp.repeat(jnp.exp(steps), shape[dim] // blocks).reshape((-1,) + (1,) * (len(shape) - dim - 1))

    factor_of = one(*shards[0])
    for cut in shards[1:]:
        factor_of = factor_of * one(*cut)
    return factor_of


def gaussian(stream_key, shape, width, most, cuts=(), kind=jnp.bfloat16):
    factor_of = block_levels(stream_key, shape, cuts, -0.22, 0.18) if cuts else 1.0
    result = jax.random.normal(stream_key, shape, jnp.float32) * width * factor_of
    return jnp.minimum(jnp.maximum(result, -most), most).astype(kind)


def setup_inputs(seed: int = 0) -> dict:
    seeds = jax.random.split(jax.random.key(seed), 21)
    tokens = gaussian(seeds[0], (TOKENS, D), 1.0, 6.0, ((0, 32),))
    doc_ids = draw_doc_ids(jax.random.fold_in(seeds[20], 71), 0)
    norm_gain = jnp.clip(1.0 + 0.18 * jax.random.normal(seeds[2], (D,), jnp.float32), 0.1, 1.9)
    w_query = gaussian(seeds[3], (D, HEAD_TOTAL * DK), D ** -0.5, 0.1875, ((1, 4),))
    w_key = gaussian(seeds[4], (D, HEAD_TOTAL * NH * DK), D ** -0.5, 0.1875, ((1, 4),))
    w_value = gaussian(seeds[5], (D, HEAD_TOTAL * NH * DK), D ** -0.5, 0.1875, ((1, 4),))
    w_beta = gaussian(seeds[6], (D, HEAD_TOTAL * NH), D ** -0.5, 0.1875, ((1, 4),))
    w_decay = gaussian(seeds[7], (D, HEAD_TOTAL), D ** -0.5, 0.1875, ((1, 4),))
    w_outgate = gaussian(seeds[8], (D, HEAD_TOTAL * DK), D ** -0.5, 0.1875, ((1, 4),))
    conv_query = gaussian(seeds[9], (TAPS, HEAD_TOTAL * DK), TAPS ** -0.5, 3.0, ((1, 4),))
    conv_key = draw_conv_key(jax.random.fold_in(seeds[20], 71), 0)
    conv_value = gaussian(seeds[11], (TAPS, HEAD_TOTAL * NH * DK), TAPS ** -0.5, 3.0, ((1, 4),))
    decay_log = jnp.clip(-15.0 + 12.0 * jax.random.uniform(seeds[12], (HEAD_TOTAL,), jnp.float32) ** block_levels(seeds[12], (HEAD_TOTAL,), ((0, 4),), -0.2, 0.2), -15.0, -3.0)
    out_gain = jnp.clip(1.0 + 0.18 * jax.random.normal(seeds[13], (HEAD_TOTAL * DK,), jnp.float32), 0.1, 1.9)
    w_out = gaussian(seeds[14], (HEAD_TOTAL * DK, D), (HEAD_TOTAL * DK) ** -0.5, 0.1875, ((0, 4),))
    mlp_gain = jnp.clip(1.0 + 0.18 * jax.random.normal(seeds[15], (D,), jnp.float32), 0.1, 1.9)
    w_gate = gaussian(seeds[16], (D, FF), D ** -0.5, 0.1875)
    w_up = gaussian(seeds[17], (D, FF), D ** -0.5, 0.1875)
    w_down = gaussian(seeds[18], (FF, D), FF ** -0.5, 0.109375)
    cotangent = gaussian(seeds[19], (TOKENS, D), 1.0, 6.0, ((0, 32),))
    return {"tokens": tokens, "doc_ids": doc_ids, "norm_gain": norm_gain, "w_query": w_query, "w_key": w_key, "w_value": w_value, "w_beta": w_beta, "w_decay": w_decay, "w_outgate": w_outgate, "conv_query": conv_query, "conv_key": conv_key, "conv_value": conv_value, "decay_log": decay_log, "out_gain": out_gain, "w_out": w_out, "mlp_gain": mlp_gain, "w_gate": w_gate, "w_up": w_up, "w_down": w_down, "cotangent": cotangent}


eps = 1e-06
precise = lax.Precision.HIGHEST

@jax.custom_vjp
def low(v):
    return lax.optimization_barrier(v.astype(jnp.bfloat16)).astype(jnp.float32)

@jax.custom_vjp
def low_back(v):
    return v

def low_keep(v):
    return (low(v), None)

def low_pass(kept, grad):
    return (grad,)

def back_keep(v):
    return (v, None)

def back_low(kept, grad):
    return (low(grad),)
low.defvjp(low_keep, low_pass)
low_back.defvjp(back_keep, back_low)

def full_dot(left, right):
    return jnp.dot(left.astype(jnp.float32), right.astype(jnp.float32), precision=precise, preferred_element_type=jnp.float32)

def inverse_rms(rows):
    return lax.rsqrt(lax.optimization_barrier(jnp.mean(rows * rows, -1, keepdims=True)) + eps)

def doc_masks(own_ids, earlier_ids, conv_rows):
    extended = jnp.concatenate([earlier_ids, own_ids])
    length = own_ids.shape[0]
    return jnp.stack([(extended[conv_rows - 1 - delay:conv_rows - 1 - delay + length] == own_ids).astype(jnp.float32) for delay in range(conv_rows)])

def short_conv(rows, rim, kernel, same_document):
    conv_rows = kernel.shape[0]
    length = rows.shape[0]
    extended = jnp.concatenate([rim, rows], 0)
    total = jnp.zeros_like(rows)
    for delay in range(conv_rows):
        offset = conv_rows - 1 - delay
        total = total + kernel[delay][None, :] * extended[offset:offset + length] * same_document[delay][:, None]
    return total

def token_input_rows(query_before_conv, key_before_conv, value_before_conv, rim_query, rim_key, rim_value, strength_logit, forget_logit, query_filter_taps, key_filter_taps, value_filter_taps, forget_rates, same_document, head_count):
    length = query_before_conv.shape[0]
    query_rows = jax.nn.silu(short_conv(query_before_conv, rim_query, query_filter_taps, same_document)).reshape(length, head_count, -1)
    head_size = query_rows.shape[-1]
    key = jax.nn.silu(short_conv(key_before_conv, rim_key, key_filter_taps, same_document)).reshape(length, head_count, -1, head_size)
    key = key * lax.rsqrt(lax.optimization_barrier(jnp.sum(key * key, -1, keepdims=True)) + eps)
    value_rows = jax.nn.silu(short_conv(value_before_conv, rim_value, value_filter_taps, same_document)).reshape(length, head_count, -1, head_size)
    write_strength = jax.nn.sigmoid(strength_logit).reshape(length, head_count, -1)
    gate_logarithm = -jnp.exp(forget_rates)[None, :] * jax.nn.softplus(forget_logit)
    return (query_rows, key, value_rows, write_strength, gate_logarithm)

def lower_solve(system, right_side):
    return jax.scipy.linalg.solve_triangular(system, right_side, lower=True)

def delta_rule_sweep(query_rows, key, value_rows, write_strength, gate_logarithm, document_index, initial_state):
    length, step_count, head_size = key.shape
    wide = value_rows.shape[-1]
    block_list = length * step_count // SCAN_BLOCK_STEPS
    opening_step = (jnp.arange(step_count) == 0).astype(jnp.float32)
    last_step = (jnp.arange(step_count) == step_count - 1).astype(jnp.float32)
    keys = key.reshape(block_list, SCAN_BLOCK_STEPS, head_size)
    values = value_rows.reshape(block_list, SCAN_BLOCK_STEPS, wide)
    betas = write_strength.reshape(block_list, SCAN_BLOCK_STEPS)
    forget_factors = (gate_logarithm[:, None] * opening_step[None, :]).reshape(block_list, SCAN_BLOCK_STEPS)
    queries = (query_rows[:, None, :] * last_step[None, :, None]).reshape(block_list, SCAN_BLOCK_STEPS, head_size)
    doc_of = (document_index[:, None] + jnp.zeros((1, step_count), jnp.int32)).reshape(block_list, SCAN_BLOCK_STEPS)
    doc_before = jnp.concatenate([doc_of[:1, :1], doc_of[:-1, -1:]], 0)
    cumulative = jnp.cumsum(forget_factors, 1)
    positions = jnp.arange(SCAN_BLOCK_STEPS)
    lower_tri = positions[:, None] >= positions[None, :]
    strict = positions[:, None] > positions[None, :]
    same_document = (doc_of[:, :, None] == doc_of[:, None, :]) & lower_tri[None]
    spread = jnp.where(same_document, jnp.exp(jnp.where(lower_tri[None], cumulative[:, :, None] - cumulative[:, None, :], 0.0)), 0.0)
    carried = jnp.exp(cumulative) * (doc_of == doc_before).astype(jnp.float32)
    key_gram = jnp.einsum('cid,cjd->cij', keys, keys, precision=precise)
    system = jnp.eye(SCAN_BLOCK_STEPS, dtype=jnp.float32)[None] + jnp.where(strict[None], betas[:, :, None] * key_gram * spread, 0.0)
    right_side = jnp.concatenate([(betas * carried)[:, :, None] * keys, betas[:, :, None] * values], -1)
    solved = jax.vmap(lower_solve)(system, right_side)
    mix_keys = solved[:, :, :head_size]
    mix_values = solved[:, :, head_size:]
    scores = jnp.einsum('cid,cjd->cij', queries, keys, precision=precise) * spread
    reaching = queries * carried[:, :, None]
    tail_keys = keys * spread[:, -1, :, None]
    survive = carried[:, -1]

    def advance(carry_state, block_data):
        mix_k, mix_v, block_scores, block_reach, block_tail, block_keep = block_data
        fresh_rows = mix_v - jnp.dot(mix_k, carry_state, precision=precise)
        output_rows = jnp.dot(block_reach, carry_state, precision=precise) + jnp.dot(block_scores, fresh_rows, precision=precise)
        next_state = block_keep * carry_state + jnp.einsum('jd,jw->dw', block_tail, fresh_rows, precision=precise)
        return (next_state, output_rows)
    closing_state, output_rows = lax.scan(jax.checkpoint(advance), initial_state, (mix_keys, mix_values, scores, reaching, tail_keys, survive))
    return (output_rows.reshape(length, step_count, wide)[:, -1], closing_state)

def gate_norm(core_out, gate_pre, gain_heads):
    length, head_count, head_size = core_out.shape
    unit = core_out * inverse_rms(core_out)
    gate_rows = gate_pre.reshape(length, head_count, head_size)
    return (unit * gain_heads.reshape(head_count, head_size) * jax.nn.silu(gate_rows)).reshape(length, head_count * head_size)

def reference(tokens, doc_ids, norm_gain, w_query, w_key, w_value, w_beta, w_decay, w_outgate, conv_query, conv_key, conv_value, decay_log, out_gain, w_out, mlp_gain, w_gate, w_up, w_down, cotangent):
    params = tuple((item.astype(jnp.float32) for item in (tokens, norm_gain, w_query, w_key, w_value, w_beta, w_decay, w_outgate, conv_query, conv_key, conv_value, decay_log, out_gain, w_out, mlp_gain, w_gate, w_up, w_down)))
    stream_count = TOKENS // STREAM
    streams = doc_ids.reshape(stream_count, STREAM)

    def forward(block_in, gain_in, query_w, key_w, value_w, beta_w, decay_w, outgate_w, query_filter_taps, key_filter_taps, value_filter_taps, forget_rates, gain_heads, out_w, gain_mid, gate_w, up_w, down_w):
        normed = low(block_in * inverse_rms(block_in) * gain_in)

        def mixer(item):
            rows, stream_ids = item
            query_before_conv = low_back(low(full_dot(rows, query_w)))
            key_before_conv = low_back(low(full_dot(rows, key_w)))
            value_before_conv = low_back(low(full_dot(rows, value_w)))
            strength_logit = low_back(full_dot(rows, beta_w))
            forget_logit = low_back(full_dot(rows, decay_w))
            gate_pre = low_back(full_dot(rows, outgate_w))
            own_ids = stream_ids.astype(jnp.float32)
            same_document = doc_masks(own_ids, -jnp.ones((TAPS - 1,), jnp.float32), TAPS)
            border_thin = jnp.zeros((TAPS - 1, HEAD_TOTAL * DK), jnp.float32)
            border_wide = jnp.zeros((TAPS - 1, HEAD_TOTAL * NH * DK), jnp.float32)
            query_rows, key, value_rows, write_strength, gate_logarithm = token_input_rows(query_before_conv, key_before_conv, value_before_conv, border_thin, border_wide, border_wide, strength_logit, forget_logit, query_filter_taps, key_filter_taps, value_filter_taps, forget_rates, same_document, HEAD_TOTAL)
            initial_state = jnp.zeros((DK, DK), jnp.float32)

            def single_head(q_head, k_head, v_head, b_head, g_head):
                return delta_rule_sweep(q_head, k_head, v_head, b_head, g_head, stream_ids, initial_state)[0]
            mixer_core = jax.vmap(single_head, in_axes=1, out_axes=1)(query_rows, key, value_rows, write_strength, gate_logarithm)
            return low(gate_norm(mixer_core, gate_pre, gain_heads))
        gated = lax.map(mixer, (normed.reshape(stream_count, STREAM, D), streams)).reshape(TOKENS, HEAD_TOTAL * DK)
        branch = low_back(full_dot(gated, out_w))
        middle = block_in + branch
        normed_mid = low(middle * inverse_rms(middle) * gain_mid)
        gate = low_back(full_dot(normed_mid, gate_w))
        up = low_back(full_dot(normed_mid, up_w))
        act = low(jax.nn.silu(gate) * up)
        return middle + full_dot(act, down_w)
    block_out, back = jax.vjp(forward, *params)
    grads = back(cotangent.astype(jnp.float32))
    return (block_out.astype(jnp.bfloat16), grads[0], grads[1], grads[2], grads[3], grads[4], grads[5], grads[6], grads[7], grads[8], grads[9], grads[10], grads[11], grads[12], grads[13], grads[14], grads[15], grads[16], grads[17])
```

```python
import functools

import jax
import jax.numpy as jnp
from jax import lax
from jax.experimental import pallas as pl
from jax.experimental.pallas import tpu as pltpu
from jax.sharding import PartitionSpec as P

bf16, f32, i32 = jnp.bfloat16, jnp.float32, jnp.int32
EPS = 1e-06
CT = 64
RIM = 16
NN = ((1,), (0,))
NT = ((1,), (1,))
MIB = 1 << 20


def mm(a, b, dims=NN):
    return lax.dot_general(a, b, (dims, ((), ())), preferred_element_type=f32)


def split(x):
    high = x.astype(bf16)
    return high, (x - high.astype(f32)).astype(bf16)


def mm3(a, b, dims=NN):
    return mm(a[0], b[0], dims) + (mm(a[0], b[1], dims) + mm(a[1], b[0], dims))


def exact(a, b):
    return lax.dot_general(
        a, b, (NN, ((), ())), precision=lax.Precision.HIGHEST, preferred_element_type=f32
    )


def iota2(shape, dim):
    return lax.broadcasted_iota(i32, shape, dim)


def rows_of(c, size=CT, start=0):
    return pl.ds(pl.multiple_of(c * size + start, 16), size)


def near(c, start):
    return pl.ds(pl.multiple_of(c * CT + start, 8), CT + 8)


def step_order():
    size = 2 * CT
    row, col = iota2((size, size), 0), iota2((size, size), 1)
    row_tok, col_tok = row & (CT - 1), col & (CT - 1)
    later = jnp.where(row_tok > col_tok, row_tok ^ col_tok, 0)
    same_token = (row_tok == col_tok) & (row >= CT) & (col < CT)
    return row, col, later, same_token


def twice(x):
    return jnp.concatenate([x, x], 0)


def head_steps(ref, rows, h):
    return jnp.concatenate(
        [ref[rows, (2 * h + j) * 128 : (2 * h + j + 1) * 128] for j in range(2)], 0
    )


def decays(gam_ref, info, rows, h, nh):
    gcol = gam_ref[rows, 2 * nh + h : 2 * nh + h + 1]
    glast = gcol[CT - 1 : CT, :]
    carried = jnp.exp(gcol) * info[:, 4:5]
    tail = jnp.exp(jnp.minimum(glast - gcol, 0.0)) * info[:, 5:6]
    keep = carried[CT - 1 : CT, :]
    return gcol, carried, tail, keep


def forward_kernel(
    nh, count, me_ref, *refs
):
    tok_refs, refs = refs[:count], refs[count:]
    forward_body(nh, me_ref, tok_refs, *refs)


def forward_body(
    nh, me_ref, tok_refs, rim_ref, ng_ref, wq_ref, wk_ref, wv_ref, wg_ref, ws_ref, tq_ref, tk_ref, tv_ref,
    info_ref, drow_ref, rate_ref,
    normed_ref, pre_ref, conv_ref, gate_ref, q_ref, k_ref, v_ref, beta_ref, glog_ref, gam_ref, dec_ref,
    t_ref, w_ref, u_ref, reach_ref, score_ref, at_ref, bt_ref, st_ref,
):
    length = pre_ref.shape[0] - RIM
    nc = length // CT
    gain = ng_ref[...]
    count = len(tok_refs)
    each = tok_refs[0].shape[0]

    def normal(x):
        x = x.astype(f32)
        scale = lax.rsqrt(jnp.mean(x * x, -1, keepdims=True) + EPS)
        return (x * scale * gain).astype(bf16)

    normed_ref[0:RIM, :] = normal(rim_ref[...])

    for shift, tok_ref in enumerate(tok_refs):
        place = lax.rem(me_ref[0] + (count - shift), count) * each

        def norm_rows(c, carry):
            target = pl.ds(pl.multiple_of(place + c * CT + RIM, 16), CT)
            normed_ref[target, :] = normal(tok_ref[rows_of(c), :])
            return carry

        lax.fori_loop(0, each // CT, norm_rows, 0)
    nq = nh * 128
    groups = ((wq_ref, 0, nq), (wk_ref, nq, 2 * nq), (wv_ref, 3 * nq, 2 * nq))

    for weight, first, width in groups:
        pre_ref[0:RIM, first : first + width] = (
            mm(normed_ref[0:RIM, :], weight[...]).astype(bf16).astype(f32)
        )

    def project(i, carry):
        rows = rows_of(i, 256, RIM)
        block = normed_ref[rows, :]
        for weight, first, width in groups:
            pre_ref[rows, first : first + width] = mm(block, weight[...]).astype(bf16).astype(f32)
        plain = rows_of(i, 256)
        gate_ref[plain, :] = mm(block, wg_ref[...])
        glog_ref[plain, :] = mm(block, ws_ref[...])
        return carry

    lax.fori_loop(0, length // 256, project, 0)
    logits = glog_ref[...]
    beta_ref[...] = jax.nn.sigmoid(logits)
    soft = jnp.maximum(logits, 0.0) + jnp.log1p(jnp.exp(-jnp.abs(logits)))
    glog = rate_ref[...] * soft
    glog_ref[...] = glog
    tri = (iota2((CT, CT), 0) >= iota2((CT, CT), 1)).astype(f32)
    for c in range(nc):
        gam_ref[c * CT : (c + 1) * CT, :] = exact(tri, glog[c * CT : (c + 1) * CT, :])

    def conv_rows(c, carry):
        rows = rows_of(c)
        info = info_ref[rows_of(c, CT, RIM), :]
        mask = [info[:, m : m + 1] for m in range(4)]
        for tap_ref, first, count, kind in (
            (tq_ref, 0, nh, "q"), (tk_ref, nq, 2 * nh, "k"), (tv_ref, 3 * nq, 2 * nh, "v")
        ):
            for j in range(count):
                cols = slice(first + j * 128, first + (j + 1) * 128)
                mine = slice(j * 128, (j + 1) * 128)
                taps = tap_ref[:, mine].astype(f32)
                block = pre_ref[near(c, RIM - 8), cols]
                total = block[8:] * taps[0:1]
                for m in range(1, 4):
                    total = total + pltpu.roll(block, m, 0)[8:] * mask[m] * taps[m : m + 1]
                conv_ref[rows, cols] = total
                out = total * jax.nn.sigmoid(total)
                if kind == "k":
                    out = out * lax.rsqrt(jnp.sum(out * out, -1, keepdims=True) + EPS)
                {"q": q_ref, "k": k_ref, "v": v_ref}[kind][rows, mine] = out
        return carry

    lax.fori_loop(0, nc, conv_rows, 0)

    row, col, later, same_token = step_order()
    eye = (row == col).astype(f32)
    small_row, small_col = iota2((CT, CT), 0), iota2((CT, CT), 1)

    def prepare(c, carry):
        rows = rows_of(c)
        heads = range(nh)
        info = info_ref[rows_of(c, CT, RIM), :]
        doc_col = info[:, 6:7]
        doc_row = drow_ref[c]
        same = (doc_col == doc_row) & (small_row >= small_col)
        keys, keys2, systems, rhs, tails, keeps = [], [], [], [], [], []
        for h in heads:
            gcol, carried, tail, keep = decays(gam_ref, info, rows, h, nh)
            grow = jnp.sum(jnp.where(small_row == small_col, gcol, 0.0), 0, keepdims=True)
            decay = jnp.where(same, jnp.exp(jnp.minimum(gcol - grow, 0.0)), 0.0)
            wide = jnp.concatenate([decay, decay], 1)
            dec_ref[c, h] = wide
            key = head_steps(k_ref, rows, h)
            value = head_steps(v_ref, rows, h)
            beta = jnp.concatenate(
                [beta_ref[rows, 2 * h + j : 2 * h + j + 1] for j in range(2)], 0
            )
            key2 = split(key)
            gram = mm3(key2, key2, NT)
            query = q_ref[rows, h * 128 : (h + 1) * 128]
            score_ref[c, h] = mm3(split(query), key2, NT) * wide
            reach_ref[c, h] = query * carried
            systems.append(
                jnp.where((later > 0) | same_token, beta * gram * twice(wide), 0.0)
            )
            rhs.append(jnp.concatenate([beta * twice(carried) * key, beta * value], 1))
            tails.append(key * twice(tail))
            keeps.append(keep)
        inverse = [eye - jnp.where(same_token, n, 0.0) for n in systems]
        for level in range(6):
            part = (later >> level) == 1
            blocks = [split(jnp.where(part, n, 0.0)) for n in systems]
            inverse2 = [split(x) for x in inverse]
            first = [split(mm3(b, x)) for b, x in zip(blocks, inverse2)]
            inverse = [x - mm3(x2, y) for x, x2, y in zip(inverse, inverse2, first)]
        for h in heads:
            t_ref[c, h] = inverse[h]
            mixed = mm3(split(inverse[h]), split(rhs[h]))
            w_ref[c, h] = mixed[:, :128]
            u_ref[c, h] = mixed[:, 128:]
            product = mm3(split(jnp.transpose(mixed)), split(tails[h]))
            at_ref[c, h] = keeps[h] * eye - product[:128]
            bt_ref[c, h] = product[128:]
        return carry

    lax.fori_loop(0, nc, prepare, 0)

    for h in range(nh):
        st_ref[h, :128] = at_ref[0, h]
        st_ref[h, 128:] = bt_ref[0, h]

    def chain(c, carry):
        for h in range(nh):
            after = mm3(split(st_ref[h]), split(at_ref[c, h]))
            st_ref[h, :128] = after[:128]
            st_ref[h, 128:] = after[128:] + bt_ref[c, h]
        return carry

    lax.fori_loop(1, nc, chain, 0)


def output_kernel(nh, count, *refs):
    output_body(nh, refs[:count], *refs[count:])


def output_body(
    nh, map_refs, w_ref, u_ref, reach_ref, score_ref, at_ref, bt_ref, gate_ref, gain_ref, wout_ref,
    sin_ref, fresh_ref, core_ref, gated_ref, branch_ref,
):
    nc = w_ref.shape[0]
    states = []
    for h in range(nh):
        state = map_refs[0][h, 128:].astype(f32)
        for map_ref in map_refs[1:]:
            passed = split(map_ref[h, :128].astype(f32))
            state = mm3(split(state), passed) + map_ref[h, 128:].astype(f32)
        states.append(state)

    def advance(c, states):
        rows = rows_of(c)
        out = []
        for h in range(nh):
            cols = slice(h * 128, (h + 1) * 128)
            state = states[h]
            state2 = split(state)
            sin_ref[c, h] = state
            out.append(mm3(state2, split(at_ref[c, h])) + bt_ref[c, h])
            probe = jnp.concatenate([w_ref[c, h], reach_ref[c, h]], 0)
            seen = mm3(split(probe), state2, NT)
            fresh = u_ref[c, h] - seen[: 2 * CT]
            fresh_ref[c, h] = fresh
            core = seen[2 * CT :] + mm3(split(score_ref[c, h]), split(fresh))
            core_ref[rows, cols] = core
            unit = core * lax.rsqrt(jnp.mean(core * core, -1, keepdims=True) + EPS)
            gate = gate_ref[rows, cols]
            gated_ref[rows, cols] = (
                unit * gain_ref[:, cols] * (gate * jax.nn.sigmoid(gate))
            ).astype(bf16)
        return tuple(out)

    states = lax.fori_loop(0, nc, advance, tuple(states))
    for h in range(nh):
        sin_ref[nc, h] = states[h]
    branch_ref[...] = mm(gated_ref[...], wout_ref[...]).astype(bf16)


def adjoint_kernel(nh, count, me_ref, *refs):
    adjoint_body(nh, me_ref, refs[:count], *refs[count:])


def adjoint_body(
    nh, me_ref, g_refs, wout_ref, core_ref, gate_ref, gain_ref, score_ref, reach_ref, w_ref, at_ref,
    dcore_ref, dft_ref, dt_ref, dgate_ref, dgain_ref, local_ref,
    dgated_ref,
):
    nc = w_ref.shape[0]
    count = len(g_refs)
    each = g_refs[0].shape[0]
    for shift, g_ref in enumerate(g_refs):
        place = lax.rem(me_ref[0] + (count - shift), count) * each
        dgated_ref[pl.ds(pl.multiple_of(place, 16), each), :] = mm(g_ref[...], wout_ref[...], NT)

    def chunk(c, dgain):
        rows = rows_of(c)
        sums = []
        for h in range(nh):
            cols = slice(h * 128, (h + 1) * 128)
            core = core_ref[rows, cols]
            scale = lax.rsqrt(jnp.mean(core * core, -1, keepdims=True) + EPS)
            unit = core * scale
            gate = gate_ref[rows, cols]
            sig = jax.nn.sigmoid(gate)
            silu = gate * sig
            gain = gain_ref[:, cols]
            grad = dgated_ref[rows, cols]
            sums.append(jnp.sum(grad * unit * silu, 0, keepdims=True))
            dgate_ref[rows, cols] = grad * unit * gain * (sig * (1.0 + gate * (1.0 - sig)))
            dunit = grad * gain * silu
            dcore = scale * (dunit - unit * jnp.mean(dunit * unit, -1, keepdims=True))
            dcore_ref[rows, cols] = dcore
            across = jnp.transpose(dcore)
            dft = mm3(split(across), split(score_ref[c, h]))
            dft_ref[c, h] = dft
            left = jnp.concatenate([-dft, across], 1)
            right = jnp.concatenate([w_ref[c, h], reach_ref[c, h]], 0)
            dt_ref[c, h] = mm3(split(left), split(right))
        return dgain + jnp.concatenate(sums, 1)

    dgain_ref[...] = lax.fori_loop(0, nc, chunk, jnp.zeros(dgain_ref.shape, f32))

    def chain(i, carry):
        c = nc - 1 - i
        return tuple(
            mm3(split(carry[h]), split(at_ref[c, h]), NT) + dt_ref[c, h] for h in range(nh)
        )

    start = tuple(dt_ref[nc - 1, h] for h in range(nh))
    total = lax.fori_loop(1, nc, chain, start)
    for h in range(nh):
        local_ref[h] = total[h]


def backward_kernel(nh, count, *refs):
    backward_body(nh, refs[:count], refs[count : 2 * count], *refs[2 * count :])


def backward_body(
    nh, map_refs, local_refs, at_ref, dt_ref, dft_ref, dcore_ref, t_ref, fresh_ref, sin_ref,
    q_ref, k_ref, v_ref, beta_ref, gam_ref, dec_ref, conv_ref, pre_ref, info_ref, tq_ref, tk_ref, tv_ref,
    rate_ref, glog_ref, dgate_ref,
    gp_ref, rim_ref, tail_ref, taps_ref, dlog_ref,
    dconv_ref, small_ref,
):
    length = q_ref.shape[0]
    nc = length // CT
    nq = nh * 128
    width = 5 * nq
    ends = []
    for h in range(nh):
        end = local_refs[0][h].astype(f32)
        for map_ref, local_ref in zip(map_refs[1:], local_refs[1:]):
            passed = split(map_ref[h].astype(f32))
            end = mm3(split(end), passed, NT) + local_ref[h].astype(f32)
        ends.append(end)
    row, col, later, same_token = step_order()
    before = (later > 0) | same_token
    last_row = (iota2((CT, 1), 0) == CT - 1).astype(f32)
    dconv_ref[0:RIM, :] = jnp.zeros((RIM, width), f32)
    dconv_ref[RIM + length :, :] = jnp.zeros((RIM, width), f32)
    lane = iota2((CT, 128), 1)
    upper = (iota2((CT, CT), 0) <= iota2((CT, CT), 1)).astype(f32)

    def chunk(i, ends):
        c = nc - 1 - i
        rows = rows_of(c)
        store = rows_of(c, CT, RIM)
        info = info_ref[store, :]
        out = []
        small = jnp.zeros((CT, 128), f32)
        dgam = jnp.zeros((CT, 128), f32)
        for h in range(nh):
            cols = slice(h * 128, (h + 1) * 128)
            end = ends[h]
            end2 = split(end)
            out.append(mm3(end2, split(at_ref[c, h]), NT) + dt_ref[c, h])
            _, carried, tail, _ = decays(gam_ref, info, rows, h, nh)
            carried2, tail2 = twice(carried), twice(tail)
            key = head_steps(k_ref, rows, h)
            value = head_steps(v_ref, rows, h)
            query = q_ref[rows, cols]
            beta = jnp.concatenate(
                [beta_ref[rows, 2 * h + j : 2 * h + j + 1] for j in range(2)], 0
            )
            wide = dec_ref[c, h]
            full = jnp.where(before, twice(wide), 0.0)
            state = sin_ref[c, h]
            fresh = fresh_ref[c, h]
            fresh2 = split(fresh)
            dcore = dcore_ref[rows, cols]
            dft = dft_ref[c, h] + mm3(end2, split(key * tail2), NT)
            solved = jnp.transpose(mm3(split(dft), split(t_ref[c, h])))
            both = split(jnp.concatenate([solved, dcore], 0))
            through = mm3(both, split(state))
            pairs = mm3(both, fresh2, NT)
            dtail = mm3(fresh2, end2)
            em = -pairs[: 2 * CT] * full
            ps = pairs[2 * CT :] * wide
            mixed = mm3(split(jnp.concatenate([em, ps], 0)), split(key))
            turned = jnp.transpose(jnp.concatenate([beta * em, ps], 0))
            dkb = mm3(split(turned), split(jnp.concatenate([key, query], 0))) + tail2 * dtail
            x1 = mixed[: 2 * CT] - carried2 * through[: 2 * CT]
            dka = beta * x1
            dkey = dka + dkb
            dbeta = jnp.sum(key * x1 + solved * value, -1, keepdims=True)
            dvalue = beta * solved
            dquery = mixed[2 * CT :] + carried * through[2 * CT :]
            turn = jnp.sum(key * (dka - dkb), -1, keepdims=True)
            closing = jnp.sum(
                jnp.sum(end * sin_ref[c + 1, h], -1, keepdims=True), 0, keepdims=True
            )
            dg = (
                jnp.sum(query * dquery, -1, keepdims=True)
                + turn[:CT]
                + turn[CT:]
                + last_row * closing
            )
            dgam = jnp.where(lane == 2 * nh + h, dg, dgam)
            for j in range(2):
                small = jnp.where(lane == 2 * h + j, dbeta[j * CT : (j + 1) * CT], small)
            pre = conv_ref[rows, cols]
            sig = jax.nn.sigmoid(pre)
            dconv_ref[store, cols] = dquery * (sig * (1.0 + pre * (1.0 - sig)))
            for j in range(2):
                kcols = slice(nq + (2 * h + j) * 128, nq + (2 * h + j + 1) * 128)
                pre = conv_ref[rows, kcols]
                sig = jax.nn.sigmoid(pre)
                act = pre * sig
                scale = lax.rsqrt(jnp.sum(act * act, -1, keepdims=True) + EPS)
                unit = key[j * CT : (j + 1) * CT]
                grad = dkey[j * CT : (j + 1) * CT]
                grad = scale * (grad - unit * jnp.sum(unit * grad, -1, keepdims=True))
                dconv_ref[store, kcols] = grad * (sig * (1.0 + pre * (1.0 - sig)))
                vcols = slice(3 * nq + (2 * h + j) * 128, 3 * nq + (2 * h + j + 1) * 128)
                pre = conv_ref[rows, vcols]
                sig = jax.nn.sigmoid(pre)
                dconv_ref[store, vcols] = dvalue[j * CT : (j + 1) * CT] * (
                    sig * (1.0 + pre * (1.0 - sig))
                )
        dglog = exact(upper, dgam)
        small_ref[rows, :] = jnp.where(lane < 2 * nh, small, dglog)
        return tuple(out)

    lax.fori_loop(0, nc, chunk, tuple(ends))

    beta = beta_ref[...]
    small = small_ref[...]
    lanes = iota2(beta.shape, 1)
    grads = small * beta * jnp.where(lanes < 2 * nh, 1.0 - beta, rate_ref[...])
    dlog_ref[...] = jnp.sum(small * glog_ref[...], 0, keepdims=True)
    gp_ref[0:RIM, :] = jnp.zeros((RIM, gp_ref.shape[1]), bf16)
    gp_ref[RIM:, width : width + nq] = dgate_ref[...].astype(bf16)
    gp_ref[RIM:, width + nq :] = grads.astype(bf16)
    groups = ((tq_ref, 0, nh), (tk_ref, nq, 2 * nh), (tv_ref, 3 * nq, 2 * nh))

    def turned_back(grad, masks, taps, count):
        total = grad[:count] * taps[0:1]
        size = grad.shape[0]
        for m in range(1, 4):
            moved = pltpu.roll(grad * masks[:, m : m + 1], size - m, 0)
            total = total + moved[:count] * taps[m : m + 1]
        return total

    def conv_back(c, sums):
        info = info_ref[near(c, RIM), :]
        new = []
        for tap_ref, first, count in groups:
            for j in range(count):
                cols = slice(first + j * 128, first + (j + 1) * 128)
                taps = tap_ref[:, j * 128 : (j + 1) * 128].astype(f32)
                grad = dconv_ref[near(c, RIM), cols]
                gp_ref[rows_of(c, CT, RIM), cols] = turned_back(grad, info, taps, CT).astype(bf16)
                block = pre_ref[near(c, RIM - 8), cols]
                parts = [jnp.sum(grad[:CT] * block[8:], 0, keepdims=True)]
                for m in range(1, 4):
                    moved = pltpu.roll(block, m, 0)[8:]
                    parts.append(
                        jnp.sum(grad[:CT] * info[:CT, m : m + 1] * moved, 0, keepdims=True)
                    )
                new.append(jnp.concatenate(parts, 0))
        return sums + jnp.concatenate(new, 1)

    taps_ref[...] = lax.fori_loop(0, nc, conv_back, jnp.zeros((4, width), f32))
    for tap_ref, first, count in groups:
        cols = slice(first, first + count * 128)
        taps = tap_ref[...].astype(f32)
        early = slice(8, 24)
        rim = turned_back(dconv_ref[early, cols], info_ref[early, :], taps, 8)
        rim_ref[:, cols] = rim
        gp_ref[0:RIM, cols] = jnp.concatenate([jnp.zeros_like(rim), rim], 0).astype(bf16)
        late = slice(length, length + 24)
        tail_ref[:, cols] = turned_back(dconv_ref[late, cols], info_ref[late, :], taps, 16)


VMEM = pl.BlockSpec(memory_space=pltpu.VMEM)
SMEM = pl.BlockSpec(memory_space=pltpu.SMEM)


def kernel_call(body, name, args, outs, scratch=(), flops=0, mib=60):
    moved = sum(a.size * a.dtype.itemsize for a in args) + sum(
        s.size * s.dtype.itemsize for s in outs
    )
    return pl.pallas_call(
        body,
        name=name,
        in_specs=[SMEM if a.dtype == i32 else VMEM for a in args],
        out_specs=[VMEM] * len(outs),
        out_shape=outs,
        scratch_shapes=list(scratch),
        compiler_params=pltpu.CompilerParams(vmem_limit_bytes=mib * MIB),
        cost_estimate=pl.CostEstimate(flops=flops, bytes_accessed=moved, transcendentals=0),
    )(*args)


def sds(*shape, dtype=f32):
    return jax.ShapeDtypeStruct(shape, dtype)


def mixer_forward(me, tokens, rim, norm_gain, weights, taps, info, doc_rows, rate):
    length, width = tokens[0].shape
    length *= len(tokens)
    w_query, w_key, w_value, w_outgate, w_small = weights
    nh = w_query.shape[1] // 128
    nc, nq = length // CT, nh * 128
    per = (nc, nh)
    outs = dict(
        normed=sds(RIM + length, width, dtype=bf16),
        pre=sds(RIM + length, 5 * nq),
        conv=sds(length, 5 * nq),
        gate=sds(length, nq),
        q=sds(length, nq),
        k=sds(length, 2 * nq),
        v=sds(length, 2 * nq),
        beta=sds(length, 128),
        glog=sds(length, 128),
        gam=sds(length, 128),
        dec=sds(*per, CT, 128),
        t=sds(*per, 128, 128),
        w=sds(*per, 128, 128),
        u=sds(*per, 128, 128),
        reach=sds(*per, CT, 128),
        score=sds(*per, CT, 128),
        at=sds(*per, 128, 128),
        bt=sds(*per, 128, 128),
        st=sds(nh, 256, 128),
    )
    args = (me, *tokens, rim, norm_gain, w_query, w_key, w_value, w_outgate, w_small, *taps, info, doc_rows, rate)
    flops = 2 * length * width * 7 * nq + nc * nh * 60 * 2 * 128**3
    res = kernel_call(
        functools.partial(forward_kernel, nh, len(tokens)), "mixer_forward", args, list(outs.values()), flops=flops
    )
    return dict(zip(outs, res))


def mixer_output(maps, fwd, out_gain, w_out):
    nc, nh = fwd["w"].shape[:2]
    length = nc * CT
    outs = dict(
        sin=sds(nc + 1, nh, 128, 128),
        fresh=sds(nc, nh, 128, 128),
        core=sds(length, nh * 128),
        gated=sds(length, nh * 128, dtype=bf16),
        branch=sds(length, w_out.shape[1], dtype=bf16),
    )
    args = (*maps, *(fwd[n] for n in ("w", "u", "reach", "score", "at", "bt", "gate")), out_gain, w_out)
    res = kernel_call(
        functools.partial(output_kernel, nh, len(maps)), "mixer_output", args, list(outs.values()),
        flops=nc * nh * 12 * 2 * 128**3,
    )
    return dict(zip(outs, res))


def mixer_adjoint(me, grad, w_out, fwd, out, out_gain):
    nc, nh = fwd["w"].shape[:2]
    length = nc * CT
    outs = dict(
        dcore=sds(length, nh * 128),
        dft=sds(nc, nh, 128, 128),
        dt=sds(nc, nh, 128, 128),
        dgate=sds(length, nh * 128),
        dgain=sds(1, nh * 128),
        local=sds(nh, 128, 128),
    )
    args = (me, *grad, w_out, out["core"], fwd["gate"], out_gain, fwd["score"], fwd["reach"], fwd["w"], fwd["at"])
    res = kernel_call(
        functools.partial(adjoint_kernel, nh, len(grad)), "mixer_adjoint", args, list(outs.values()),
        scratch=[pltpu.VMEM((length, nh * 128), f32)],
        flops=nc * nh * 8 * 2 * 128**3,
    )
    return dict(zip(outs, res))


def mixer_backward(maps, local_sums, fwd, out, adj, info, taps, rate):
    nc, nh = fwd["w"].shape[:2]
    length, nq = nc * CT, nh * 128
    width = 5 * nq
    outs = dict(
        gp=sds(RIM + length, width + nq + 128, dtype=bf16),
        rim=sds(8, width),
        tail=sds(16, width),
        taps=sds(4, width),
        dlog=sds(1, 128),
    )
    args = (
        *maps, *local_sums, fwd["at"], adj["dt"], adj["dft"], adj["dcore"], fwd["t"], out["fresh"], out["sin"],
        *(fwd[n] for n in ("q", "k", "v", "beta", "gam", "dec", "conv", "pre")), info, *taps, rate,
        fwd["glog"], adj["dgate"],
    )
    res = kernel_call(
        functools.partial(backward_kernel, nh, len(maps)), "mixer_backward", args, list(outs.values()),
        scratch=[pltpu.VMEM((length + 2 * RIM, width), f32), pltpu.VMEM((length, 128), f32)],
        flops=nc * nh * 36 * 2 * 128**3,
    )
    return dict(zip(outs, res))


def token_info(doc_ids, rim_ids):
    ids = doc_ids.astype(f32)
    length = ids.shape[0]
    extended = jnp.concatenate([rim_ids.astype(f32), ids])
    masks = [(extended[3 - m : 3 - m + length] == ids).astype(f32) for m in range(4)]
    blocks = ids.reshape(-1, CT)
    last = blocks[:, -1:]
    previous = jnp.concatenate([rim_ids[-1:].astype(f32)[None], last[:-1]], 0)
    columns = masks + [
        (blocks == previous).astype(f32).reshape(-1),
        (blocks == last).astype(f32).reshape(-1),
        ids,
        jnp.zeros_like(ids),
    ]
    info = jnp.pad(jnp.stack(columns, 1), ((RIM, RIM), (0, 0)))
    return info, blocks[:, None, :]


def middle_kernel(count, tok_ref, *refs):
    parts, (gain_ref, middle_ref, normed_ref) = refs[:count], refs[count:]
    middle = tok_ref[...].astype(f32)
    total = parts[0][...].astype(f32)
    for part in parts[1:]:
        total = total + part[...].astype(f32)
    middle = middle + total
    middle_ref[...] = middle
    scale = lax.rsqrt(jnp.mean(middle * middle, -1, keepdims=True) + EPS)
    normed_ref[...] = (middle * scale * gain_ref[...]).astype(bf16)


def feed_kernel(
    own_ref, near_ref, far_ref, cot_ref, gate_w, up_w, down_w,
    x_ref, act_ref, ggate_ref, gup_ref, gnorm_ref, block_ref,
):
    each = own_ref.shape[0]
    x_ref[0:each, :] = own_ref[...]
    x_ref[each : 2 * each, :] = near_ref[...]
    x_ref[2 * each :, :] = far_ref[...]

    def rows(i, carry):
        at = rows_of(i, 2 * each)
        x = x_ref[at, :]
        gate = mm(x, gate_w[...])
        up = mm(x, up_w[...])
        sig = jax.nn.sigmoid(gate)
        silu = gate * sig
        act = (silu * up).astype(bf16)
        act_ref[at, :] = act
        grad = mm(cot_ref[at, :], down_w[...], NT)
        ggate = (grad * up * sig * (1.0 + gate * (1.0 - sig))).astype(bf16)
        gup = (grad * silu).astype(bf16)
        ggate_ref[at, :] = ggate
        gup_ref[at, :] = gup
        gnorm_ref[at, :] = (mm(ggate, gate_w[...], NT) + mm(gup, up_w[...], NT)).astype(bf16)
        block_ref[at, :] = mm(act, down_w[...]).astype(bf16)
        return carry

    lax.fori_loop(0, 2, rows, 0)


def norm_back(grad_normed, rows, gain):
    scale = lax.rsqrt(jnp.mean(rows * rows, -1, keepdims=True) + EPS)
    unit = rows * scale
    scaled = grad_normed * gain
    grad_rows = scale * (scaled - unit * jnp.mean(scaled * unit, -1, keepdims=True))
    return grad_rows, jnp.sum(grad_normed * unit, 0, keepdims=True)


def middle_back_kernel(a_ref, b_ref, c_ref, middle_ref, cot_ref, gain_ref, grad_ref, low_ref, sum_ref):
    total = a_ref[...].astype(f32) + b_ref[...].astype(f32) + c_ref[...].astype(f32)
    rows, sum_ref[...] = norm_back(total, middle_ref[...], gain_ref[...])
    grad = cot_ref[...].astype(f32) + rows
    grad_ref[...] = grad
    low_ref[...] = grad.astype(bf16)


def tokens_back_kernel(count, *refs):
    parts, (tok_ref, gain_ref, middle_ref, grad_ref) = refs[:count], refs[count:]
    total = parts[0][...].astype(f32)
    for part in parts[1:]:
        total = total + part[...].astype(f32)
    rows, _ = norm_back(total, tok_ref[...].astype(f32), gain_ref[...])
    grad_ref[...] = middle_ref[...] + rows


def normed_back_kernel(gp_ref, tail_ref, late_ref, w_ref, normed_ref, gain_ref, out_ref, sum_ref, full_ref):
    length = out_ref.shape[0]
    width = tail_ref.shape[1]
    last = slice(length, length + RIM)
    full_ref[...] = gp_ref[...]
    late = jnp.concatenate([jnp.zeros_like(late_ref), late_ref[...]], 0)
    full_ref[last, 0:width] = (tail_ref[...] + late).astype(bf16)

    def rows(i, total):
        grad = mm(full_ref[rows_of(i, 256, RIM), :], w_ref[...], NT)
        out_ref[rows_of(i, 256), :] = grad.astype(bf16)
        unit = normed_ref[rows_of(i, 256, RIM), :].astype(f32)
        return total + jnp.sum(grad * unit, 0, keepdims=True)

    total = lax.fori_loop(0, length // 256, rows, jnp.zeros(sum_ref.shape, f32))
    sum_ref[...] = total / gain_ref[...]


def ring(value, axis):
    count = lax.axis_size(axis)
    return [value] + [
        lax.ppermute(value, axis, [(i, (i + shift) % count) for i in range(count)])
        for shift in range(1, count)
    ]


def along(value, axis, shift):
    count = lax.axis_size(axis)
    pairs = [(i, i + shift) for i in range(count) if 0 <= i + shift < count]
    return lax.ppermute(value, axis, pairs)


def crossed(value, axis, bit=0):
    return lax.ppermute(value, axis, [(i, i ^ (1 << bit)) for i in range(lax.axis_size(axis))])


def ring_scatter(value, axis):
    count, me = lax.axis_size(axis), lax.axis_index(axis)
    blocks = value.reshape((count, -1) + value.shape[1:])

    def block(place):
        return lax.dynamic_index_in_dim(blocks, lax.rem(place, count), 0, False)

    return [block(me)] + [
        lax.ppermute(block(me + shift), axis, [(i, (i + shift) % count) for i in range(count)])
        for shift in range(1, count)
    ]


def add_up(parts):
    total = parts[0].astype(f32)
    for part in parts[1:]:
        total = total + part.astype(f32)
    return total


def sum_over(value, axis):
    return add_up(ring(value, axis))


def halved(value, dim, axis, bit):
    mine = (lax.axis_index(axis) >> bit) & 1
    given = lax.dynamic_slice_in_dim(value, 1 - mine, 1, dim)
    kept = lax.dynamic_slice_in_dim(value, mine, 1, dim)
    got = crossed(given, axis, bit)
    return (kept.astype(f32) + got.astype(f32)).astype(bf16)


def in_order(own, other, axis):
    first = (lax.axis_index(axis) & 1) == 0
    return [jnp.where(first, own, other), jnp.where(first, other, own)]


def bits_of(count):
    return count.bit_length() - 1


def rows_dot(left, right):
    return lax.dot_general(
        left, right, (((0,), (0,)), ((), ())), preferred_element_type=f32
    )


def on_device(
    tokens, doc_ids, norm_gain, w_query, w_key, w_value, w_beta, w_decay, w_outgate, conv_query,
    conv_key, conv_value, decay_log, out_gain, w_out, mlp_gain, w_gate, w_up, w_down, cotangent,
):
    head_n, seq_n, batch_n = (lax.axis_size(a) for a in ("head", "seq", "batch"))
    me = lax.axis_index("head")
    nh = w_decay.shape[1]
    nq = nh * 128
    each, model = tokens.shape
    length = each * head_n
    me_array = me.astype(i32).reshape(1)

    blocks = ring(tokens, "head")
    rim = jnp.zeros((RIM, model), bf16)
    for target in range(head_n):
        rim = rim + lax.ppermute(
            tokens[-RIM:],
            ("seq", "head"),
            [
                (s * head_n + head_n - 1, (s + 1) * head_n + target)
                for s in range(seq_n - 1)
            ],
        )
    rim_ids = along(doc_ids[-3:], "seq", 1)
    info, doc_rows = token_info(doc_ids, rim_ids)
    w_small = jnp.pad(
        jnp.concatenate([w_beta, w_decay], 1), ((0, 0), (0, 128 - 3 * nh))
    )
    rate = jnp.pad(-jnp.exp(decay_log), (2 * nh, 128 - 3 * nh))[None]
    weights = (w_query, w_key, w_value, w_outgate, w_small)
    taps = (conv_query, conv_key, conv_value)
    gain = norm_gain[None]
    fwd = mixer_forward(me_array, blocks, rim, gain, weights, taps, info, doc_rows, rate)

    state = fwd["st"]
    earlier = [along(state, "seq", s) for s in range(seq_n - 1, 0, -1)]
    out = mixer_output(earlier, fwd, out_gain[None], w_out)

    parts = ring_scatter(out["branch"], "head")
    middle, normed_mid = kernel_call(
        functools.partial(middle_kernel, len(parts)), "middle",
        (tokens, *parts, mlp_gain[None]),
        [sds(each, model), sds(each, model, dtype=bf16)],
    )
    near = crossed(normed_mid, "head")
    far = crossed(jnp.concatenate([normed_mid, near], 0), "batch")
    cot_pair = jnp.concatenate([cotangent, crossed(cotangent, "head")], 0)
    cot_all = jnp.concatenate([cot_pair, crossed(cot_pair, "batch")], 0)
    ways = 2 * batch_n
    hidden = w_gate.shape[1] // ways
    mine = ((me & 1) * batch_n + lax.axis_index("batch")) * hidden
    gate_w = lax.dynamic_slice_in_dim(w_gate, mine, hidden, 1)
    up_w = lax.dynamic_slice_in_dim(w_up, mine, hidden, 1)
    down_w = lax.dynamic_slice_in_dim(w_down, mine, hidden, 0)
    rows = 4 * each
    x_all, act, ggate, gup, gnorm, block_part = kernel_call(
        feed_kernel, "feed",
        (normed_mid, near, far, cot_all, gate_w, up_w, down_w),
        [
            sds(rows, model, dtype=bf16),
            *[sds(rows, hidden, dtype=bf16)] * 3,
            *[sds(rows, model, dtype=bf16)] * 2,
        ],
        flops=12 * rows * model * hidden,
    )

    def own_parts(value):
        pair = value[: 2 * each]
        other = crossed(value[2 * each :], "batch")
        given = (pair[each:].astype(f32) + other[each:].astype(f32)).astype(bf16)
        return pair[:each], other[:each], crossed(given, "head")

    grad_middle, grad_branch, grad_mlp_gain = kernel_call(
        middle_back_kernel, "middle_back",
        (*own_parts(gnorm), middle, cotangent, mlp_gain[None]),
        [sds(each, model), sds(each, model, dtype=bf16), sds(1, model)],
    )
    block_out = (middle + add_up(own_parts(block_part))).astype(bf16)

    grad_blocks = ring(grad_branch, "head")
    adj = mixer_adjoint(me_array, grad_blocks, w_out, fwd, out, out_gain[None])
    later_maps = [along(state[:, :128], "seq", -s) for s in range(seq_n - 1, 0, -1)]
    later = [along(adj["local"], "seq", -s) for s in range(seq_n - 1, 0, -1)]
    back = mixer_backward(later_maps, later, fwd, out, adj, info, taps, rate)
    late_rim = along(back["rim"], "seq", -1)
    w_all = jnp.concatenate(weights, 1)
    partial_normed, gain_part = kernel_call(
        normed_back_kernel, "normed_back",
        (back["gp"], back["tail"], late_rim, w_all, fwd["normed"], gain),
        [sds(length, model, dtype=bf16), sds(1, model)],
        scratch=[pltpu.VMEM(back["gp"].shape, bf16)],
        flops=2 * length * model * w_all.shape[1],
    )
    normed_parts = ring_scatter(partial_normed, "head")
    (grad_tokens,) = kernel_call(
        functools.partial(tokens_back_kernel, len(normed_parts)), "tokens_back",
        (*normed_parts, tokens, gain, grad_middle),
        [sds(each, model)],
    )

    def mixer_rows(partial):
        spread = partial.reshape((2, -1) + partial.shape[1:])
        half = halved(spread, 0, "batch", 0)[0]
        return add_up(ring_scatter(half, "seq"))

    grad_weights = mixer_rows(rows_dot(fwd["normed"], back["gp"]).astype(bf16))
    g_all = jnp.concatenate(grad_blocks[:1] + grad_blocks[:0:-1], 0)
    g_all = lax.dynamic_slice_in_dim(
        jnp.concatenate([g_all, g_all], 0), (head_n - me) * each, length, 0
    )
    grad_w_out = mixer_rows(rows_dot(g_all, out["gated"]).astype(bf16)).T

    seq_bits, pair_bits = bits_of(seq_n), bits_of(head_n) - 1
    own_rows = model // (batch_n * seq_n * head_n)
    dims = (batch_n,) + (2,) * (seq_bits + pair_bits + 1)

    def feed_rows(partial, order):
        value = partial.reshape(dims + (own_rows, partial.shape[1]))
        for bit in order:
            value = halved(value, seq_bits - bit, "seq", bit)
        for bit in range(pair_bits, 0, -1):
            value = halved(value, 1 + seq_bits + pair_bits - bit, "head", bit)
        value = value.reshape((batch_n, 2) + value.shape[-2:])
        mine = me & 1
        given = lax.dynamic_index_in_dim(value, 1 - mine, 1, False)
        kept = lax.dynamic_index_in_dim(value, mine, 1, False)
        pair = jnp.stack(in_order(kept, crossed(given, "head"), "head"), 1)
        core = lax.axis_index("batch")
        given = lax.dynamic_index_in_dim(pair, 1 - core, 0, False)
        kept = lax.dynamic_index_in_dim(pair, core, 0, False)
        quad = jnp.stack(in_order(kept, crossed(given, "batch"), "batch"), 1)
        return quad.reshape((ways,) + quad.shape[2:])

    up_order = list(range(seq_bits))
    in_parts = rows_dot(x_all, jnp.concatenate([ggate, gup], 1)).astype(bf16)
    down_part = rows_dot(cot_all, act).astype(bf16)
    in_rows = feed_rows(in_parts, up_order)
    down_rows = feed_rows(down_part, up_order[::-1])

    def joined(value):
        return jnp.swapaxes(value, 0, 1).reshape(own_rows, -1).astype(f32)

    grad_w_gate = joined(in_rows[..., :hidden])
    grad_w_up = joined(in_rows[..., hidden:])
    grad_w_down = joined(down_rows).T

    width = 5 * nq
    wide = max(width, model)

    def padded(value):
        return jnp.pad(value, ((0, 0), (0, wide - value.shape[1])))

    small = jnp.concatenate(
        [padded(v) for v in (back["taps"], back["dlog"], adj["dgain"], grad_mlp_gain, gain_part)], 0
    )
    small = sum_over(sum_over(small, "batch"), "seq")
    gains = sum_over(small[6:8, :model], "head")
    index = (lax.axis_index("batch") * seq_n + lax.axis_index("seq")) * head_n + me
    gains = lax.dynamic_slice_in_dim(gains, index * own_rows, own_rows, 1)

    cols = [0, nq, 3 * nq, 5 * nq, 6 * nq, 6 * nq + 2 * nh, 6 * nq + 3 * nh]
    grad_q, grad_k, grad_v, grad_g, grad_b, grad_d = (
        grad_weights[:, a:b] for a, b in zip(cols[:-1], cols[1:])
    )
    return (
        block_out, grad_tokens, gains[1], grad_q, grad_k, grad_v, grad_b, grad_d, grad_g,
        small[0:4, :nq], small[0:4, nq : 3 * nq], small[0:4, 3 * nq : width],
        small[4, 2 * nh : 3 * nh], small[5, :nq], grad_w_out, gains[0], grad_w_gate, grad_w_up,
        grad_w_down,
    )


def solution(mesh):
    return jax.shard_map(
        on_device,
        mesh=mesh,
        in_specs=(
            P(("batch", "seq", "head"), None),
            P(("batch", "seq")),
            P(),
            P(None, "head"),
            P(None, "head"),
            P(None, "head"),
            P(None, "head"),
            P(None, "head"),
            P(None, "head"),
            P(None, "head"),
            P(None, "head"),
            P(None, "head"),
            P("head"),
            P("head"),
            P("head", None),
            P(),
            P(),
            P(),
            P(),
            P(("batch", "seq", "head"), None),
        ),
        out_specs=(
            P(("batch", "seq", "head"), None),
            P(("batch", "seq", "head"), None),
            P(("batch", "seq", "head")),
            P(("batch", "seq"), "head"),
            P(("batch", "seq"), "head"),
            P(("batch", "seq"), "head"),
            P(("batch", "seq"), "head"),
            P(("batch", "seq"), "head"),
            P(("batch", "seq"), "head"),
            P(None, "head"),
            P(None, "head"),
            P(None, "head"),
            P("head"),
            P("head"),
            P("head", ("batch", "seq")),
            P(("batch", "seq", "head")),
            P(("batch", "seq", "head"), None),
            P(("batch", "seq", "head"), None),
            P(None, ("batch", "seq", "head")),
        ),
        check_vma=False,
    )
```

```python
import functools

import jax
import jax.numpy as jnp
from jax import lax
from jax.experimental import pallas as pl
from jax.experimental.pallas import tpu as pltpu
from jax.sharding import Mesh
from jax.sharding import PartitionSpec as P

bf16, f32, i32 = jnp.bfloat16, jnp.float32, jnp.int32
EPS = 1e-06
CT = 64
RIM = 16
NN = ((1,), (0,))
NT = ((1,), (1,))
MIB = 1 << 20
FORWARD, OUTPUT, ADJOINT, BACKWARD = 4, 4, 4, 4


def mm(a, b, dims=NN):
    return lax.dot_general(a, b, (dims, ((), ())), preferred_element_type=f32)


def split(x):
    high = x.astype(bf16)
    return high, (x - high.astype(f32)).astype(bf16)


def mm3(a, b, dims=NN):
    return mm(a[0], b[0], dims) + (mm(a[0], b[1], dims) + mm(a[1], b[0], dims))


def exact(a, b):
    return lax.dot_general(
        a, b, (NN, ((), ())), precision=lax.Precision.HIGHEST, preferred_element_type=f32
    )


def iota2(shape, dim):
    return lax.broadcasted_iota(i32, shape, dim)


def rows_of(c, size=CT, start=0):
    return pl.ds(pl.multiple_of(c * size + start, 16), size)


def near(c, start):
    return pl.ds(pl.multiple_of(c * CT + start, 8), CT + 8)


def step_order():
    size = 2 * CT
    row, col = iota2((size, size), 0), iota2((size, size), 1)
    row_tok, col_tok = row & (CT - 1), col & (CT - 1)
    later = jnp.where(row_tok > col_tok, row_tok ^ col_tok, 0)
    same_token = (row_tok == col_tok) & (row >= CT) & (col < CT)
    return row, col, later, same_token


def twice(x):
    return jnp.concatenate([x, x], 0)


def head_steps(ref, rows, h):
    return jnp.concatenate(
        [ref[rows, (2 * h + j) * 128 : (2 * h + j + 1) * 128] for j in range(2)], 0
    )


def decays(gam_ref, info, rows, h, nh):
    gcol = gam_ref[rows, 2 * nh + h : 2 * nh + h + 1]
    glast = gcol[CT - 1 : CT, :]
    carried = jnp.exp(gcol) * info[:, 4:5]
    tail = jnp.exp(jnp.minimum(glast - gcol, 0.0)) * info[:, 5:6]
    keep = carried[CT - 1 : CT, :]
    return gcol, carried, tail, keep


def forward_kernel(
    nh, count, me_ref, *refs
):
    tok_refs, refs = refs[:count], refs[count:]
    forward_body(nh, me_ref, tok_refs, *refs)


def forward_body(
    nh, me_ref, tok_refs, rim_ref, ng_ref, wq_ref, wk_ref, wv_ref, wg_ref, ws_ref, tq_ref, tk_ref, tv_ref,
    flags_ref, drow_ref, rate_ref,
    normed_ref, pre_ref, conv_ref, gate_ref, q_ref, k_ref, v_ref, beta_ref, glog_ref, gam_ref, dec_ref,
    t_ref, w_ref, u_ref, reach_ref, score_ref, at_ref, bt_ref, info_ref, low_ref, st_ref,
):
    length = pre_ref.shape[0] - RIM
    nc = length // CT
    gain = ng_ref[...]
    count = len(tok_refs)
    each = tok_refs[0].shape[0]

    def normal(x):
        x = x.astype(f32)
        scale = lax.rsqrt(jnp.mean(x * x, -1, keepdims=True) + EPS)
        return (x * scale * gain).astype(bf16)

    model = ng_ref.shape[1]
    normed_ref[0:RIM, :] = normal(rim_ref[:, :model])
    info_ref[...] = flags_ref[...]
    first = flags_ref[RIM : RIM + 8, :]
    ids = jnp.concatenate([rim_ref[8:, model : model + 8].astype(f32), first[:, 6:7] + jnp.zeros((8, 8), f32)], 0)
    row, col = iota2((8, 8), 0), iota2((8, 8), 1)
    for m in range(1, 4):
        same = (pltpu.roll(ids, m, 0)[8:] == ids[8:]).astype(f32)
        first = jnp.where((col == m) & (row < m), same, first)
    info_ref[RIM : RIM + 8, :] = first

    for shift, tok_ref in enumerate(tok_refs):
        place = lax.rem(me_ref[0] + (count - shift), count) * each

        def norm_rows(c, carry):
            target = pl.ds(pl.multiple_of(place + c * CT + RIM, 16), CT)
            normed_ref[target, :] = normal(tok_ref[rows_of(c), :])
            return carry

        lax.fori_loop(0, each // CT, norm_rows, 0)
    nq = nh * 128
    groups = ((wq_ref, 0, nq), (wk_ref, nq, 2 * nq), (wv_ref, 3 * nq, 2 * nq))

    for weight, first, width in groups:
        pre_ref[0:RIM, first : first + width] = (
            mm(normed_ref[0:RIM, :], weight[...]).astype(bf16).astype(f32)
        )

    def project(i, carry):
        rows = rows_of(i, 256, RIM)
        block = normed_ref[rows, :]
        for weight, first, width in groups:
            pre_ref[rows, first : first + width] = mm(block, weight[...]).astype(bf16).astype(f32)
        plain = rows_of(i, 256)
        gate_ref[plain, :] = mm(block, wg_ref[...])
        glog_ref[plain, :] = mm(block, ws_ref[...])
        return carry

    lax.fori_loop(0, length // 256, project, 0)
    logits = glog_ref[...]
    beta_ref[...] = jax.nn.sigmoid(logits)
    soft = jnp.maximum(logits, 0.0) + jnp.log1p(jnp.exp(-jnp.abs(logits)))
    glog = rate_ref[...] * soft
    glog_ref[...] = glog
    tri = (iota2((CT, CT), 0) >= iota2((CT, CT), 1)).astype(f32)
    for c in range(nc):
        gam_ref[c * CT : (c + 1) * CT, :] = exact(tri, glog[c * CT : (c + 1) * CT, :])

    def conv_rows(c, carry):
        rows = rows_of(c)
        info = info_ref[rows_of(c, CT, RIM), :]
        mask = [info[:, m : m + 1] for m in range(4)]
        for tap_ref, first, count, kind in (
            (tq_ref, 0, nh, "q"), (tk_ref, nq, 2 * nh, "k"), (tv_ref, 3 * nq, 2 * nh, "v")
        ):
            for j in range(count):
                cols = slice(first + j * 128, first + (j + 1) * 128)
                mine = slice(j * 128, (j + 1) * 128)
                taps = tap_ref[:, mine].astype(f32)
                block = pre_ref[near(c, RIM - 8), cols]
                total = block[8:] * taps[0:1]
                for m in range(1, 4):
                    total = total + pltpu.roll(block, m, 0)[8:] * mask[m] * taps[m : m + 1]
                conv_ref[rows, cols] = total
                out = total * jax.nn.sigmoid(total)
                if kind == "k":
                    out = out * lax.rsqrt(jnp.sum(out * out, -1, keepdims=True) + EPS)
                {"q": q_ref, "k": k_ref, "v": v_ref}[kind][rows, mine] = out
        return carry

    lax.fori_loop(0, nc, conv_rows, 0)

    row, col, later, same_token = step_order()
    eye = (row == col).astype(f32)
    small_row, small_col = iota2((CT, CT), 0), iota2((CT, CT), 1)

    def prepare(group, carry):
        items = [(group * FORWARD + i, h) for i in range(FORWARD) for h in range(nh)]
        systems, rhs, tails, keeps = [], [], [], []
        for c, h in items:
            rows = rows_of(c)
            info = info_ref[rows_of(c, CT, RIM), :]
            same = (info[:, 6:7] == drow_ref[c]) & (small_row >= small_col)
            gcol, carried, tail, keep = decays(gam_ref, info, rows, h, nh)
            grow = jnp.sum(jnp.where(small_row == small_col, gcol, 0.0), 0, keepdims=True)
            decay = jnp.where(same, jnp.exp(jnp.minimum(gcol - grow, 0.0)), 0.0)
            wide = jnp.concatenate([decay, decay], 1)
            dec_ref[c, h] = wide
            key = head_steps(k_ref, rows, h)
            value = head_steps(v_ref, rows, h)
            beta = jnp.concatenate(
                [beta_ref[rows, 2 * h + j : 2 * h + j + 1] for j in range(2)], 0
            )
            key2 = split(key)
            query = q_ref[rows, h * 128 : (h + 1) * 128]
            query2 = split(query)
            pairs = mm3([jnp.concatenate(x, 0) for x in zip(key2, query2)], key2, NT)
            score_ref[c, h] = pairs[2 * CT :] * wide
            reach_ref[c, h] = query * carried
            systems.append(
                jnp.where((later > 0) | same_token, beta * pairs[: 2 * CT] * twice(wide), 0.0)
            )
            rhs.append(jnp.concatenate([beta * twice(carried) * key, beta * value], 1))
            tails.append(key * twice(tail))
            keeps.append(keep)
        inverse = [eye - jnp.where(same_token, n, 0.0) for n in systems]
        for level in range(6):
            part = (later >> level) == 1
            blocks = [split(jnp.where(part, n, 0.0)) for n in systems]
            inverse2 = [split(x) for x in inverse]
            first = [split(mm3(b, x)) for b, x in zip(blocks, inverse2)]
            inverse = [x - mm3(x2, y) for x, x2, y in zip(inverse, inverse2, first)]
        mixed = [mm3(split(x), split(r)) for x, r in zip(inverse, rhs)]
        products = [mm3(split(jnp.transpose(m)), split(t)) for m, t in zip(mixed, tails)]
        for n, (c, h) in enumerate(items):
            t_ref[c, h] = inverse[n]
            w_ref[c, h] = mixed[n][:, :128]
            u_ref[c, h] = mixed[n][:, 128:]
            at_ref[c, h] = keeps[n] * eye - products[n][:128]
            bt_ref[c, h] = products[n][128:]
        return carry

    lax.fori_loop(0, nc // FORWARD, prepare, 0)

    for h in range(nh):
        st_ref[h, :128] = at_ref[0, h]
        st_ref[h, 128:] = bt_ref[0, h]

    def chain(c, carry):
        for h in range(nh):
            after = mm3(split(st_ref[h]), split(at_ref[c, h]))
            st_ref[h, :128] = after[:128]
            st_ref[h, 128:] = after[128:] + bt_ref[c, h]
        return carry

    lax.fori_loop(1, nc, chain, 0)
    low_ref[...] = st_ref[...].astype(bf16)


def output_kernel(nh, count, blocks, me_ref, *refs):
    output_body(nh, me_ref, refs[:count], *refs[count : -blocks - 1], refs[-blocks - 1 : -1], refs[-1])


def output_body(
    nh, me_ref, map_refs, w_ref, u_ref, reach_ref, score_ref, at_ref, bt_ref, gate_ref, gain_ref, wout_ref,
    sin_ref, fresh_ref, core_ref, gated_ref, branch_refs, all_ref,
):
    nc = w_ref.shape[0]
    states = []
    for h in range(nh):
        state = jnp.zeros((128, 128), f32)
        for distance in range(len(map_refs), 0, -1):
            map_ref = map_refs[distance - 1]
            passed = split(map_ref[h, :128].astype(f32))
            state = mm3(split(state), passed) + map_ref[h, 128:].astype(f32)
            state = jnp.where(me_ref[2] >= distance, state, 0.0)
        states.append(state)

    def chain(c, states):
        out = []
        for h in range(nh):
            sin_ref[c, h] = states[h]
            out.append(mm3(split(states[h]), split(at_ref[c, h])) + bt_ref[c, h])
        return tuple(out)

    states = lax.fori_loop(0, nc, chain, tuple(states))
    for h in range(nh):
        sin_ref[nc, h] = states[h]

    def outputs(group, carry):
        for c, h in [(group * OUTPUT + i, h) for i in range(OUTPUT) for h in range(nh)]:
            rows = rows_of(c)
            cols = slice(h * 128, (h + 1) * 128)
            state2 = split(sin_ref[c, h])
            probe = jnp.concatenate([w_ref[c, h], reach_ref[c, h]], 0)
            seen = mm3(split(probe), state2, NT)
            fresh = u_ref[c, h] - seen[: 2 * CT]
            fresh_ref[c, h] = fresh
            core = seen[2 * CT :] + mm3(split(score_ref[c, h]), split(fresh))
            core_ref[rows, cols] = core
            unit = core * lax.rsqrt(jnp.mean(core * core, -1, keepdims=True) + EPS)
            gate = gate_ref[rows, cols]
            gated_ref[rows, cols] = (
                unit * gain_ref[:, cols] * (gate * jax.nn.sigmoid(gate))
            ).astype(bf16)
        return carry

    lax.fori_loop(0, nc // OUTPUT, outputs, 0)
    all_ref[...] = mm(gated_ref[...], wout_ref[...]).astype(bf16)
    count = len(branch_refs)
    each = branch_refs[0].shape[0]
    for shift, branch_ref in enumerate(branch_refs):
        place = lax.rem(me_ref[0] + shift, count) * each
        branch_ref[...] = all_ref[pl.ds(pl.multiple_of(place, 16), each), :]


def adjoint_kernel(nh, count, me_ref, *refs):
    adjoint_body(nh, me_ref, refs[:count], *refs[count:])


def adjoint_body(
    nh, me_ref, g_refs, wout_ref, core_ref, gate_ref, gain_ref, score_ref, reach_ref, w_ref, at_ref,
    dcore_ref, dft_ref, dt_ref, dgate_ref, dgain_ref, local_ref, all_ref,
    dgated_ref,
):
    nc = w_ref.shape[0]
    count = len(g_refs)
    each = g_refs[0].shape[0]
    for shift, g_ref in enumerate(g_refs):
        place = lax.rem(me_ref[0] + (count - shift), count) * each
        all_ref[pl.ds(pl.multiple_of(place, 16), each), :] = g_ref[...]
    dgated_ref[...] = mm(all_ref[...], wout_ref[...], NT)

    def chunks(group, dgain):
        for i in range(ADJOINT):
            dgain = dgain + chunk(group * ADJOINT + i)
        return dgain

    def chunk(c):
        rows = rows_of(c)
        sums = []
        for h in range(nh):
            cols = slice(h * 128, (h + 1) * 128)
            core = core_ref[rows, cols]
            scale = lax.rsqrt(jnp.mean(core * core, -1, keepdims=True) + EPS)
            unit = core * scale
            gate = gate_ref[rows, cols]
            sig = jax.nn.sigmoid(gate)
            silu = gate * sig
            gain = gain_ref[:, cols]
            grad = dgated_ref[rows, cols]
            sums.append(jnp.sum(grad * unit * silu, 0, keepdims=True))
            dgate_ref[rows, cols] = (
                grad * unit * gain * (sig * (1.0 + gate * (1.0 - sig)))
            ).astype(bf16)
            dunit = grad * gain * silu
            dcore = scale * (dunit - unit * jnp.mean(dunit * unit, -1, keepdims=True))
            dcore_ref[rows, cols] = dcore
            across = jnp.transpose(dcore)
            dft = mm3(split(across), split(score_ref[c, h]))
            dft_ref[c, h] = dft
            left = jnp.concatenate([-dft, across], 1)
            right = jnp.concatenate([w_ref[c, h], reach_ref[c, h]], 0)
            dt_ref[c, h] = mm3(split(left), split(right))
        return jnp.concatenate(sums, 1)

    dgain_ref[...] = lax.fori_loop(0, nc // ADJOINT, chunks, jnp.zeros(dgain_ref.shape, f32))

    def chain(i, carry):
        c = nc - 1 - i
        return tuple(
            mm3(split(carry[h]), split(at_ref[c, h]), NT) + dt_ref[c, h] for h in range(nh)
        )

    start = tuple(dt_ref[nc - 1, h] for h in range(nh))
    total = lax.fori_loop(1, nc, chain, start)
    for h in range(nh):
        local_ref[h] = total[h].astype(bf16)


def normed_back(count, place_ref, gp_ref, weights, normed_ref, gain_ref, mlp_ref, out_refs, all_ref):
    each = out_refs[0].shape[0] - RIM
    length = all_ref.shape[0] - RIM
    total = jnp.zeros(gain_ref.shape, f32)
    for start in range(0, length, 256):
        rows = slice(start + (RIM if start else 0), start + 256 + RIM)
        first = 0
        grad = None
        for weight in weights:
            width = weight.shape[1]
            term = mm(gp_ref[rows, first : first + width], weight[...], NT)
            grad = term if grad is None else grad + term
            first += width
        all_ref[rows, :] = grad.astype(bf16)
        total = total + jnp.sum(grad * normed_ref[rows, :].astype(f32), 0, keepdims=True)
    rim = all_ref[0:RIM, :].astype(f32)
    row = iota2((RIM, 1), 0)
    gains = [*split(total / gain_ref[...]), *split(mlp_ref[...])]
    for n, gain in enumerate(gains):
        rim = jnp.where(row == n, gain.astype(f32), rim)
    rim = rim.astype(bf16)
    for shift, out_ref in enumerate(out_refs):
        place = lax.rem(place_ref[0] + shift, count) * each + RIM
        out_ref[0:each, :] = all_ref[pl.ds(pl.multiple_of(place, 16), each), :]
        out_ref[each:, :] = rim


def turn(left_ref, turned_ref):
    tokens, width = left_ref.shape
    for n in range(width // 128):
        turned_ref[n * 128 : (n + 1) * 128, :tokens] = jnp.transpose(
            left_ref[:, n * 128 : (n + 1) * 128]
        )


def two_halves(place_ref, turned, right, own_ref, given_ref, cols):
    half = turned.shape[0] // 2
    for core, out_ref in ((place_ref[1], own_ref), (1 - place_ref[1], given_ref)):
        rows = pl.ds(pl.multiple_of(core * half, 16), half)
        out_ref[0:half, cols] = mm(turned[rows, : right.shape[0]], right[...]).astype(out_ref.dtype)


def two_parts(value):
    high, low = split(value)
    return jnp.concatenate([high, low], 0)


def backward_kernel(nh, count, blocks, *refs):
    at = 2 * count + 1
    maps, local_sums, place, refs = refs[:count], refs[count : at - 1], refs[at - 1], refs[at:]
    inputs, refs = refs[:21], refs[21:]
    dgate, weights, (normed, gain, mlp, dgain), refs = refs[0], refs[1:6], refs[6:10], refs[10:]
    (grad, gated), refs = refs[:2], refs[2:]
    out_refs, (own, given), refs = refs[:blocks], refs[blocks : blocks + 2], refs[blocks + 2 :]
    gp, taps, dlog, dconv, small, ends, everything, turned = refs
    half, width = own.shape[0] - 8, gp.shape[1]
    wide, nq = own.shape[1], gated.shape[1]
    gp[0:RIM, width - nq :] = jnp.zeros((RIM, nq), bf16)
    gp[RIM:, width - nq :] = dgate[...]
    backward_body(nh, maps, local_sums, *inputs, gp, taps, dlog, dconv, small, ends)
    normed_back(blocks, place, gp, weights, normed, gain, mlp, out_refs, everything)
    turn(normed, turned)
    two_halves(place, turned, gp, own, given, slice(0, width))
    turn(grad, turned)
    two_halves(place, turned, gated, own, given, slice(width, wide))
    own[half:, :] = jnp.zeros((8, wide), f32)
    own[half : half + 4, : taps.shape[1]] = taps[...]
    own[half + 4 : half + 5, :128] = dlog[...]
    own[half + 4 : half + 5, 128 : 128 + dgain.shape[1]] = dgain[...]
    given[half:, :] = two_parts(own[half:, :])


def backward_body(
    nh, map_refs, local_refs, at_ref, dt_ref, dft_ref, dcore_ref, t_ref, fresh_ref, sin_ref,
    q_ref, k_ref, v_ref, beta_ref, gam_ref, dec_ref, conv_ref, pre_ref, info_ref, tq_ref, tk_ref, tv_ref,
    rate_ref, glog_ref,
    gp_ref, taps_ref, dlog_ref,
    dconv_ref, small_ref, ends_ref,
):
    length = q_ref.shape[0]
    nc = length // CT
    nq = nh * 128
    width = 5 * nq
    ends = []
    for h in range(nh):
        end = local_refs[0][h].astype(f32)
        for map_ref, local_ref in zip(map_refs[1:], local_refs[1:]):
            passed = split(map_ref[h, :128].astype(f32))
            end = mm3(split(end), passed, NT) + local_ref[h].astype(f32)
        ends.append(end)
    row, col, later, same_token = step_order()
    before = (later > 0) | same_token
    last_row = (iota2((CT, 1), 0) == CT - 1).astype(f32)
    dconv_ref[0:RIM, :] = jnp.zeros((RIM, width), f32)
    dconv_ref[RIM + length :, :] = jnp.zeros((RIM, width), f32)
    lane = iota2((CT, 128), 1)
    upper = (iota2((CT, CT), 0) <= iota2((CT, CT), 1)).astype(f32)

    def chain(i, ends):
        c = nc - 1 - i
        out = []
        for h in range(nh):
            ends_ref[c, h] = ends[h]
            out.append(mm3(split(ends[h]), split(at_ref[c, h]), NT) + dt_ref[c, h])
        return tuple(out)

    lax.fori_loop(0, nc, chain, tuple(ends))

    def chunks(group, carry):
        for i in range(BACKWARD):
            chunk(group * BACKWARD + i)
        return carry

    def chunk(c):
        rows = rows_of(c)
        store = rows_of(c, CT, RIM)
        info = info_ref[store, :]
        small = jnp.zeros((CT, 128), f32)
        dgam = jnp.zeros((CT, 128), f32)
        for h in range(nh):
            cols = slice(h * 128, (h + 1) * 128)
            end = ends_ref[c, h]
            end2 = split(end)
            _, carried, tail, _ = decays(gam_ref, info, rows, h, nh)
            carried2, tail2 = twice(carried), twice(tail)
            key = head_steps(k_ref, rows, h)
            value = head_steps(v_ref, rows, h)
            query = q_ref[rows, cols]
            beta = jnp.concatenate(
                [beta_ref[rows, 2 * h + j : 2 * h + j + 1] for j in range(2)], 0
            )
            wide = dec_ref[c, h]
            full = jnp.where(before, twice(wide), 0.0)
            state = sin_ref[c, h]
            fresh = fresh_ref[c, h]
            fresh2 = split(fresh)
            dcore = dcore_ref[rows, cols]
            dft = dft_ref[c, h] + mm3(end2, split(key * tail2), NT)
            solved = jnp.transpose(mm3(split(dft), split(t_ref[c, h])))
            both = split(jnp.concatenate([solved, dcore], 0))
            through = mm3(both, split(state))
            pairs = mm3(both, fresh2, NT)
            dtail = mm3(fresh2, end2)
            em = -pairs[: 2 * CT] * full
            ps = pairs[2 * CT :] * wide
            mixed = mm3(split(jnp.concatenate([em, ps], 0)), split(key))
            turned = jnp.transpose(jnp.concatenate([beta * em, ps], 0))
            dkb = mm3(split(turned), split(jnp.concatenate([key, query], 0))) + tail2 * dtail
            x1 = mixed[: 2 * CT] - carried2 * through[: 2 * CT]
            dka = beta * x1
            dkey = dka + dkb
            dbeta = jnp.sum(key * x1 + solved * value, -1, keepdims=True)
            dvalue = beta * solved
            dquery = mixed[2 * CT :] + carried * through[2 * CT :]
            turn = jnp.sum(key * (dka - dkb), -1, keepdims=True)
            closing = jnp.sum(
                jnp.sum(end * sin_ref[c + 1, h], -1, keepdims=True), 0, keepdims=True
            )
            dg = (
                jnp.sum(query * dquery, -1, keepdims=True)
                + turn[:CT]
                + turn[CT:]
                + last_row * closing
            )
            dgam = jnp.where(lane == 2 * nh + h, dg, dgam)
            for j in range(2):
                small = jnp.where(lane == 2 * h + j, dbeta[j * CT : (j + 1) * CT], small)
            pre = conv_ref[rows, cols]
            sig = jax.nn.sigmoid(pre)
            dconv_ref[store, cols] = dquery * (sig * (1.0 + pre * (1.0 - sig)))
            for j in range(2):
                kcols = slice(nq + (2 * h + j) * 128, nq + (2 * h + j + 1) * 128)
                pre = conv_ref[rows, kcols]
                sig = jax.nn.sigmoid(pre)
                act = pre * sig
                scale = lax.rsqrt(jnp.sum(act * act, -1, keepdims=True) + EPS)
                unit = key[j * CT : (j + 1) * CT]
                grad = dkey[j * CT : (j + 1) * CT]
                grad = scale * (grad - unit * jnp.sum(unit * grad, -1, keepdims=True))
                dconv_ref[store, kcols] = grad * (sig * (1.0 + pre * (1.0 - sig)))
                vcols = slice(3 * nq + (2 * h + j) * 128, 3 * nq + (2 * h + j + 1) * 128)
                pre = conv_ref[rows, vcols]
                sig = jax.nn.sigmoid(pre)
                dconv_ref[store, vcols] = dvalue[j * CT : (j + 1) * CT] * (
                    sig * (1.0 + pre * (1.0 - sig))
                )
        dglog = exact(upper, dgam)
        small_ref[rows, :] = jnp.where(lane < 2 * nh, small, dglog)

    lax.fori_loop(0, nc // BACKWARD, chunks, 0)

    beta = beta_ref[...]
    small = small_ref[...]
    lanes = iota2(beta.shape, 1)
    grads = small * beta * jnp.where(lanes < 2 * nh, 1.0 - beta, rate_ref[...])
    dlog_ref[...] = jnp.sum(small * glog_ref[...], 0, keepdims=True)
    gp_ref[0:RIM, 0 : width + 128] = jnp.zeros((RIM, width + 128), bf16)
    gp_ref[RIM:, width : width + 128] = grads.astype(bf16)
    groups = ((tq_ref, 0, nh), (tk_ref, nq, 2 * nh), (tv_ref, 3 * nq, 2 * nh))

    def turned_back(grad, masks, taps, count):
        total = grad[:count] * taps[0:1]
        size = grad.shape[0]
        for m in range(1, 4):
            moved = pltpu.roll(grad * masks[:, m : m + 1], size - m, 0)
            total = total + moved[:count] * taps[m : m + 1]
        return total

    def conv_back(c, sums):
        info = info_ref[near(c, RIM), :]
        new = []
        for tap_ref, first, count in groups:
            for j in range(count):
                cols = slice(first + j * 128, first + (j + 1) * 128)
                taps = tap_ref[:, j * 128 : (j + 1) * 128].astype(f32)
                grad = dconv_ref[near(c, RIM), cols]
                gp_ref[rows_of(c, CT, RIM), cols] = turned_back(grad, info, taps, CT).astype(bf16)
                block = pre_ref[near(c, RIM - 8), cols]
                parts = [jnp.sum(grad[:CT] * block[8:], 0, keepdims=True)]
                for m in range(1, 4):
                    moved = pltpu.roll(block, m, 0)[8:]
                    parts.append(
                        jnp.sum(grad[:CT] * info[:CT, m : m + 1] * moved, 0, keepdims=True)
                    )
                new.append(jnp.concatenate(parts, 0))
        return sums + jnp.concatenate(new, 1)

    taps_ref[...] = lax.fori_loop(0, nc, conv_back, jnp.zeros((4, width), f32))
    for tap_ref, first, count in groups:
        cols = slice(first, first + count * 128)
        taps = tap_ref[...].astype(f32)
        early = slice(8, 24)
        rim = turned_back(dconv_ref[early, cols], info_ref[early, :], taps, 8)
        gp_ref[0:RIM, cols] = jnp.concatenate([jnp.zeros_like(rim), rim], 0).astype(bf16)


VMEM = pl.BlockSpec(memory_space=pltpu.VMEM)
SMEM = pl.BlockSpec(memory_space=pltpu.SMEM)
ANY = pl.BlockSpec(memory_space=pl.ANY)


def kernel_call(body, name, args, outs, scratch=(), after=(), mib=60, cost=2):
    extra = len(after)

    def run(*refs):
        body(*refs[: len(args)], *refs[len(args) + extra :])

    return pl.pallas_call(
        run,
        name=name,
        in_specs=[SMEM if a.dtype == i32 else VMEM for a in args] + [ANY] * extra,
        out_specs=[VMEM] * len(outs),
        out_shape=outs,
        scratch_shapes=list(scratch),
        compiler_params=pltpu.CompilerParams(vmem_limit_bytes=mib * MIB),
        cost_estimate=pl.CostEstimate(flops=cost * 10**9, bytes_accessed=0, transcendentals=0),
    )(*args, *after)


def sds(*shape, dtype=f32):
    return jax.ShapeDtypeStruct(shape, dtype)


def mixer_forward(me, tokens, rim, norm_gain, weights, taps, info, doc_rows, rate):
    length, width = tokens[0].shape
    length *= len(tokens)
    w_query, w_key, w_value, w_outgate, w_small = weights
    nh = w_query.shape[1] // 128
    nc, nq = length // CT, nh * 128
    per = (nc, nh)
    outs = dict(
        normed=sds(RIM + length, width, dtype=bf16),
        pre=sds(RIM + length, 5 * nq),
        conv=sds(length, 5 * nq),
        gate=sds(length, nq),
        q=sds(length, nq),
        k=sds(length, 2 * nq),
        v=sds(length, 2 * nq),
        beta=sds(length, 128),
        glog=sds(length, 128),
        gam=sds(length, 128),
        dec=sds(*per, CT, 128),
        t=sds(*per, 128, 128),
        w=sds(*per, 128, 128),
        u=sds(*per, 128, 128),
        reach=sds(*per, CT, 128),
        score=sds(*per, CT, 128),
        at=sds(*per, 128, 128),
        bt=sds(*per, 128, 128),
        info=sds(length + 2 * RIM, 8),
        low=sds(nh, 256, 128, dtype=bf16),
    )
    args = (me, *tokens, rim, norm_gain, w_query, w_key, w_value, w_outgate, w_small, *taps, info, doc_rows, rate)
    res = kernel_call(
        functools.partial(forward_kernel, nh, len(tokens)), "mixer_forward", args, list(outs.values()),
        cost=25,
        scratch=[pltpu.VMEM((nh, 256, 128), f32)],
    )
    return dict(zip(outs, res))


def mixer_output(me, maps, fwd, out_gain, w_out, blocks, after=()):
    nc, nh = fwd["w"].shape[:2]
    length = nc * CT
    outs = dict(
        sin=sds(nc + 1, nh, 128, 128),
        fresh=sds(nc, nh, 128, 128),
        core=sds(length, nh * 128),
        gated=sds(length, nh * 128, dtype=bf16),
    )
    parts = [sds(length // blocks, w_out.shape[1], dtype=bf16)] * blocks
    args = (me, *maps, *(fwd[n] for n in ("w", "u", "reach", "score", "at", "bt", "gate")), out_gain, w_out)
    res = kernel_call(
        functools.partial(output_kernel, nh, len(maps), blocks), "mixer_output", args,
        [*outs.values(), *parts], cost=10,
        scratch=[pltpu.VMEM((length, w_out.shape[1]), bf16)],
        after=after,
    )
    return dict(zip(outs, res), branch=res[len(outs) :])


def mixer_adjoint(me, grad, w_out, fwd, out, out_gain, after=()):
    nc, nh = fwd["w"].shape[:2]
    length = nc * CT
    outs = dict(
        dcore=sds(length, nh * 128),
        dft=sds(nc, nh, 128, 128),
        dt=sds(nc, nh, 128, 128),
        dgate=sds(length, nh * 128, dtype=bf16),
        dgain=sds(1, nh * 128),
        local=sds(nh, 128, 128, dtype=bf16),
        g=sds(length, w_out.shape[1], dtype=bf16),
    )
    args = (me, *grad, w_out, out["core"], fwd["gate"], out_gain, fwd["score"], fwd["reach"], fwd["w"], fwd["at"])
    res = kernel_call(
        functools.partial(adjoint_kernel, nh, len(grad)), "mixer_adjoint", args, list(outs.values()),
        cost=10,
        scratch=[pltpu.VMEM((length, nh * 128), f32)],
        after=after,
    )
    return dict(zip(outs, res))


def mixer_backward(
    place, maps, local_sums, fwd, out, adj, taps, rate, weights, gain, mlp, blocks, after=()
):
    nc, nh = fwd["w"].shape[:2]
    length, nq = nc * CT, nh * 128
    width = 5 * nq
    model = gain.shape[1]
    parts = [sds(RIM + length // blocks, model, dtype=bf16)] * blocks
    columns = width + 128 + 2 * nq
    halves = [sds(model // 2 + 8, columns), sds(model // 2 + 16, columns, dtype=bf16)]
    args = (
        *maps, *local_sums, place, fwd["at"], adj["dt"], adj["dft"], adj["dcore"], fwd["t"], out["fresh"],
        out["sin"], *(fwd[n] for n in ("q", "k", "v", "beta", "gam", "dec", "conv", "pre", "info")), *taps,
        rate, fwd["glog"], adj["dgate"], *weights, fwd["normed"], gain, mlp, adj["dgain"],
        adj["g"], out["gated"],
    )
    *res, own, given = kernel_call(
        functools.partial(backward_kernel, nh, len(maps), blocks), "mixer_backward", args,
        [*parts, *halves], cost=300,
        scratch=[
            pltpu.VMEM((RIM + length, width + 128 + nq), bf16), pltpu.VMEM((4, width), f32),
            pltpu.VMEM((1, 128), f32),
            pltpu.VMEM((length + 2 * RIM, width), f32), pltpu.VMEM((length, 128), f32),
            pltpu.VMEM((nc, nh, 128, 128), f32), pltpu.VMEM((RIM + length, model), bf16),
            pltpu.VMEM((model, RIM + length), bf16),
        ],
        after=after,
    )
    return res, (own, given)


def token_info(doc_ids):
    ids = doc_ids.astype(f32)
    length = ids.shape[0]
    extended = jnp.concatenate([ids[:3], ids])
    masks = [(extended[3 - m : 3 - m + length] == ids).astype(f32) for m in range(4)]
    blocks = ids.reshape(-1, CT)
    last = blocks[:, -1:]
    previous = jnp.concatenate([blocks[:1, :1], last[:-1]], 0)
    columns = masks + [
        (blocks == previous).astype(f32).reshape(-1),
        (blocks == last).astype(f32).reshape(-1),
        ids,
        jnp.zeros_like(ids),
    ]
    info = jnp.pad(jnp.stack(columns, 1), ((RIM, RIM), (0, 0)))
    return info, blocks[:, None, :]


def middle_kernel(count, tok_ref, *refs):
    parts, (gain_ref, middle_ref, normed_ref) = refs[:count], refs[count:]
    middle = tok_ref[...].astype(f32)
    total = parts[0][...].astype(f32)
    for part in parts[1:]:
        total = total + part[...].astype(f32)
    middle = middle + total
    middle_ref[...] = middle
    scale = lax.rsqrt(jnp.mean(middle * middle, -1, keepdims=True) + EPS)
    normed_ref[...] = (middle * scale * gain_ref[...]).astype(bf16)


def feed_kernel(hidden, place_ref, *refs):
    x_refs, cot_refs, weights, refs = refs[:4], refs[4:8], refs[8:11], refs[11:]
    norm_refs, block_refs, cols_ref, refs = refs[:4], refs[4:8], refs[8], refs[9:]
    gate_w, up_w, down_w, sems = refs
    width = gate_w.shape[1]
    each = x_refs[0].shape[0]
    start = pl.multiple_of(place_ref[3], 128)
    window = pl.ds(start, width)
    copies = [
        pltpu.make_async_copy(weights[0].at[:, window], gate_w, sems.at[0]),
        pltpu.make_async_copy(weights[1].at[:, window], up_w, sems.at[1]),
        pltpu.make_async_copy(weights[2].at[window, :], down_w, sems.at[2]),
    ]
    for copy in copies:
        copy.start()
    lane = iota2((1, width), 1) - place_ref[4]
    mask = ((lane >= 0) & (lane < hidden)).astype(f32)
    for n, pair in enumerate(((1, 3), (0, 2))):
        x = jnp.concatenate([x_refs[p][...] for p in pair], 0)
        cot = jnp.concatenate([cot_refs[p][...] for p in pair], 0)
        if n == 0:
            copies[0].wait()
        gate = mm(x, gate_w[...])
        if n == 0:
            copies[1].wait()
        up = mm(x, up_w[...]) * mask
        sig = jax.nn.sigmoid(gate)
        silu = gate * sig * mask
        act = (silu * up).astype(bf16)
        if n == 0:
            copies[2].wait()
        grad = mm(cot, down_w[...], NT)
        ggate = (grad * up * sig * (1.0 + gate * (1.0 - sig))).astype(bf16)
        gup = (grad * silu).astype(bf16)
        gnorm = (mm(ggate, gate_w[...], NT) + mm(gup, up_w[...], NT)).astype(bf16)
        block = mm(act, down_w[...]).astype(bf16)
        for n, p in enumerate(pair):
            half, at = slice(n * each, (n + 1) * each), slice(p * each, (p + 1) * each)
            norm_refs[p][...] = gnorm[half]
            block_refs[p][...] = block[half]
            for k, value in enumerate((ggate, gup, act)):
                cols_ref[k, at, :] = value[half]


def feed_grads_kernel(seq_n, head_n, place_ref, *refs):
    x_refs, cot_refs, cols_ref, refs = refs[:4], refs[4:8], refs[8], refs[9:]
    out_ref, turned_ref, full_ref = refs
    each = x_refs[0].shape[0]
    half = full_ref.shape[0]
    rows = half // (seq_n * head_n)
    for n, blocks in enumerate((x_refs, cot_refs)):
        for p, ref in enumerate(blocks):
            turned_ref[n, :, p * each : (p + 1) * each] = jnp.transpose(ref[...])
    for k in range(3):
        for b in range(2):
            left = turned_ref[k // 2, b * half : (b + 1) * half, :]
            full_ref[...] = mm(left, cols_ref[k]).astype(bf16)
            for n in range(seq_n * head_n):
                first = ((n // 2 * 2 + b) * 2 + n % 2) * 3 + k
                out_ref[first * rows : (first + 1) * rows, :] = full_ref[n * rows : (n + 1) * rows, :]


def feed_group_kernel(place_ref, *refs):
    sum_ref, out_refs = refs[0], refs[1:]
    rows = out_refs[0].shape[0] // 2
    blocks = [sum_ref[n * rows : (n + 1) * rows, :] for n in range(4)]
    halves = [blocks[:2], blocks[2:]]
    for other, out_ref in enumerate(out_refs):
        odd = lax.rem(place_ref[0] + other, 2) == 1
        values = [jnp.where(odd, high, low) for low, high in halves]
        for n in range(2):
            core = lax.rem(place_ref[1] + n, 2) == 1
            out_ref[n * rows : (n + 1) * rows, :] = jnp.where(core, values[1], values[0])


def feed_out_kernel(hidden, place_ref, *refs):
    parts, (gate_ref, up_ref, down_ref) = refs[:4], refs[4:]
    rows = parts[0].shape[0] // 6
    own = lax.rem(place_ref[0], 2) * 2 + place_ref[1]
    for k, out_ref in enumerate((gate_ref, up_ref, down_ref)):
        values = [
            part[(n % 2 * 3 + k) * rows : (n % 2 * 3 + k + 1) * rows, :].astype(f32)
            for n, part in enumerate(parts)
        ]
        for g in range(4):
            value = values[0]
            for n in range(1, 4):
                value = jnp.where(own == (g ^ n), values[n], value)
            start = g * hidden % 128
            value = value[:, start : start + hidden]
            out_ref[:, g * hidden : (g + 1) * hidden] = value


def mixer_blocks_kernel(place_ref, own_ref, got_ref, *out_refs):
    extra = 8
    count = len(out_refs)
    half = own_ref.shape[0] - extra
    rows = half // count
    for shift, out_ref in enumerate(out_refs):
        at = pl.ds(pl.multiple_of(lax.rem(place_ref[2] + shift, count) * rows, 16), rows)
        out_ref[0:rows, :] = (own_ref[at, :] + got_ref[at, :].astype(f32)).astype(out_ref.dtype)
        small = own_ref[half:, :] + joined_parts(got_ref, half, extra)
        out_ref[rows:, :] = two_parts(small) if shift else small


def joined_parts(ref, start, extra):
    both = ref[start : start + 2 * extra, :].astype(f32)
    return both[:extra] + both[extra:]


def mixer_sum_kernel(count, nh, *refs):
    parts, out_refs = refs[:count], refs[count:]
    weight_refs, conv_refs, (decay_ref, gain_ref) = out_refs[:7], out_refs[7:10], out_refs[10:]
    rows = weight_refs[0].shape[0]
    nq = nh * 128
    starts = (0, nq, 3 * nq, 5 * nq, 5 * nq + 2 * nh, 5 * nq + 128, 6 * nq + 128)
    for n, (start, out_ref) in enumerate(zip(starts, weight_refs)):
        turned = n in (3, 4, 6)
        width = out_ref.shape[0] if turned else out_ref.shape[1]
        total = add_up([part[0:rows, start : start + width] for part in parts])
        out_ref[...] = jnp.transpose(total) if turned else total
    small = parts[0][rows:, :]
    for part in parts[1:]:
        small = small + joined_parts(part, rows, 8)
    for start, out_ref in zip(starts, conv_refs):
        out_ref[...] = small[0:4, start : start + out_ref.shape[1]]
    decay_ref[...] = small[4:5, 2 * nh : 3 * nh]
    gain_ref[...] = small[4:5, 128 : 128 + nq]


def norm_back(grad_normed, rows, gain):
    scale = lax.rsqrt(jnp.mean(rows * rows, -1, keepdims=True) + EPS)
    unit = rows * scale
    scaled = grad_normed * gain
    grad_rows = scale * (scaled - unit * jnp.mean(scaled * unit, -1, keepdims=True))
    return grad_rows, jnp.sum(grad_normed * unit, 0, keepdims=True)


def middle_back_kernel(a_ref, b_ref, c_ref, middle_ref, cot_ref, gain_ref, grad_ref, low_ref, sum_ref):
    total = a_ref[...].astype(f32) + b_ref[...].astype(f32) + c_ref[...].astype(f32)
    rows, sum_ref[...] = norm_back(total, middle_ref[...], gain_ref[...])
    grad = cot_ref[...].astype(f32) + rows
    grad_ref[...] = grad
    low_ref[...] = grad.astype(bf16)


def extra_rows_kernel(count, *refs):
    parts, (rim_ref, gains_ref) = refs[:count], refs[count:]
    each = parts[0].shape[0] - RIM
    total = add_up([part[each:, :] for part in parts])
    row = iota2((RIM, 1), 0)
    rim_ref[...] = jnp.where(row >= RIM - 3, total, 0.0).astype(bf16)
    gains_ref[...] = jnp.zeros(gains_ref.shape, f32)
    for n in range(2):
        gains_ref[n : n + 1, :] = total[2 * n : 2 * n + 1] + total[2 * n + 1 : 2 * n + 2]


def tokens_back_kernel(count, *refs):
    parts, (rim_ref, tok_ref, gain_ref, middle_ref, grad_ref) = refs[:count], refs[count:]
    each = tok_ref.shape[0]
    total = add_up([part[0:each, :] for part in parts])
    rim = rim_ref[...].astype(f32)
    total = total + jnp.concatenate([jnp.zeros((each - RIM, rim.shape[1]), f32), rim], 0)
    rows, _ = norm_back(total, tok_ref[...].astype(f32), gain_ref[...])
    grad_ref[...] = middle_ref[...] + rows


HEAD = ("pair", "half")


def axis_size(axis):
    return lax.axis_size(axis) if isinstance(axis, str) else lax.psum(1, axis)


def ring(value, axis):
    count = axis_size(axis)
    return [value] + [
        lax.ppermute(value, axis, [(i, (i + shift) % count) for i in range(count)])
        for shift in range(1, count)
    ]


def along(value, axis, shift):
    count = axis_size(axis)
    pairs = [(i, i + shift) for i in range(count) if 0 <= i + shift < count]
    return lax.ppermute(value, axis, pairs)


def crossed(value, axis, bit=0):
    return lax.ppermute(value, axis, [(i, i ^ (1 << bit)) for i in range(axis_size(axis))])


def spread(blocks, axis):
    count = axis_size(axis)
    return [blocks[0]] + [
        lax.ppermute(blocks[shift], axis, [(i, (i + shift) % count) for i in range(count)])
        for shift in range(1, count)
    ]


def add_up(parts):
    total = parts[0].astype(f32)
    for part in parts[1:]:
        total = total + part.astype(f32)
    return total


def sum_over(value, axis):
    return add_up(ring(value, axis))


def tied(*values):
    return lax.optimization_barrier(values)


def on_device(
    tokens, doc_ids, norm_gain, w_query, w_key, w_value, w_beta, w_decay, w_outgate, conv_query,
    conv_key, conv_value, decay_log, out_gain, w_out, mlp_gain, w_gate, w_up, w_down, cotangent,
):
    head_n, seq_n, batch_n = (axis_size(a) for a in (HEAD, "seq", "batch"))
    me = lax.axis_index(HEAD)
    nh = w_decay.shape[1]
    nq = nh * 128
    each, model = tokens.shape
    length = each * head_n
    me_array = me.astype(i32).reshape(1)

    head_last = head_n - 1
    blocks = ring(tokens, HEAD)
    seq_place = lax.axis_index("seq")
    core = lax.axis_index("batch")
    ways = 2 * batch_n
    hidden = w_gate.shape[1] // ways
    mine = ((me & 1) * batch_n + core) * hidden
    place = jnp.stack([me, core, seq_place, mine // 128 * 128, mine % 128]).astype(i32)
    window = -(-(hidden + 64) // 128) * 128
    ids = jnp.broadcast_to(doc_ids[-RIM:, None], (RIM, 128)).astype(bf16)
    tail = tied(jnp.concatenate([tokens[-RIM:], ids], 1), blocks[1])[0]
    rim = add_up(
        [
            lax.ppermute(
                tail,
                ("seq", *HEAD),
                [(s * head_n + head_last, (s + 1) * head_n + h) for s in range(seq_n - 1)],
            )
            for h in range(head_n)
        ]
    ).astype(bf16)
    info, doc_rows = token_info(doc_ids)
    w_small = jnp.pad(jnp.concatenate([w_beta, w_decay], 1), ((0, 0), (0, 128 - 3 * nh)))
    rate = jnp.pad(-jnp.exp(decay_log), (2 * nh, 128 - 3 * nh))[None]
    weights = (w_query, w_key, w_value, w_outgate, w_small)
    taps = (conv_query, conv_key, conv_value)
    gain = norm_gain[None]
    fwd = mixer_forward(me_array, blocks, rim, gain, weights, taps, info, doc_rows, rate)

    states = ring(fwd["low"], "seq")
    cot_near = crossed(tied(cotangent, *blocks[1:])[0], HEAD)
    cot_sent = tied(cotangent, cot_near, fwd["low"])
    cots = [cotangent, cot_near, *[crossed(value, "batch") for value in cot_sent[:2]]]
    out = mixer_output(place, states[1:], fwd, out_gain[None], w_out, head_n, after=cots[1:])

    low = lambda *shape: sds(*shape, dtype=bf16)
    parts = spread(out["branch"], HEAD)
    middle, normed_mid = kernel_call(
        functools.partial(middle_kernel, len(parts)), "middle",
        (tokens, *parts, mlp_gain[None]), [sds(each, model), low(each, model)],
    )
    near = crossed(normed_mid, HEAD)
    rows = [normed_mid, near, crossed(normed_mid, "batch"), crossed(near, "batch")]
    fed = pl.pallas_call(
        functools.partial(feed_kernel, hidden),
        name="feed",
        in_specs=[SMEM] + [VMEM] * 8 + [ANY] * 3,
        out_specs=[VMEM] * 9,
        out_shape=[low(each, model)] * 8 + [low(3, 4 * each, window)],
        scratch_shapes=[
            pltpu.VMEM((model, window), bf16), pltpu.VMEM((model, window), bf16),
            pltpu.VMEM((window, model), bf16), pltpu.SemaphoreType.DMA((3,)),
        ],
        compiler_params=pltpu.CompilerParams(vmem_limit_bytes=60 * MIB),
        cost_estimate=pl.CostEstimate(flops=10**10, bytes_accessed=0, transcendentals=0),
    )(place, *rows, *cots, w_gate, w_up, w_down)

    def own_parts(blocks):
        given = (blocks[1].astype(f32) + crossed(blocks[3], "batch").astype(f32)).astype(bf16)
        return given, (blocks[0], crossed(blocks[2], "batch"), crossed(given, HEAD))

    given, norm_parts = own_parts(fed[:4])
    block_own = crossed(fed[6], "batch")
    block_given = (fed[5].astype(f32) + crossed(fed[7], "batch").astype(f32)).astype(bf16)

    (feed_grads,) = kernel_call(
        functools.partial(feed_grads_kernel, seq_n, head_n), "feed_grads",
        (place, *rows, *cots, fed[8]), [low(3 * model, window)],
        scratch=[
            pltpu.VMEM((2, model, 4 * each), bf16), pltpu.VMEM((model // 2, window), bf16),
        ],
        after=[given], cost=8,
    )
    grad_middle, grad_branch, grad_mlp_gain = kernel_call(
        middle_back_kernel, "middle_back",
        (*norm_parts, middle, cotangent, mlp_gain[None]),
        [sds(each, model), low(each, model), sds(1, model)],
        after=[feed_grads],
    )
    grad_blocks = ring(grad_branch, HEAD)

    feed_sums = lax.psum_scatter(feed_grads, "seq", scatter_dimension=0, tiled=True)

    adj = mixer_adjoint(
        me_array, grad_blocks, w_out, fwd, out, out_gain[None], after=[block_given, block_own]
    )
    block_given = crossed(tied(adj["local"], block_given)[1], HEAD)
    block_out = (middle + add_up([fed[4], block_own, block_given])).astype(bf16)
    later = [along(adj["local"], "seq", -s) for s in range(seq_n - 1, 0, -1)]

    own_rows = model // (batch_n * seq_n * head_n)
    seq_rows = own_rows * head_n
    normed_parts, wide = mixer_backward(
        place, states[1:], later, fwd, out, adj, taps, rate,
        (w_query, w_key, w_value, w_small, w_outgate), gain, grad_mlp_gain, head_n,
        after=[block_given, feed_sums],
    )
    feed_sums = lax.psum_scatter(feed_sums, "pair", scatter_dimension=0, tiled=True)
    normed_parts = spread(normed_parts, HEAD)

    columns = wide[0].shape[1]
    wide_blocks = kernel_call(
        mixer_blocks_kernel, "mixer_blocks",
        (place, wide[0], crossed(wide[1], "batch")),
        [sds(seq_rows + 8, columns)] + [low(seq_rows + 16, columns)] * (seq_n - 1),
        after=[feed_sums],
    )
    wide_parts = spread(wide_blocks, "seq")
    extra, gains = kernel_call(
        functools.partial(extra_rows_kernel, head_n), "extra_rows", normed_parts,
        [low(RIM, model), sds(8, model)],
        after=wide_parts[1:2],
    )
    gains = add_up([gains, crossed(gains, "batch")])
    gain_parts = ring(gains, "seq")
    rim_part = lax.ppermute(
        extra,
        ("seq", *HEAD),
        [(s * head_n + head_last, (s - 1) * head_n + head_last) for s in range(1, seq_n)],
    )
    group_own, group_sent = kernel_call(
        feed_group_kernel, "feed_group", (place, feed_sums),
        [low(6 * own_rows, window)] * 2,
        after=[extra],
    )
    group_got = crossed(group_sent, HEAD)
    group = [group_own, crossed(group_own, "batch"), group_got, crossed(group_got, "batch")]
    grad_gate, grad_up, grad_down = kernel_call(
        functools.partial(feed_out_kernel, hidden), "feed_out", (place, *group),
        [sds(own_rows, ways * hidden)] * 3,
    )
    (grad_tokens,) = kernel_call(
        functools.partial(tokens_back_kernel, head_n), "tokens_back",
        (*normed_parts, rim_part, tokens, gain, grad_middle),
        [sds(each, model)],
    )
    *sums, grad_decay, grad_out_gain = kernel_call(
        functools.partial(mixer_sum_kernel, seq_n, nh), "mixer_sum", wide_parts,
        [sds(seq_rows, w) for w in (nq, 2 * nq, 2 * nq)] + [sds(w, seq_rows) for w in (2 * nh, nh)]
        + [sds(seq_rows, nq), sds(nq, seq_rows)]
        + [sds(4, w) for w in (nq, 2 * nq, 2 * nq)] + [sds(1, nh), sds(1, nq)],
    )
    grad_q, grad_k, grad_v, grad_b, grad_d, grad_g, grad_out, *grad_convs = sums
    gains = add_up(gain_parts)
    index = (core * seq_n + seq_place) * head_n + me
    gains = lax.dynamic_slice_in_dim(gains, index * own_rows, own_rows, 1)
    return (
        block_out, grad_tokens, gains[0], grad_q, grad_k, grad_v, grad_b.T, grad_d.T, grad_g,
        *grad_convs, grad_decay[0], grad_out_gain[0], grad_out, gains[1], grad_gate, grad_up,
        grad_down.T,
    )


def solution(mesh):
    batch, seq, head = mesh.devices.shape
    split_mesh = Mesh(mesh.devices.reshape(batch, seq, head // 2, 2), ("batch", "seq", *HEAD))
    return jax.shard_map(
        on_device,
        mesh=split_mesh,
        in_specs=(
            P(("batch", "seq", *HEAD), None),
            P(("batch", "seq")),
            P(),
            P(None, HEAD),
            P(None, HEAD),
            P(None, HEAD),
            P(None, HEAD),
            P(None, HEAD),
            P(None, HEAD),
            P(None, HEAD),
            P(None, HEAD),
            P(None, HEAD),
            P(HEAD),
            P(HEAD),
            P(HEAD, None),
            P(),
            P(),
            P(),
            P(),
            P(("batch", "seq", *HEAD), None),
        ),
        out_specs=(
            P(("batch", "seq", *HEAD), None),
            P(("batch", "seq", *HEAD), None),
            P(("batch", "seq", *HEAD)),
            P(("batch", "seq"), HEAD),
            P(("batch", "seq"), HEAD),
            P(("batch", "seq"), HEAD),
            P(("batch", "seq"), HEAD),
            P(("batch", "seq"), HEAD),
            P(("batch", "seq"), HEAD),
            P(None, HEAD),
            P(None, HEAD),
            P(None, HEAD),
            P(HEAD),
            P(HEAD),
            P(HEAD, ("batch", "seq")),
            P(("batch", "seq", *HEAD)),
            P(("batch", "seq", *HEAD), None),
            P(("batch", "seq", *HEAD), None),
            P(None, ("batch", "seq", *HEAD)),
        ),
        check_vma=False,
    )
```

```python
import functools

import jax
import jax.numpy as jnp
from jax import lax
from jax.experimental import pallas as pl
from jax.experimental.pallas import tpu as pltpu
from jax.sharding import Mesh
from jax.sharding import PartitionSpec as P

bf16, f32, i32 = jnp.bfloat16, jnp.float32, jnp.int32
EPS = 1e-06
CT = 64
RIM = 16
NN = ((1,), (0,))
NT = ((1,), (1,))
MIB = 1 << 20
FORWARD, OUTPUT, ADJOINT, BACKWARD = 4, 4, 4, 4


def mm(a, b, dims=NN):
    return lax.dot_general(a, b, (dims, ((), ())), preferred_element_type=f32)


def split(x):
    high = x.astype(bf16)
    return high, (x - high.astype(f32)).astype(bf16)


def mm3(a, b, dims=NN):
    return mm(a[0], b[0], dims) + (mm(a[0], b[1], dims) + mm(a[1], b[0], dims))


def exact(a, b):
    return lax.dot_general(
        a, b, (NN, ((), ())), precision=lax.Precision.HIGHEST, preferred_element_type=f32
    )


def iota2(shape, dim):
    return lax.broadcasted_iota(i32, shape, dim)


def rows_of(c, size=CT, start=0):
    return pl.ds(pl.multiple_of(c * size + start, 16), size)


def near(c, start):
    return pl.ds(pl.multiple_of(c * CT + start, 8), CT + 8)


def step_order():
    size = 2 * CT
    row, col = iota2((size, size), 0), iota2((size, size), 1)
    row_tok, col_tok = row & (CT - 1), col & (CT - 1)
    later = jnp.where(row_tok > col_tok, row_tok ^ col_tok, 0)
    same_token = (row_tok == col_tok) & (row >= CT) & (col < CT)
    return row, col, later, same_token


def twice(x):
    return jnp.concatenate([x, x], 0)


def head_steps(ref, rows, h):
    return jnp.concatenate(
        [ref[rows, (2 * h + j) * 128 : (2 * h + j + 1) * 128] for j in range(2)], 0
    )


def decays(gam_ref, info, rows, h, nh):
    gcol = gam_ref[rows, 2 * nh + h : 2 * nh + h + 1]
    glast = gcol[CT - 1 : CT, :]
    carried = jnp.exp(gcol) * info[:, 4:5]
    tail = jnp.exp(jnp.minimum(glast - gcol, 0.0)) * info[:, 5:6]
    keep = carried[CT - 1 : CT, :]
    return gcol, carried, tail, keep


def forward_kernel(
    nh, count, me_ref, *refs
):
    tok_refs, refs = refs[:count], refs[count:]
    forward_body(nh, me_ref, tok_refs, *refs)


def forward_body(
    nh, me_ref, tok_refs, rim_ref, ng_ref, wq_ref, wk_ref, wv_ref, wg_ref, ws_ref, tq_ref, tk_ref, tv_ref,
    flags_ref, drow_ref, rate_ref,
    normed_ref, pre_ref, conv_ref, gate_ref, q_ref, k_ref, v_ref, beta_ref, glog_ref, gam_ref, dec_ref,
    t_ref, w_ref, u_ref, reach_ref, score_ref, at_ref, bt_ref, info_ref, low_ref, st_ref,
):
    length = pre_ref.shape[0] - RIM
    nc = length // CT
    gain = ng_ref[...]
    count = len(tok_refs)
    each = tok_refs[0].shape[0]

    def normal(x):
        x = x.astype(f32)
        scale = lax.rsqrt(jnp.mean(x * x, -1, keepdims=True) + EPS)
        return (x * scale * gain).astype(bf16)

    model = ng_ref.shape[1]
    normed_ref[0:RIM, :] = normal(rim_ref[:, :model])
    info_ref[...] = flags_ref[...]
    first = flags_ref[RIM : RIM + 8, :]
    ids = jnp.concatenate([rim_ref[8:, model : model + 8].astype(f32), first[:, 6:7] + jnp.zeros((8, 8), f32)], 0)
    row, col = iota2((8, 8), 0), iota2((8, 8), 1)
    for m in range(1, 4):
        same = (pltpu.roll(ids, m, 0)[8:] == ids[8:]).astype(f32)
        first = jnp.where((col == m) & (row < m), same, first)
    info_ref[RIM : RIM + 8, :] = first

    for shift, tok_ref in enumerate(tok_refs):
        place = lax.rem(me_ref[0] + (count - shift), count) * each

        def norm_rows(c, carry):
            target = pl.ds(pl.multiple_of(place + c * CT + RIM, 16), CT)
            normed_ref[target, :] = normal(tok_ref[rows_of(c), :])
            return carry

        lax.fori_loop(0, each // CT, norm_rows, 0)
    copies.done(normed_ref)
    copies.need(wq_ref, wk_ref, wv_ref, wg_ref, ws_ref)
    nq = nh * 128
    groups = ((wq_ref, 0, nq), (wk_ref, nq, 2 * nq), (wv_ref, 3 * nq, 2 * nq))

    for weight, first, width in groups:
        pre_ref[0:RIM, first : first + width] = (
            mm(normed_ref[0:RIM, :], weight[...]).astype(bf16).astype(f32)
        )

    def project(i, carry):
        rows = rows_of(i, 256, RIM)
        block = normed_ref[rows, :]
        for weight, first, width in groups:
            pre_ref[rows, first : first + width] = mm(block, weight[...]).astype(bf16).astype(f32)
        plain = rows_of(i, 256)
        gate_ref[plain, :] = mm(block, wg_ref[...])
        glog_ref[plain, :] = mm(block, ws_ref[...])
        return carry

    lax.fori_loop(0, length // 256, project, 0)
    copies.done(pre_ref, gate_ref)
    logits = glog_ref[...]
    beta_ref[...] = jax.nn.sigmoid(logits)
    soft = jnp.maximum(logits, 0.0) + jnp.log1p(jnp.exp(-jnp.abs(logits)))
    glog = rate_ref[...] * soft
    glog_ref[...] = glog
    tri = (iota2((CT, CT), 0) >= iota2((CT, CT), 1)).astype(f32)
    for c in range(nc):
        gam_ref[c * CT : (c + 1) * CT, :] = exact(tri, glog[c * CT : (c + 1) * CT, :])

    def conv_rows(c, carry):
        rows = rows_of(c)
        info = info_ref[rows_of(c, CT, RIM), :]
        mask = [info[:, m : m + 1] for m in range(4)]
        for tap_ref, first, count, kind in (
            (tq_ref, 0, nh, "q"), (tk_ref, nq, 2 * nh, "k"), (tv_ref, 3 * nq, 2 * nh, "v")
        ):
            for j in range(count):
                cols = slice(first + j * 128, first + (j + 1) * 128)
                mine = slice(j * 128, (j + 1) * 128)
                taps = tap_ref[:, mine].astype(f32)
                block = pre_ref[near(c, RIM - 8), cols]
                total = block[8:] * taps[0:1]
                for m in range(1, 4):
                    total = total + pltpu.roll(block, m, 0)[8:] * mask[m] * taps[m : m + 1]
                conv_ref[rows, cols] = total
                out = total * jax.nn.sigmoid(total)
                if kind == "k":
                    out = out * lax.rsqrt(jnp.sum(out * out, -1, keepdims=True) + EPS)
                {"q": q_ref, "k": k_ref, "v": v_ref}[kind][rows, mine] = out
        return carry

    lax.fori_loop(0, nc, conv_rows, 0)
    copies.done(conv_ref, q_ref, k_ref, v_ref, beta_ref, glog_ref, gam_ref)

    row, col, later, same_token = step_order()
    eye = (row == col).astype(f32)
    small_row, small_col = iota2((CT, CT), 0), iota2((CT, CT), 1)

    def prepare(group, carry):
        items = [(group * FORWARD + i, h) for i in range(FORWARD) for h in range(nh)]
        systems, rhs, tails, keeps = [], [], [], []
        for c, h in items:
            rows = rows_of(c)
            info = info_ref[rows_of(c, CT, RIM), :]
            same = (info[:, 6:7] == drow_ref[c]) & (small_row >= small_col)
            gcol, carried, tail, keep = decays(gam_ref, info, rows, h, nh)
            grow = jnp.sum(jnp.where(small_row == small_col, gcol, 0.0), 0, keepdims=True)
            decay = jnp.where(same, jnp.exp(jnp.minimum(gcol - grow, 0.0)), 0.0)
            wide = jnp.concatenate([decay, decay], 1)
            dec_ref[c, h] = wide
            key = head_steps(k_ref, rows, h)
            value = head_steps(v_ref, rows, h)
            beta = jnp.concatenate(
                [beta_ref[rows, 2 * h + j : 2 * h + j + 1] for j in range(2)], 0
            )
            key2 = split(key)
            query = q_ref[rows, h * 128 : (h + 1) * 128]
            query2 = split(query)
            pairs = mm3([jnp.concatenate(x, 0) for x in zip(key2, query2)], key2, NT)
            score_ref[c, h] = pairs[2 * CT :] * wide
            reach_ref[c, h] = query * carried
            systems.append(
                jnp.where((later > 0) | same_token, beta * pairs[: 2 * CT] * twice(wide), 0.0)
            )
            rhs.append(jnp.concatenate([beta * twice(carried) * key, beta * value], 1))
            tails.append(key * twice(tail))
            keeps.append(keep)
        inverse = [eye - jnp.where(same_token, n, 0.0) for n in systems]
        for level in range(6):
            part = (later >> level) == 1
            blocks = [split(jnp.where(part, n, 0.0)) for n in systems]
            inverse2 = [split(x) for x in inverse]
            first = [split(mm3(b, x)) for b, x in zip(blocks, inverse2)]
            inverse = [x - mm3(x2, y) for x, x2, y in zip(inverse, inverse2, first)]
        mixed = [mm3(split(x), split(r)) for x, r in zip(inverse, rhs)]
        products = [mm3(split(jnp.transpose(m)), split(t)) for m, t in zip(mixed, tails)]
        for n, (c, h) in enumerate(items):
            t_ref[c, h] = inverse[n]
            w_ref[c, h] = mixed[n][:, :128]
            u_ref[c, h] = mixed[n][:, 128:]
            at_ref[c, h] = keeps[n] * eye - products[n][:128]
            bt_ref[c, h] = products[n][128:]
        part = pl.ds(group * FORWARD, FORWARD)
        copies.done(dec_ref, score_ref, reach_ref, t_ref, w_ref, u_ref, at_ref, bt_ref, at=part)
        return carry

    lax.fori_loop(0, nc // FORWARD, prepare, 0)

    for h in range(nh):
        st_ref[h, :128] = at_ref[0, h]
        st_ref[h, 128:] = bt_ref[0, h]

    def chain(c, carry):
        for h in range(nh):
            after = mm3(split(st_ref[h]), split(at_ref[c, h]))
            st_ref[h, :128] = after[:128]
            st_ref[h, 128:] = after[128:] + bt_ref[c, h]
        return carry

    lax.fori_loop(1, nc, chain, 0)
    low_ref[...] = st_ref[...].astype(bf16)


def output_kernel(nh, count, blocks, me_ref, *refs):
    output_body(nh, me_ref, refs[:count], *refs[count : -blocks - 1], refs[-blocks - 1 : -1], refs[-1])


def output_body(
    nh, me_ref, map_refs, at_ref, bt_ref, w_ref, reach_ref, u_ref, score_ref, gate_ref, gain_ref, wout_ref,
    sin_ref, fresh_ref, core_ref, gated_ref, branch_refs, all_ref,
):
    nc = w_ref.shape[0]
    states = []
    for h in range(nh):
        state = jnp.zeros((128, 128), f32)
        for distance in range(len(map_refs), 0, -1):
            map_ref = map_refs[distance - 1]
            passed = split(map_ref[h, :128].astype(f32))
            state = mm3(split(state), passed) + map_ref[h, 128:].astype(f32)
            state = jnp.where(me_ref[2] >= distance, state, 0.0)
        states.append(state)

    def chain(c, states):
        out = []
        for h in range(nh):
            sin_ref[c, h] = states[h]
            out.append(mm3(split(states[h]), split(at_ref[c, h])) + bt_ref[c, h])
        return tuple(out)

    copies.need(at_ref, bt_ref)
    states = lax.fori_loop(0, nc, chain, tuple(states))
    for h in range(nh):
        sin_ref[nc, h] = states[h]
    copies.done(sin_ref)
    copies.need(w_ref, reach_ref, u_ref, score_ref, gate_ref)

    def outputs(group, carry):
        for c, h in [(group * OUTPUT + i, h) for i in range(OUTPUT) for h in range(nh)]:
            rows = rows_of(c)
            cols = slice(h * 128, (h + 1) * 128)
            state2 = split(sin_ref[c, h])
            probe = jnp.concatenate([w_ref[c, h], reach_ref[c, h]], 0)
            seen = mm3(split(probe), state2, NT)
            fresh = u_ref[c, h] - seen[: 2 * CT]
            fresh_ref[c, h] = fresh
            core = seen[2 * CT :] + mm3(split(score_ref[c, h]), split(fresh))
            core_ref[rows, cols] = core
            unit = core * lax.rsqrt(jnp.mean(core * core, -1, keepdims=True) + EPS)
            gate = gate_ref[rows, cols]
            gated_ref[rows, cols] = (
                unit * gain_ref[:, cols] * (gate * jax.nn.sigmoid(gate))
            ).astype(bf16)
        copies.done(fresh_ref, at=pl.ds(group * OUTPUT, OUTPUT))
        copies.done(core_ref, gated_ref, at=rows_of(group, OUTPUT * CT))
        return carry

    lax.fori_loop(0, nc // OUTPUT, outputs, 0)
    copies.need(wout_ref)
    all_ref[...] = mm(gated_ref[...], wout_ref[...]).astype(bf16)
    count = len(branch_refs)
    each = branch_refs[0].shape[0]
    for shift, branch_ref in enumerate(branch_refs):
        place = lax.rem(me_ref[0] + shift, count) * each
        branch_ref[...] = all_ref[pl.ds(pl.multiple_of(place, 16), each), :]
        copies.done(branch_ref)


def adjoint_kernel(nh, count, me_ref, *refs):
    adjoint_body(nh, me_ref, refs[:count], *refs[count:])


def adjoint_body(
    nh, me_ref, g_refs, wout_ref, core_ref, gate_ref, gain_ref, score_ref, reach_ref, w_ref, at_ref,
    dcore_ref, dft_ref, dt_ref, dgate_ref, dgain_ref, local_ref, all_ref,
    dgated_ref,
):
    nc = w_ref.shape[0]
    count = len(g_refs)
    each = g_refs[0].shape[0]
    for shift, g_ref in enumerate(g_refs):
        place = lax.rem(me_ref[0] + (count - shift), count) * each
        all_ref[pl.ds(pl.multiple_of(place, 16), each), :] = g_ref[...]
    copies.done(all_ref)
    copies.need(wout_ref)
    dgated_ref[...] = mm(all_ref[...], wout_ref[...], NT)
    copies.need(core_ref, gate_ref, score_ref, reach_ref, w_ref)

    def chunks(group, dgain):
        for i in range(ADJOINT):
            dgain = dgain + chunk(group * ADJOINT + i)
        copies.done(dft_ref, dt_ref, at=pl.ds(group * ADJOINT, ADJOINT))
        copies.done(dcore_ref, dgate_ref, at=rows_of(group, ADJOINT * CT))
        return dgain

    def chunk(c):
        rows = rows_of(c)
        sums = []
        for h in range(nh):
            cols = slice(h * 128, (h + 1) * 128)
            core = core_ref[rows, cols]
            scale = lax.rsqrt(jnp.mean(core * core, -1, keepdims=True) + EPS)
            unit = core * scale
            gate = gate_ref[rows, cols]
            sig = jax.nn.sigmoid(gate)
            silu = gate * sig
            gain = gain_ref[:, cols]
            grad = dgated_ref[rows, cols]
            sums.append(jnp.sum(grad * unit * silu, 0, keepdims=True))
            dgate_ref[rows, cols] = (
                grad * unit * gain * (sig * (1.0 + gate * (1.0 - sig)))
            ).astype(bf16)
            dunit = grad * gain * silu
            dcore = scale * (dunit - unit * jnp.mean(dunit * unit, -1, keepdims=True))
            dcore_ref[rows, cols] = dcore
            across = jnp.transpose(dcore)
            dft = mm3(split(across), split(score_ref[c, h]))
            dft_ref[c, h] = dft
            left = jnp.concatenate([-dft, across], 1)
            right = jnp.concatenate([w_ref[c, h], reach_ref[c, h]], 0)
            dt_ref[c, h] = mm3(split(left), split(right))
        return jnp.concatenate(sums, 1)

    dgain_ref[...] = lax.fori_loop(0, nc // ADJOINT, chunks, jnp.zeros(dgain_ref.shape, f32))

    copies.need(at_ref)

    def chain(i, carry):
        c = nc - 1 - i
        return tuple(
            mm3(split(carry[h]), split(at_ref[c, h]), NT) + dt_ref[c, h] for h in range(nh)
        )

    start = tuple(dt_ref[nc - 1, h] for h in range(nh))
    total = lax.fori_loop(1, nc, chain, start)
    for h in range(nh):
        local_ref[h] = total[h].astype(bf16)


def normed_back(count, place_ref, gp_ref, weights, normed_ref, gain_ref, mlp_ref, out_refs, all_ref):
    each = out_refs[0].shape[0] - RIM
    length = all_ref.shape[0] - RIM
    total = jnp.zeros(gain_ref.shape, f32)
    for start in range(0, length, 256):
        rows = slice(start + (RIM if start else 0), start + 256 + RIM)
        first = 0
        grad = None
        for weight in weights:
            width = weight.shape[1]
            term = mm(gp_ref[rows, first : first + width], weight[...], NT)
            grad = term if grad is None else grad + term
            first += width
        all_ref[rows, :] = grad.astype(bf16)
        total = total + jnp.sum(grad * normed_ref[rows, :].astype(f32), 0, keepdims=True)
    rim = all_ref[0:RIM, :].astype(f32)
    row = iota2((RIM, 1), 0)
    gains = [*split(total / gain_ref[...]), *split(mlp_ref[...])]
    for n, gain in enumerate(gains):
        rim = jnp.where(row == n, gain.astype(f32), rim)
    rim = rim.astype(bf16)
    for shift, out_ref in enumerate(out_refs):
        place = lax.rem(place_ref[0] + shift, count) * each + RIM
        out_ref[0:each, :] = all_ref[pl.ds(pl.multiple_of(place, 16), each), :]
        out_ref[each:, :] = rim
        copies.done(out_ref)


def turn(left_ref, turned_ref):
    tokens, width = left_ref.shape
    for n in range(width // 128):
        turned_ref[n * 128 : (n + 1) * 128, :tokens] = jnp.transpose(
            left_ref[:, n * 128 : (n + 1) * 128]
        )


def two_halves(place_ref, turned, right, own_ref, given_ref, cols):
    half = turned.shape[0] // 2
    for core, out_ref in ((place_ref[1], own_ref), (1 - place_ref[1], given_ref)):
        rows = pl.ds(pl.multiple_of(core * half, 16), half)
        out_ref[0:half, cols] = mm(turned[rows, : right.shape[0]], right[...]).astype(out_ref.dtype)


def two_parts(value):
    high, low = split(value)
    return jnp.concatenate([high, low], 0)


def backward_kernel(nh, count, blocks, *refs):
    at = 2 * count + 1
    maps, local_sums, place, refs = refs[:count], refs[count : at - 1], refs[at - 1], refs[at:]
    inputs, refs = refs[:21], refs[21:]
    dgate, weights, (normed, gain, mlp, dgain), refs = refs[0], refs[1:6], refs[6:10], refs[10:]
    (grad, gated), refs = refs[:2], refs[2:]
    out_refs, (own, given), refs = refs[:blocks], refs[blocks : blocks + 2], refs[blocks + 2 :]
    gp, taps, dlog, dconv, small, ends, everything, turned = refs
    half, width = own.shape[0] - 8, gp.shape[1]
    wide, nq = own.shape[1], gated.shape[1]
    gp[0:RIM, width - nq :] = jnp.zeros((RIM, nq), bf16)
    backward_body(nh, maps, local_sums, *inputs, gp, taps, dlog, dconv, small, ends)
    copies.need(dgate, normed, grad, gated)
    gp[RIM:, width - nq :] = dgate[...]
    turn(normed, turned)
    two_halves(place, turned, gp, own, given, slice(0, width))
    turn(grad, turned)
    two_halves(place, turned, gated, own, given, slice(width, wide))
    own[half:, :] = jnp.zeros((8, wide), f32)
    own[half : half + 4, : taps.shape[1]] = taps[...]
    own[half + 4 : half + 5, :128] = dlog[...]
    own[half + 4 : half + 5, 128 : 128 + dgain.shape[1]] = dgain[...]
    given[half:, :] = two_parts(own[half:, :])
    copies.done(given, own)
    copies.need(*weights)
    normed_back(blocks, place, gp, weights, normed, gain, mlp, out_refs, everything)


def backward_body(
    nh, map_refs, local_refs, at_ref, dt_ref, dft_ref, dcore_ref, t_ref, fresh_ref, sin_ref,
    q_ref, k_ref, v_ref, beta_ref, gam_ref, dec_ref, conv_ref, pre_ref, info_ref, tq_ref, tk_ref, tv_ref,
    rate_ref, glog_ref,
    gp_ref, taps_ref, dlog_ref,
    dconv_ref, small_ref, ends_ref,
):
    length = q_ref.shape[0]
    nc = length // CT
    nq = nh * 128
    width = 5 * nq
    ends = []
    for h in range(nh):
        end = local_refs[0][h].astype(f32)
        for map_ref, local_ref in zip(map_refs[1:], local_refs[1:]):
            passed = split(map_ref[h, :128].astype(f32))
            end = mm3(split(end), passed, NT) + local_ref[h].astype(f32)
        ends.append(end)
    row, col, later, same_token = step_order()
    before = (later > 0) | same_token
    last_row = (iota2((CT, 1), 0) == CT - 1).astype(f32)
    dconv_ref[0:RIM, :] = jnp.zeros((RIM, width), f32)
    dconv_ref[RIM + length :, :] = jnp.zeros((RIM, width), f32)
    lane = iota2((CT, 128), 1)
    upper = (iota2((CT, CT), 0) <= iota2((CT, CT), 1)).astype(f32)

    def chain(i, ends):
        c = nc - 1 - i
        out = []
        for h in range(nh):
            ends_ref[c, h] = ends[h]
            out.append(mm3(split(ends[h]), split(at_ref[c, h]), NT) + dt_ref[c, h])
        return tuple(out)

    copies.need(at_ref, dt_ref)
    lax.fori_loop(0, nc, chain, tuple(ends))
    copies.need(dft_ref, dcore_ref, t_ref, fresh_ref, sin_ref, q_ref, k_ref, v_ref, dec_ref, conv_ref)

    def chunks(group, carry):
        for i in range(BACKWARD):
            chunk(group * BACKWARD + i)
        return carry

    def chunk(c):
        rows = rows_of(c)
        store = rows_of(c, CT, RIM)
        info = info_ref[store, :]
        small = jnp.zeros((CT, 128), f32)
        dgam = jnp.zeros((CT, 128), f32)
        for h in range(nh):
            cols = slice(h * 128, (h + 1) * 128)
            end = ends_ref[c, h]
            end2 = split(end)
            _, carried, tail, _ = decays(gam_ref, info, rows, h, nh)
            carried2, tail2 = twice(carried), twice(tail)
            key = head_steps(k_ref, rows, h)
            value = head_steps(v_ref, rows, h)
            query = q_ref[rows, cols]
            beta = jnp.concatenate(
                [beta_ref[rows, 2 * h + j : 2 * h + j + 1] for j in range(2)], 0
            )
            wide = dec_ref[c, h]
            full = jnp.where(before, twice(wide), 0.0)
            state = sin_ref[c, h]
            fresh = fresh_ref[c, h]
            fresh2 = split(fresh)
            dcore = dcore_ref[rows, cols]
            dft = dft_ref[c, h] + mm3(end2, split(key * tail2), NT)
            solved = jnp.transpose(mm3(split(dft), split(t_ref[c, h])))
            both = split(jnp.concatenate([solved, dcore], 0))
            through = mm3(both, split(state))
            pairs = mm3(both, fresh2, NT)
            dtail = mm3(fresh2, end2)
            em = -pairs[: 2 * CT] * full
            ps = pairs[2 * CT :] * wide
            mixed = mm3(split(jnp.concatenate([em, ps], 0)), split(key))
            turned = jnp.transpose(jnp.concatenate([beta * em, ps], 0))
            dkb = mm3(split(turned), split(jnp.concatenate([key, query], 0))) + tail2 * dtail
            x1 = mixed[: 2 * CT] - carried2 * through[: 2 * CT]
            dka = beta * x1
            dkey = dka + dkb
            dbeta = jnp.sum(key * x1 + solved * value, -1, keepdims=True)
            dvalue = beta * solved
            dquery = mixed[2 * CT :] + carried * through[2 * CT :]
            turn = jnp.sum(key * (dka - dkb), -1, keepdims=True)
            closing = jnp.sum(
                jnp.sum(end * sin_ref[c + 1, h], -1, keepdims=True), 0, keepdims=True
            )
            dg = (
                jnp.sum(query * dquery, -1, keepdims=True)
                + turn[:CT]
                + turn[CT:]
                + last_row * closing
            )
            dgam = jnp.where(lane == 2 * nh + h, dg, dgam)
            for j in range(2):
                small = jnp.where(lane == 2 * h + j, dbeta[j * CT : (j + 1) * CT], small)
            pre = conv_ref[rows, cols]
            sig = jax.nn.sigmoid(pre)
            dconv_ref[store, cols] = dquery * (sig * (1.0 + pre * (1.0 - sig)))
            for j in range(2):
                kcols = slice(nq + (2 * h + j) * 128, nq + (2 * h + j + 1) * 128)
                pre = conv_ref[rows, kcols]
                sig = jax.nn.sigmoid(pre)
                act = pre * sig
                scale = lax.rsqrt(jnp.sum(act * act, -1, keepdims=True) + EPS)
                unit = key[j * CT : (j + 1) * CT]
                grad = dkey[j * CT : (j + 1) * CT]
                grad = scale * (grad - unit * jnp.sum(unit * grad, -1, keepdims=True))
                dconv_ref[store, kcols] = grad * (sig * (1.0 + pre * (1.0 - sig)))
                vcols = slice(3 * nq + (2 * h + j) * 128, 3 * nq + (2 * h + j + 1) * 128)
                pre = conv_ref[rows, vcols]
                sig = jax.nn.sigmoid(pre)
                dconv_ref[store, vcols] = dvalue[j * CT : (j + 1) * CT] * (
                    sig * (1.0 + pre * (1.0 - sig))
                )
        dglog = exact(upper, dgam)
        small_ref[rows, :] = jnp.where(lane < 2 * nh, small, dglog)

    lax.fori_loop(0, nc // BACKWARD, chunks, 0)

    copies.need(pre_ref, glog_ref)
    beta = beta_ref[...]
    small = small_ref[...]
    lanes = iota2(beta.shape, 1)
    grads = small * beta * jnp.where(lanes < 2 * nh, 1.0 - beta, rate_ref[...])
    dlog_ref[...] = jnp.sum(small * glog_ref[...], 0, keepdims=True)
    gp_ref[0:RIM, 0 : width + 128] = jnp.zeros((RIM, width + 128), bf16)
    gp_ref[RIM:, width : width + 128] = grads.astype(bf16)
    groups = ((tq_ref, 0, nh), (tk_ref, nq, 2 * nh), (tv_ref, 3 * nq, 2 * nh))

    def turned_back(grad, masks, taps, count):
        total = grad[:count] * taps[0:1]
        size = grad.shape[0]
        for m in range(1, 4):
            moved = pltpu.roll(grad * masks[:, m : m + 1], size - m, 0)
            total = total + moved[:count] * taps[m : m + 1]
        return total

    def conv_back(c, sums):
        info = info_ref[near(c, RIM), :]
        new = []
        for tap_ref, first, count in groups:
            for j in range(count):
                cols = slice(first + j * 128, first + (j + 1) * 128)
                taps = tap_ref[:, j * 128 : (j + 1) * 128].astype(f32)
                grad = dconv_ref[near(c, RIM), cols]
                gp_ref[rows_of(c, CT, RIM), cols] = turned_back(grad, info, taps, CT).astype(bf16)
                block = pre_ref[near(c, RIM - 8), cols]
                parts = [jnp.sum(grad[:CT] * block[8:], 0, keepdims=True)]
                for m in range(1, 4):
                    moved = pltpu.roll(block, m, 0)[8:]
                    parts.append(
                        jnp.sum(grad[:CT] * info[:CT, m : m + 1] * moved, 0, keepdims=True)
                    )
                new.append(jnp.concatenate(parts, 0))
        return sums + jnp.concatenate(new, 1)

    taps_ref[...] = lax.fori_loop(0, nc, conv_back, jnp.zeros((4, width), f32))
    for tap_ref, first, count in groups:
        cols = slice(first, first + count * 128)
        taps = tap_ref[...].astype(f32)
        early = slice(8, 24)
        rim = turned_back(dconv_ref[early, cols], info_ref[early, :], taps, 8)
        gp_ref[0:RIM, cols] = jnp.concatenate([jnp.zeros_like(rim), rim], 0).astype(bf16)


VMEM = pl.BlockSpec(memory_space=pltpu.VMEM)
SMEM = pl.BlockSpec(memory_space=pltpu.SMEM)
ANY = pl.BlockSpec(memory_space=pl.ANY)


class Late:
    def __init__(self, value):
        self.value = value


def late(*values):
    return [Late(value) for value in values]


class Copies:
    def __init__(self):
        self.coming, self.going = {}, {}

    def need(self, *refs):
        for ref in refs:
            copy = self.coming.pop(id(ref), None)
            if copy is not None:
                copy.wait()

    def done(self, *refs, at=None):
        for ref in refs:
            entry = self.going.get(id(ref))
            if entry is None:
                continue
            target, sem, _ = entry
            source = ref
            if at is not None:
                source, target = ref.at[at], target.at[at]
            pltpu.make_async_copy(source, target, sem).start()
            self.going[id(ref)] = (entry[0], sem, True)

    def finish(self, refs):
        for copy in self.coming.values():
            copy.wait()
        self.coming = {}
        for ref in refs:
            if id(ref) in self.going and not self.going[id(ref)][2]:
                self.done(ref)
        for ref in refs:
            if id(ref) in self.going:
                target, sem, _ = self.going.pop(id(ref))
                pltpu.make_async_copy(ref, target, sem).wait()


copies = Copies()


def kernel_call(body, name, args, outs, scratch=(), after=(), hbm=(), mib=24, cost=2):
    late_in = [n for n, a in enumerate(args) if isinstance(a, Late)]
    late_out = [n for n, s in enumerate(outs) if isinstance(s, Late)]
    args = [a.value if isinstance(a, Late) else a for a in args]
    outs = [s.value if isinstance(s, Late) else s for s in outs]
    extra, n_in, n_out, n_scratch = len(after), len(args), len(outs), len(scratch)
    buffers = [pltpu.VMEM(args[n].shape, args[n].dtype) for n in late_in]
    buffers += [pltpu.VMEM(outs[n].shape, outs[n].dtype) for n in late_out]
    sems = [pltpu.SemaphoreType.DMA((len(late_in) + len(late_out),))] if buffers else []

    def run(*refs):
        in_refs, refs = list(refs[:n_in]), refs[n_in + extra :]
        out_refs, refs = list(refs[:n_out]), refs[n_out:]
        own_scratch, refs = refs[:n_scratch], refs[n_scratch:]
        held = []
        for k, n in enumerate(late_in):
            copy = pltpu.make_async_copy(in_refs[n], refs[k], refs[-1].at[k])
            copy.start()
            copies.coming[id(refs[k])] = copy
            in_refs[n] = refs[k]
        for k, n in enumerate(late_out, len(late_in)):
            copies.going[id(refs[k])] = (out_refs[n], refs[-1].at[k], False)
            out_refs[n] = refs[k]
            held.append(refs[k])
        body(*in_refs, *out_refs, *own_scratch)
        copies.finish(held)

    in_specs = [SMEM if a.dtype == i32 else VMEM for a in args]
    out_specs = [VMEM] * n_out
    for n in (*late_in, *hbm):
        in_specs[n] = ANY
    for n in late_out:
        out_specs[n] = ANY
    return pl.pallas_call(
        run,
        name=name,
        in_specs=in_specs + [ANY] * extra,
        out_specs=out_specs,
        out_shape=outs,
        scratch_shapes=[*scratch, *buffers, *sems],
        compiler_params=pltpu.CompilerParams(vmem_limit_bytes=mib * MIB),
        cost_estimate=pl.CostEstimate(flops=cost * 10**9, bytes_accessed=0, transcendentals=0),
    )(*args, *after)


def sds(*shape, dtype=f32):
    return jax.ShapeDtypeStruct(shape, dtype)


def mixer_forward(me, tokens, rim, norm_gain, weights, taps, info, doc_rows, rate):
    length, width = tokens[0].shape
    length *= len(tokens)
    w_query, w_key, w_value, w_outgate, w_small = weights
    nh = w_query.shape[1] // 128
    nc, nq = length // CT, nh * 128
    per = (nc, nh)
    outs = dict(
        normed=sds(RIM + length, width, dtype=bf16),
        pre=sds(RIM + length, 5 * nq),
        conv=sds(length, 5 * nq),
        gate=sds(length, nq),
        q=sds(length, nq),
        k=sds(length, 2 * nq),
        v=sds(length, 2 * nq),
        beta=sds(length, 128),
        glog=sds(length, 128),
        gam=sds(length, 128),
        dec=sds(*per, CT, 128),
        t=sds(*per, 128, 128),
        w=sds(*per, 128, 128),
        u=sds(*per, 128, 128),
        reach=sds(*per, CT, 128),
        score=sds(*per, CT, 128),
        at=sds(*per, 128, 128),
        bt=sds(*per, 128, 128),
        info=sds(length + 2 * RIM, 8),
        low=sds(nh, 256, 128, dtype=bf16),
    )
    args = (
        me, *tokens, rim, norm_gain, *late(w_query, w_key, w_value, w_outgate, w_small), *taps, info, doc_rows,
        rate,
    )
    res = kernel_call(
        functools.partial(forward_kernel, nh, len(tokens)), "mixer_forward", args,
        [s if n in ("info", "low") else Late(s) for n, s in outs.items()],
        cost=25, mib=60,
        scratch=[pltpu.VMEM((nh, 256, 128), f32)],
    )
    return dict(zip(outs, res))


def mixer_output(me, maps, fwd, out_gain, w_out, blocks, after=()):
    nc, nh = fwd["w"].shape[:2]
    length = nc * CT
    outs = dict(
        sin=sds(nc + 1, nh, 128, 128),
        fresh=sds(nc, nh, 128, 128),
        core=sds(length, nh * 128),
        gated=sds(length, nh * 128, dtype=bf16),
    )
    parts = [sds(length // blocks, w_out.shape[1], dtype=bf16)] * blocks
    names = ("at", "bt", "w", "reach", "u", "score", "gate")
    args = (me, *maps, *late(*(fwd[n] for n in names)), out_gain, *late(w_out))
    res = kernel_call(
        functools.partial(output_kernel, nh, len(maps), blocks), "mixer_output", args,
        late(*outs.values(), *parts), cost=10, mib=60,
        scratch=[pltpu.VMEM((length, w_out.shape[1]), bf16)],
        after=after,
    )
    return dict(zip(outs, res), branch=res[len(outs) :])


def mixer_adjoint(me, grad, w_out, fwd, out, out_gain, after=()):
    nc, nh = fwd["w"].shape[:2]
    length = nc * CT
    outs = dict(
        dcore=sds(length, nh * 128),
        dft=sds(nc, nh, 128, 128),
        dt=sds(nc, nh, 128, 128),
        dgate=sds(length, nh * 128, dtype=bf16),
        dgain=sds(1, nh * 128),
        local=sds(nh, 128, 128, dtype=bf16),
        g=sds(length, w_out.shape[1], dtype=bf16),
    )
    args = (
        me, *grad, *late(w_out, out["core"], fwd["gate"]), out_gain,
        *late(*(fwd[n] for n in ("score", "reach", "w", "at"))),
    )
    res = kernel_call(
        functools.partial(adjoint_kernel, nh, len(grad)), "mixer_adjoint", args,
        [s if n in ("dgain", "local") else Late(s) for n, s in outs.items()],
        cost=10, mib=60,
        scratch=[pltpu.VMEM((length, nh * 128), f32)],
        after=after,
    )
    return dict(zip(outs, res))


def mixer_backward(
    place, maps, local_sums, fwd, out, adj, taps, rate, weights, gain, mlp, blocks, after=()
):
    nc, nh = fwd["w"].shape[:2]
    length, nq = nc * CT, nh * 128
    width = 5 * nq
    model = gain.shape[1]
    parts = [sds(RIM + length // blocks, model, dtype=bf16)] * blocks
    columns = width + 128 + 2 * nq
    halves = [sds(model // 2 + 8, columns), sds(model // 2 + 16, columns, dtype=bf16)]
    args = (
        *maps, *local_sums, place,
        *late(
            fwd["at"], adj["dt"], adj["dft"], adj["dcore"], fwd["t"], out["fresh"], out["sin"],
            *(fwd[n] for n in ("q", "k", "v")),
        ),
        fwd["beta"], fwd["gam"], *late(fwd["dec"], fwd["conv"], fwd["pre"]), fwd["info"], *taps, rate,
        *late(fwd["glog"], adj["dgate"], *weights, fwd["normed"]), gain, mlp, adj["dgain"],
        *late(adj["g"], out["gated"]),
    )
    *res, own, given = kernel_call(
        functools.partial(backward_kernel, nh, len(maps), blocks), "mixer_backward", args,
        late(*parts, *halves), cost=300, mib=60,
        scratch=[
            pltpu.VMEM((RIM + length, width + 128 + nq), bf16), pltpu.VMEM((4, width), f32),
            pltpu.VMEM((1, 128), f32),
            pltpu.VMEM((length + 2 * RIM, width), f32), pltpu.VMEM((length, 128), f32),
            pltpu.VMEM((nc, nh, 128, 128), f32), pltpu.VMEM((RIM + length, model), bf16),
            pltpu.VMEM((model, RIM + length), bf16),
        ],
        after=after,
    )
    return res, (own, given)


def token_info(doc_ids):
    ids = doc_ids.astype(f32)
    length = ids.shape[0]
    extended = jnp.concatenate([ids[:3], ids])
    masks = [(extended[3 - m : 3 - m + length] == ids).astype(f32) for m in range(4)]
    blocks = ids.reshape(-1, CT)
    last = blocks[:, -1:]
    previous = jnp.concatenate([blocks[:1, :1], last[:-1]], 0)
    columns = masks + [
        (blocks == previous).astype(f32).reshape(-1),
        (blocks == last).astype(f32).reshape(-1),
        ids,
        jnp.zeros_like(ids),
    ]
    info = jnp.pad(jnp.stack(columns, 1), ((RIM, RIM), (0, 0)))
    return info, blocks[:, None, :]


def middle_kernel(count, tok_ref, *refs):
    parts, (gain_ref, middle_ref, normed_ref) = refs[:count], refs[count:]
    middle = tok_ref[...].astype(f32)
    total = parts[0][...].astype(f32)
    for part in parts[1:]:
        total = total + part[...].astype(f32)
    middle = middle + total
    middle_ref[...] = middle
    scale = lax.rsqrt(jnp.mean(middle * middle, -1, keepdims=True) + EPS)
    normed_ref[...] = (middle * scale * gain_ref[...]).astype(bf16)


def feed_kernel(hidden, place_ref, *refs):
    x_refs, cot_refs, weights, refs = refs[:4], refs[4:8], refs[8:11], refs[11:]
    norm_refs, block_refs, cols_ref, refs = refs[:4], refs[4:8], refs[8], refs[9:]
    gate_w, up_w, down_w, sems = refs
    width = gate_w.shape[1]
    each = x_refs[0].shape[0]
    start = pl.multiple_of(place_ref[3], 128)
    window = pl.ds(start, width)
    copies = [
        pltpu.make_async_copy(weights[0].at[:, window], gate_w, sems.at[0]),
        pltpu.make_async_copy(weights[1].at[:, window], up_w, sems.at[1]),
        pltpu.make_async_copy(weights[2].at[window, :], down_w, sems.at[2]),
    ]
    for copy in copies:
        copy.start()
    lane = iota2((1, width), 1) - place_ref[4]
    mask = ((lane >= 0) & (lane < hidden)).astype(f32)
    for n, pair in enumerate(((1, 3), (0, 2))):
        x = jnp.concatenate([x_refs[p][...] for p in pair], 0)
        cot = jnp.concatenate([cot_refs[p][...] for p in pair], 0)
        if n == 0:
            copies[0].wait()
        gate = mm(x, gate_w[...])
        if n == 0:
            copies[1].wait()
        up = mm(x, up_w[...]) * mask
        sig = jax.nn.sigmoid(gate)
        silu = gate * sig * mask
        act = (silu * up).astype(bf16)
        if n == 0:
            copies[2].wait()
        grad = mm(cot, down_w[...], NT)
        ggate = (grad * up * sig * (1.0 + gate * (1.0 - sig))).astype(bf16)
        gup = (grad * silu).astype(bf16)
        gnorm = (mm(ggate, gate_w[...], NT) + mm(gup, up_w[...], NT)).astype(bf16)
        block = mm(act, down_w[...]).astype(bf16)
        for n, p in enumerate(pair):
            half, at = slice(n * each, (n + 1) * each), slice(p * each, (p + 1) * each)
            norm_refs[p][...] = gnorm[half]
            block_refs[p][...] = block[half]
            for k, value in enumerate((ggate, gup, act)):
                cols_ref[k, at, :] = value[half]


def with_bit(index, position, bit):
    low = index & ((1 << position) - 1)
    return ((index >> position) << (position + 1)) + bit * (1 << position) + low


def seq_bit(place_ref, bit):
    return lax.rem(lax.div(place_ref[2], 1 << bit), 2)


def feed_grads_kernel(bits, place_ref, *refs):
    x_refs, cot_refs, cols_ref, refs = refs[:4], refs[4:8], refs[8], refs[9:]
    out_refs, (turned_ref, full_ref) = refs[:-2], refs[-2:]
    each = x_refs[0].shape[0]
    half = full_ref.shape[0]
    rows = half >> bits
    for n, blocks in enumerate((x_refs, cot_refs)):
        for p, ref in enumerate(blocks):
            turned_ref[n, :, p * each : (p + 1) * each] = jnp.transpose(ref[...])
    for k in range(3):
        for b in range(2):
            left = turned_ref[k // 2, b * half : (b + 1) * half, :]
            copies.need(cols_ref)
            full_ref[...] = mm(left, cols_ref[k]).astype(bf16)
            position = (bits - 1) * b
            mine = seq_bit(place_ref, position)
            for n, bit in enumerate((mine, 1 - mine)):
                out_ref = out_refs[2 * b + n]
                for i in range(1 << (bits - 1)):
                    at = with_bit(i, position, bit) * rows
                    first = (k * (1 << (bits - 1)) + i) * rows
                    out_ref[first : first + rows, :] = full_ref[
                        pl.ds(pl.multiple_of(at, rows), rows), :
                    ]


def feed_seq_kernel(bits, left, place_ref, *refs):
    in_refs, out_refs, (sum_ref,) = refs[:4], refs[4:8], refs[8:]
    for b in range(2):
        sum_ref[...] = in_refs[2 * b][...].astype(f32) + in_refs[2 * b + 1][...].astype(f32)
        rows = sum_ref.shape[0] // (3 << left)
        position = (left - 1) * b
        mine = seq_bit(place_ref, bits - left if b == 0 else left - 1)
        for n, bit in enumerate((mine, 1 - mine)):
            out_ref = out_refs[2 * b + n]
            for k in range(3):
                for i in range(1 << (left - 1)):
                    at = ((k << left) + with_bit(i, position, bit)) * rows
                    first = ((k << (left - 1)) + i) * rows
                    out_ref[first : first + rows, :] = sum_ref[
                        pl.ds(pl.multiple_of(at, rows), rows), :
                    ].astype(bf16)


def feed_head_kernel(pairs, place_ref, *refs):
    in_refs, out_refs, (sum_ref,) = refs[:4], refs[4:-1], refs[-1:]
    size = in_refs[0].shape[0]
    for b in range(2):
        sum_ref[b * size : (b + 1) * size, :] = in_refs[2 * b][...].astype(f32) + in_refs[
            2 * b + 1
        ][...].astype(f32)
    rows = out_refs[0].shape[0] // 6
    for shift, out_ref in enumerate(out_refs):
        at = lax.rem(lax.div(place_ref[0], 2) + shift, pairs) * rows
        for n in range(6):
            piece = sum_ref[pl.ds(pl.multiple_of(at + n * rows * pairs, rows), rows), :]
            out_ref[n * rows : (n + 1) * rows, :] = piece.astype(bf16)


def feed_pair_kernel(count, place_ref, *refs):
    parts, out_refs, (sum_ref,) = refs[:count], refs[count:-1], refs[-1:]
    sum_ref[...] = add_up([part[...] for part in parts])
    rows = out_refs[0].shape[0] // 6
    for other, out_ref in enumerate(out_refs):
        odd = lax.rem(place_ref[0] + other, 2) == 1
        for n in range(2):
            core = lax.rem(place_ref[1] + n, 2)
            for k in range(3):
                both = sum_ref[pl.ds(pl.multiple_of((core * 3 + k) * 2 * rows, 2 * rows), 2 * rows), :]
                first = (n * 3 + k) * rows
                value = jnp.where(odd, both[rows:], both[:rows])
                out_ref[first : first + rows, :] = value.astype(bf16)


def feed_out_kernel(hidden, place_ref, *refs):
    parts, (gate_ref, up_ref, down_ref) = refs[:4], refs[4:]
    rows = parts[0].shape[0] // 6
    own = lax.rem(place_ref[0], 2) * 2 + place_ref[1]
    for k, out_ref in enumerate((gate_ref, up_ref, down_ref)):
        values = [
            part[(n % 2 * 3 + k) * rows : (n % 2 * 3 + k + 1) * rows, :].astype(f32)
            for n, part in enumerate(parts)
        ]
        for g in range(4):
            value = values[0]
            for n in range(1, 4):
                value = jnp.where(own == (g ^ n), values[n], value)
            start = g * hidden % 128
            value = value[:, start : start + hidden]
            out_ref[:, g * hidden : (g + 1) * hidden] = value


def mixer_blocks_kernel(place_ref, own_ref, got_ref, *refs):
    extra = 8
    *out_refs, mine_ref, theirs_ref, sems = refs
    count = len(out_refs)
    rows = (own_ref.shape[0] - extra) // count
    last = (rows * count, extra)
    moves = []
    for shift in range(count + 1):
        at = pl.multiple_of(lax.rem(place_ref[2] + shift, count) * rows, 16)
        first, size = (at, rows) if shift < count else last
        to = shift * rows
        wide = size if shift < count else 2 * size
        moves.append(
            (
                pltpu.make_async_copy(
                    own_ref.at[pl.ds(first, size), :], mine_ref.at[to : to + size, :], sems.at[0, shift]
                ),
                pltpu.make_async_copy(
                    got_ref.at[pl.ds(first, wide), :], theirs_ref.at[to : to + wide, :], sems.at[1, shift]
                ),
            )
        )
    for shift in (count, *range(count)):
        for move in moves[shift]:
            move.start()
    for shift in (count, *range(count)):
        for move in moves[shift]:
            move.wait()
        if shift == count:
            small = mine_ref[last[0] :, :] + joined_parts(theirs_ref, last[0], extra)
            continue
        at = slice(shift * rows, (shift + 1) * rows)
        out_ref = out_refs[shift]
        out_ref[0:rows, :] = (mine_ref[at, :] + theirs_ref[at, :].astype(f32)).astype(out_ref.dtype)
        out_ref[rows:, :] = two_parts(small) if shift else small
        copies.done(out_ref)


def joined_parts(ref, start, extra):
    both = ref[start : start + 2 * extra, :].astype(f32)
    return both[:extra] + both[extra:]


def mixer_sum_kernel(count, nh, *refs):
    parts, out_refs = refs[:count], refs[count:]
    weight_refs, conv_refs, (decay_ref, gain_ref) = out_refs[:7], out_refs[7:10], out_refs[10:]
    rows = weight_refs[0].shape[0]
    nq = nh * 128
    starts = (0, nq, 3 * nq, 5 * nq, 5 * nq + 2 * nh, 5 * nq + 128, 6 * nq + 128)
    for n, (start, out_ref) in enumerate(zip(starts, weight_refs)):
        turned = n in (3, 4, 6)
        width = out_ref.shape[0] if turned else out_ref.shape[1]
        total = add_up([part[0:rows, start : start + width] for part in parts])
        out_ref[...] = jnp.transpose(total) if turned else total
    small = parts[0][rows:, :]
    for part in parts[1:]:
        small = small + joined_parts(part, rows, 8)
    for start, out_ref in zip(starts, conv_refs):
        out_ref[...] = small[0:4, start : start + out_ref.shape[1]]
    decay_ref[...] = small[4:5, 2 * nh : 3 * nh]
    gain_ref[...] = small[4:5, 128 : 128 + nq]


def norm_back(grad_normed, rows, gain):
    scale = lax.rsqrt(jnp.mean(rows * rows, -1, keepdims=True) + EPS)
    unit = rows * scale
    scaled = grad_normed * gain
    grad_rows = scale * (scaled - unit * jnp.mean(scaled * unit, -1, keepdims=True))
    return grad_rows, jnp.sum(grad_normed * unit, 0, keepdims=True)


def middle_back_kernel(a_ref, b_ref, c_ref, middle_ref, cot_ref, gain_ref, grad_ref, low_ref, sum_ref):
    total = a_ref[...].astype(f32) + b_ref[...].astype(f32) + c_ref[...].astype(f32)
    rows, sum_ref[...] = norm_back(total, middle_ref[...], gain_ref[...])
    grad = cot_ref[...].astype(f32) + rows
    grad_ref[...] = grad
    low_ref[...] = grad.astype(bf16)


def extra_rows_kernel(count, *refs):
    parts, (rim_ref, gains_ref) = refs[:count], refs[count:]
    each = parts[0].shape[0] - RIM
    total = add_up([part[each:, :] for part in parts])
    row = iota2((RIM, 1), 0)
    rim_ref[...] = jnp.where(row >= RIM - 3, total, 0.0).astype(bf16)
    gains_ref[...] = jnp.zeros(gains_ref.shape, f32)
    for n in range(2):
        gains_ref[n : n + 1, :] = total[2 * n : 2 * n + 1] + total[2 * n + 1 : 2 * n + 2]


def tokens_back_kernel(count, *refs):
    parts, (rim_ref, tok_ref, gain_ref, middle_ref, grad_ref) = refs[:count], refs[count:]
    each = tok_ref.shape[0]
    total = add_up([part[0:each, :] for part in parts])
    rim = rim_ref[...].astype(f32)
    total = total + jnp.concatenate([jnp.zeros((each - RIM, rim.shape[1]), f32), rim], 0)
    rows, _ = norm_back(total, tok_ref[...].astype(f32), gain_ref[...])
    grad_ref[...] = middle_ref[...] + rows


HEAD = ("pair", "half")


def axis_size(axis):
    return lax.axis_size(axis) if isinstance(axis, str) else lax.psum(1, axis)


def ring(value, axis):
    count = axis_size(axis)
    return [value] + [
        lax.ppermute(value, axis, [(i, (i + shift) % count) for i in range(count)])
        for shift in range(1, count)
    ]


def along(value, axis, shift):
    count = axis_size(axis)
    pairs = [(i, i + shift) for i in range(count) if 0 <= i + shift < count]
    return lax.ppermute(value, axis, pairs)


def crossed(value, axis, bit=0):
    return lax.ppermute(value, axis, [(i, i ^ (1 << bit)) for i in range(axis_size(axis))])


def spread(blocks, axis):
    count = axis_size(axis)
    return [blocks[0]] + [
        lax.ppermute(blocks[shift], axis, [(i, (i + shift) % count) for i in range(count)])
        for shift in range(1, count)
    ]


def add_up(parts):
    total = parts[0].astype(f32)
    for part in parts[1:]:
        total = total + part.astype(f32)
    return total


def sum_over(value, axis):
    return add_up(ring(value, axis))


def tied(*values):
    return lax.optimization_barrier(values)


def on_device(
    tokens, doc_ids, norm_gain, w_query, w_key, w_value, w_beta, w_decay, w_outgate, conv_query,
    conv_key, conv_value, decay_log, out_gain, w_out, mlp_gain, w_gate, w_up, w_down, cotangent,
):
    head_n, seq_n, batch_n = (axis_size(a) for a in (HEAD, "seq", "batch"))
    me = lax.axis_index(HEAD)
    nh = w_decay.shape[1]
    nq = nh * 128
    each, model = tokens.shape
    length = each * head_n
    me_array = me.astype(i32).reshape(1)

    head_last = head_n - 1
    blocks = ring(tokens, HEAD)
    seq_place = lax.axis_index("seq")
    core = lax.axis_index("batch")
    ways = 2 * batch_n
    hidden = w_gate.shape[1] // ways
    mine = ((me & 1) * batch_n + core) * hidden
    place = jnp.stack([me, core, seq_place, mine // 128 * 128, mine % 128]).astype(i32)
    window = -(-(hidden + 64) // 128) * 128
    ids = jnp.broadcast_to(doc_ids[-RIM:, None], (RIM, 128)).astype(bf16)
    tail = tied(jnp.concatenate([tokens[-RIM:], ids], 1), blocks[1])[0]
    rim = add_up(
        [
            lax.ppermute(
                tail,
                ("seq", *HEAD),
                [(s * head_n + head_last, (s + 1) * head_n + h) for s in range(seq_n - 1)],
            )
            for h in range(head_n)
        ]
    ).astype(bf16)
    info, doc_rows = token_info(doc_ids)
    w_small = jnp.pad(jnp.concatenate([w_beta, w_decay], 1), ((0, 0), (0, 128 - 3 * nh)))
    rate = jnp.pad(-jnp.exp(decay_log), (2 * nh, 128 - 3 * nh))[None]
    weights = (w_query, w_key, w_value, w_outgate, w_small)
    taps = (conv_query, conv_key, conv_value)
    gain = norm_gain[None]
    fwd = mixer_forward(me_array, blocks, rim, gain, weights, taps, info, doc_rows, rate)

    states = ring(fwd["low"], "seq")
    cot_near = crossed(tied(cotangent, *blocks[1:])[0], HEAD)
    cot_sent = tied(cotangent, cot_near, fwd["low"])
    cots = [cotangent, cot_near, *[crossed(value, "batch") for value in cot_sent[:2]]]
    out = mixer_output(place, states[1:], fwd, out_gain[None], w_out, head_n, after=cots[1:])

    low = lambda *shape: sds(*shape, dtype=bf16)
    parts = spread(out["branch"], HEAD)
    middle, normed_mid = kernel_call(
        functools.partial(middle_kernel, len(parts)), "middle",
        (tokens, *parts, mlp_gain[None]), [sds(each, model), low(each, model)],
    )
    near = crossed(normed_mid, HEAD)
    rows = [normed_mid, near, crossed(normed_mid, "batch"), crossed(near, "batch")]
    fed = pl.pallas_call(
        functools.partial(feed_kernel, hidden),
        name="feed",
        in_specs=[SMEM] + [VMEM] * 8 + [ANY] * 3,
        out_specs=[VMEM] * 9,
        out_shape=[low(each, model)] * 8 + [low(3, 4 * each, window)],
        scratch_shapes=[
            pltpu.VMEM((model, window), bf16), pltpu.VMEM((model, window), bf16),
            pltpu.VMEM((window, model), bf16), pltpu.SemaphoreType.DMA((3,)),
        ],
        compiler_params=pltpu.CompilerParams(vmem_limit_bytes=40 * MIB),
        cost_estimate=pl.CostEstimate(flops=10**10, bytes_accessed=0, transcendentals=0),
    )(place, *rows, *cots, w_gate, w_up, w_down)

    def own_parts(blocks):
        given = (blocks[1].astype(f32) + crossed(blocks[3], "batch").astype(f32)).astype(bf16)
        return given, (blocks[0], crossed(blocks[2], "batch"), crossed(given, HEAD))

    given, norm_parts = own_parts(fed[:4])
    block_own = crossed(fed[6], "batch")
    block_given = (fed[5].astype(f32) + crossed(fed[7], "batch").astype(f32)).astype(bf16)

    seq_rows = model // (batch_n * seq_n)
    seq_bits = seq_n.bit_length() - 1
    size = 3 * model // 4
    feed_kept = kernel_call(
        functools.partial(feed_grads_kernel, seq_bits), "feed_grads",
        (place, *rows, *cots, *late(fed[8])), late(*[low(size, window)] * 4),
        scratch=[
            pltpu.VMEM((2, model, 4 * each), bf16), pltpu.VMEM((model // 2, window), bf16),
        ],
        after=[given],
    )

    def exchanged(values, step):
        bits = (step, seq_bits - 1 - step)
        return [
            value
            for b in range(2)
            for value in (values[2 * b], crossed(values[2 * b + 1], "seq", bits[b]))
        ]

    grad_middle, grad_branch, grad_mlp_gain = kernel_call(
        middle_back_kernel, "middle_back",
        (*norm_parts, middle, cotangent, mlp_gain[None]),
        [sds(each, model), low(each, model), sds(1, model)],
        after=feed_kept[1::2], cost=100,
    )
    feed_grads = exchanged(feed_kept, 0)
    grad_blocks = ring(grad_branch, HEAD)

    for step in range(1, seq_bits):
        size //= 2
        feed_kept = kernel_call(
            functools.partial(feed_seq_kernel, seq_bits, seq_bits - step), "feed_seq",
            (place, *feed_grads), late(*[low(size, window)] * 4),
            scratch=[pltpu.VMEM((2 * size, window), f32)],
            after=grad_blocks[1:2],
        )
        feed_grads = exchanged(feed_kept, step)
    adj = mixer_adjoint(
        me_array, grad_blocks, w_out, fwd, out, out_gain[None],
        after=[block_given, block_own, feed_kept[1]],
    )
    later = [along(adj["local"], "seq", -s) for s in range(seq_n - 1, 0, -1)]

    own_rows = model // (batch_n * seq_n * head_n)
    seq_rows = own_rows * head_n
    pairs = head_n // 2
    feed_kept = kernel_call(
        functools.partial(feed_head_kernel, pairs), "feed_head", (place, *feed_grads),
        late(*[low(12 * own_rows, window)] * pairs),
        scratch=[pltpu.VMEM((6 * seq_rows, window), f32)],
        after=[adj["local"]],
    )
    normed_parts, wide = mixer_backward(
        place, states[1:], later, fwd, out, adj, taps, rate,
        (w_query, w_key, w_value, w_small, w_outgate), gain, grad_mlp_gain, head_n,
        after=[feed_kept[-1]],
    )
    feed_grads = [feed_kept[0]] + [
        lax.ppermute(
            feed_kept[shift], HEAD, [(i, (i + 2 * shift) % head_n) for i in range(head_n)]
        )
        for shift in range(1, pairs)
    ]
    block_given = crossed(tied(feed_kept[0], block_given)[1], HEAD)
    block_out = (middle + add_up([fed[4], block_own, block_given])).astype(bf16)
    normed_parts = spread(normed_parts, HEAD)

    columns = wide[0].shape[1]
    wide_blocks = kernel_call(
        mixer_blocks_kernel, "mixer_blocks",
        (place, wide[0], crossed(tied(wide[1], block_given, *feed_grads[1:])[0], "batch")),
        late(sds(seq_rows + 8, columns), *[low(seq_rows + 16, columns)] * (seq_n - 1)),
        scratch=[
            pltpu.VMEM((model // 2 + 8, columns), f32), pltpu.VMEM((model // 2 + 16, columns), bf16),
            pltpu.SemaphoreType.DMA((2, seq_n + 1)),
        ],
        hbm=(1, 2),
    )
    wide_parts = spread(wide_blocks, "seq")
    extra, gains = kernel_call(
        functools.partial(extra_rows_kernel, head_n), "extra_rows", normed_parts,
        [low(RIM, model), sds(8, model)],
        after=wide_parts[1:2],
    )
    gains = add_up([gains, crossed(gains, "batch")])
    gain_parts = ring(gains, "seq")
    rim_part = lax.ppermute(
        extra,
        ("seq", *HEAD),
        [(s * head_n + head_last, (s - 1) * head_n + head_last) for s in range(1, seq_n)],
    )
    group_own, group_sent = kernel_call(
        functools.partial(feed_pair_kernel, pairs), "feed_pair", (place, *feed_grads),
        [low(6 * own_rows, window)] * 2,
        scratch=[pltpu.VMEM((12 * own_rows, window), f32)],
        after=[extra],
    )
    group_got = crossed(group_sent, HEAD)
    group = [group_own, crossed(group_own, "batch"), group_got, crossed(group_got, "batch")]
    grad_gate, grad_up, grad_down = kernel_call(
        functools.partial(feed_out_kernel, hidden), "feed_out", (place, *group),
        [sds(own_rows, ways * hidden)] * 3,
    )
    (grad_tokens,) = kernel_call(
        functools.partial(tokens_back_kernel, head_n), "tokens_back",
        (*normed_parts, rim_part, tokens, gain, grad_middle),
        [sds(each, model)],
    )
    *sums, grad_decay, grad_out_gain = kernel_call(
        functools.partial(mixer_sum_kernel, seq_n, nh), "mixer_sum", wide_parts,
        [sds(seq_rows, w) for w in (nq, 2 * nq, 2 * nq)] + [sds(w, seq_rows) for w in (2 * nh, nh)]
        + [sds(seq_rows, nq), sds(nq, seq_rows)]
        + [sds(4, w) for w in (nq, 2 * nq, 2 * nq)] + [sds(1, nh), sds(1, nq)],
    )
    grad_q, grad_k, grad_v, grad_b, grad_d, grad_g, grad_out, *grad_convs = sums
    gains = add_up(gain_parts)
    index = (core * seq_n + seq_place) * head_n + me
    gains = lax.dynamic_slice_in_dim(gains, index * own_rows, own_rows, 1)
    return (
        block_out, grad_tokens, gains[0], grad_q, grad_k, grad_v, grad_b.T, grad_d.T, grad_g,
        *grad_convs, grad_decay[0], grad_out_gain[0], grad_out, gains[1], grad_gate, grad_up,
        grad_down.T,
    )


def solution(mesh):
    batch, seq, head = mesh.devices.shape
    split_mesh = Mesh(mesh.devices.reshape(batch, seq, head // 2, 2), ("batch", "seq", *HEAD))
    return jax.shard_map(
        on_device,
        mesh=split_mesh,
        in_specs=(
            P(("batch", "seq", *HEAD), None),
            P(("batch", "seq")),
            P(),
            P(None, HEAD),
            P(None, HEAD),
            P(None, HEAD),
            P(None, HEAD),
            P(None, HEAD),
            P(None, HEAD),
            P(None, HEAD),
            P(None, HEAD),
            P(None, HEAD),
            P(HEAD),
            P(HEAD),
            P(HEAD, None),
            P(),
            P(),
            P(),
            P(),
            P(("batch", "seq", *HEAD), None),
        ),
        out_specs=(
            P(("batch", "seq", *HEAD), None),
            P(("batch", "seq", *HEAD), None),
            P(("batch", "seq", *HEAD)),
            P(("batch", "seq"), HEAD),
            P(("batch", "seq"), HEAD),
            P(("batch", "seq"), HEAD),
            P(("batch", "seq"), HEAD),
            P(("batch", "seq"), HEAD),
            P(("batch", "seq"), HEAD),
            P(None, HEAD),
            P(None, HEAD),
            P(None, HEAD),
            P(HEAD),
            P(HEAD),
            P(HEAD, ("batch", "seq")),
            P(("batch", "seq", *HEAD)),
            P(("batch", "seq", *HEAD), None),
            P(("batch", "seq", *HEAD), None),
            P(None, ("batch", "seq", *HEAD)),
        ),
        check_vma=False,
    )
```

```python
import functools

import jax
import jax.numpy as jnp
from jax import lax
from jax.experimental import pallas as pl
from jax.experimental.pallas import tpu as pltpu
from jax.sharding import Mesh
from jax.sharding import PartitionSpec as P

bf16, f32, i32 = jnp.bfloat16, jnp.float32, jnp.int32
EPS = 1e-06
CT = 64
RIM = 16
NN = ((1,), (0,))
NT = ((1,), (1,))
MIB = 1 << 20
FORWARD, OUTPUT, ADJOINT, BACKWARD = 4, 4, 4, 4


def mm(a, b, dims=NN):
    return lax.dot_general(a, b, (dims, ((), ())), preferred_element_type=f32)


def split(x):
    high = x.astype(bf16)
    return high, (x - high.astype(f32)).astype(bf16)


def mm3(a, b, dims=NN):
    return mm(a[0], b[0], dims) + (mm(a[0], b[1], dims) + mm(a[1], b[0], dims))


def exact(a, b):
    return lax.dot_general(
        a, b, (NN, ((), ())), precision=lax.Precision.HIGHEST, preferred_element_type=f32
    )


def iota2(shape, dim):
    return lax.broadcasted_iota(i32, shape, dim)


def rows_of(c, size=CT, start=0):
    return pl.ds(pl.multiple_of(c * size + start, 16), size)


def near(c, start):
    return pl.ds(pl.multiple_of(c * CT + start, 8), CT + 8)


def step_order():
    size = 2 * CT
    row, col = iota2((size, size), 0), iota2((size, size), 1)
    row_tok, col_tok = row & (CT - 1), col & (CT - 1)
    later = jnp.where(row_tok > col_tok, row_tok ^ col_tok, 0)
    same_token = (row_tok == col_tok) & (row >= CT) & (col < CT)
    return row, col, later, same_token


def twice(x):
    return jnp.concatenate([x, x], 0)


def head_steps(ref, rows, h):
    return jnp.concatenate(
        [ref[rows, (2 * h + j) * 128 : (2 * h + j + 1) * 128] for j in range(2)], 0
    )


def decays(gam_ref, info, rows, h, nh):
    gcol = gam_ref[rows, 2 * nh + h : 2 * nh + h + 1]
    glast = gcol[CT - 1 : CT, :]
    carried = jnp.exp(gcol) * info[:, 4:5]
    tail = jnp.exp(jnp.minimum(glast - gcol, 0.0)) * info[:, 5:6]
    keep = carried[CT - 1 : CT, :]
    return gcol, carried, tail, keep


def forward_kernel(
    nh, count, me_ref, *refs
):
    tok_refs, refs = refs[:count], refs[count:]
    forward_body(nh, me_ref, tok_refs, *refs)


def forward_body(
    nh, me_ref, tok_refs, rim_ref, ng_ref, wq_ref, wk_ref, wv_ref, wg_ref, ws_ref, tq_ref, tk_ref, tv_ref,
    flags_ref, drow_ref, rate_ref,
    normed_ref, pre_ref, conv_ref, gate_ref, q_ref, k_ref, v_ref, beta_ref, glog_ref, gam_ref, dec_ref,
    t_ref, w_ref, u_ref, reach_ref, score_ref, at_ref, bt_ref, info_ref, low_ref, st_ref,
):
    length = pre_ref.shape[0] - RIM
    nc = length // CT
    gain = ng_ref[...]
    count = len(tok_refs)
    each = tok_refs[0].shape[0]

    def normal(x):
        x = x.astype(f32)
        scale = lax.rsqrt(jnp.mean(x * x, -1, keepdims=True) + EPS)
        return (x * scale * gain).astype(bf16)

    model = ng_ref.shape[1]
    normed_ref[0:RIM, :] = normal(rim_ref[:, :model])
    info_ref[...] = flags_ref[...]
    first = flags_ref[RIM : RIM + 8, :]
    ids = jnp.concatenate([rim_ref[8:, model : model + 8].astype(f32), first[:, 6:7] + jnp.zeros((8, 8), f32)], 0)
    row, col = iota2((8, 8), 0), iota2((8, 8), 1)
    for m in range(1, 4):
        same = (pltpu.roll(ids, m, 0)[8:] == ids[8:]).astype(f32)
        first = jnp.where((col == m) & (row < m), same, first)
    info_ref[RIM : RIM + 8, :] = first

    for shift, tok_ref in enumerate(tok_refs):
        place = lax.rem(me_ref[0] + (count - shift), count) * each

        def norm_rows(c, carry):
            target = pl.ds(pl.multiple_of(place + c * CT + RIM, 16), CT)
            normed_ref[target, :] = normal(tok_ref[rows_of(c), :])
            return carry

        lax.fori_loop(0, each // CT, norm_rows, 0)
    copies.done(normed_ref)
    copies.need(wq_ref, wk_ref, wv_ref, wg_ref, ws_ref)
    nq = nh * 128
    groups = ((wq_ref, 0, nq), (wk_ref, nq, 2 * nq), (wv_ref, 3 * nq, 2 * nq))

    for weight, first, width in groups:
        pre_ref[0:RIM, first : first + width] = (
            mm(normed_ref[0:RIM, :], weight[...]).astype(bf16).astype(f32)
        )

    def project(i, carry):
        rows = rows_of(i, 256, RIM)
        block = normed_ref[rows, :]
        for weight, first, width in groups:
            pre_ref[rows, first : first + width] = mm(block, weight[...]).astype(bf16).astype(f32)
        plain = rows_of(i, 256)
        gate_ref[plain, :] = mm(block, wg_ref[...])
        glog_ref[plain, :] = mm(block, ws_ref[...])
        return carry

    lax.fori_loop(0, length // 256, project, 0)
    copies.done(pre_ref, gate_ref)
    logits = glog_ref[...]
    beta_ref[...] = jax.nn.sigmoid(logits)
    soft = jnp.maximum(logits, 0.0) + jnp.log1p(jnp.exp(-jnp.abs(logits)))
    glog = rate_ref[...] * soft
    glog_ref[...] = glog
    tri = (iota2((CT, CT), 0) >= iota2((CT, CT), 1)).astype(f32)
    for c in range(nc):
        gam_ref[c * CT : (c + 1) * CT, :] = exact(tri, glog[c * CT : (c + 1) * CT, :])

    def conv_rows(c, carry):
        rows = rows_of(c)
        info = info_ref[rows_of(c, CT, RIM), :]
        mask = [info[:, m : m + 1] for m in range(4)]
        for tap_ref, first, count, kind in (
            (tq_ref, 0, nh, "q"), (tk_ref, nq, 2 * nh, "k"), (tv_ref, 3 * nq, 2 * nh, "v")
        ):
            for j in range(count):
                cols = slice(first + j * 128, first + (j + 1) * 128)
                mine = slice(j * 128, (j + 1) * 128)
                taps = tap_ref[:, mine].astype(f32)
                block = pre_ref[near(c, RIM - 8), cols]
                total = block[8:] * taps[0:1]
                for m in range(1, 4):
                    total = total + pltpu.roll(block, m, 0)[8:] * mask[m] * taps[m : m + 1]
                conv_ref[rows, cols] = total
                out = total * jax.nn.sigmoid(total)
                if kind == "k":
                    out = out * lax.rsqrt(jnp.sum(out * out, -1, keepdims=True) + EPS)
                {"q": q_ref, "k": k_ref, "v": v_ref}[kind][rows, mine] = out
        return carry

    lax.fori_loop(0, nc, conv_rows, 0)
    copies.done(conv_ref, q_ref, k_ref, v_ref, beta_ref, glog_ref, gam_ref)

    row, col, later, same_token = step_order()
    eye = (row == col).astype(f32)
    small_row, small_col = iota2((CT, CT), 0), iota2((CT, CT), 1)

    def prepare(group, carry):
        items = [(group * FORWARD + i, h) for i in range(FORWARD) for h in range(nh)]
        systems, rhs, tails, keeps = [], [], [], []
        for c, h in items:
            rows = rows_of(c)
            info = info_ref[rows_of(c, CT, RIM), :]
            same = (info[:, 6:7] == drow_ref[c]) & (small_row >= small_col)
            gcol, carried, tail, keep = decays(gam_ref, info, rows, h, nh)
            grow = jnp.sum(jnp.where(small_row == small_col, gcol, 0.0), 0, keepdims=True)
            decay = jnp.where(same, jnp.exp(jnp.minimum(gcol - grow, 0.0)), 0.0)
            wide = jnp.concatenate([decay, decay], 1)
            dec_ref[c, h] = wide
            key = head_steps(k_ref, rows, h)
            value = head_steps(v_ref, rows, h)
            beta = jnp.concatenate(
                [beta_ref[rows, 2 * h + j : 2 * h + j + 1] for j in range(2)], 0
            )
            key2 = split(key)
            query = q_ref[rows, h * 128 : (h + 1) * 128]
            query2 = split(query)
            pairs = mm3([jnp.concatenate(x, 0) for x in zip(key2, query2)], key2, NT)
            score_ref[c, h] = pairs[2 * CT :] * wide
            reach_ref[c, h] = query * carried
            systems.append(
                jnp.where((later > 0) | same_token, beta * pairs[: 2 * CT] * twice(wide), 0.0)
            )
            rhs.append(jnp.concatenate([beta * twice(carried) * key, beta * value], 1))
            tails.append(key * twice(tail))
            keeps.append(keep)
        inverse = [eye - jnp.where(same_token, n, 0.0) for n in systems]
        for level in range(6):
            part = (later >> level) == 1
            blocks = [split(jnp.where(part, n, 0.0)) for n in systems]
            inverse2 = [split(x) for x in inverse]
            first = [split(mm3(b, x)) for b, x in zip(blocks, inverse2)]
            inverse = [x - mm3(x2, y) for x, x2, y in zip(inverse, inverse2, first)]
        mixed = [mm3(split(x), split(r)) for x, r in zip(inverse, rhs)]
        products = [mm3(split(jnp.transpose(m)), split(t)) for m, t in zip(mixed, tails)]
        for n, (c, h) in enumerate(items):
            t_ref[c, h] = inverse[n]
            w_ref[c, h] = mixed[n][:, :128]
            u_ref[c, h] = mixed[n][:, 128:]
            at_ref[c, h] = keeps[n] * eye - products[n][:128]
            bt_ref[c, h] = products[n][128:]
        part = pl.ds(group * FORWARD, FORWARD)
        copies.done(dec_ref, score_ref, reach_ref, t_ref, w_ref, u_ref, at_ref, bt_ref, at=part)
        return carry

    lax.fori_loop(0, nc // FORWARD, prepare, 0)

    for h in range(nh):
        st_ref[h, :128] = at_ref[0, h]
        st_ref[h, 128:] = bt_ref[0, h]

    def chain(c, carry):
        for h in range(nh):
            after = mm3(split(st_ref[h]), split(at_ref[c, h]))
            st_ref[h, :128] = after[:128]
            st_ref[h, 128:] = after[128:] + bt_ref[c, h]
        return carry

    lax.fori_loop(1, nc, chain, 0)
    low_ref[...] = st_ref[...].astype(bf16)


def output_kernel(nh, count, blocks, me_ref, *refs):
    output_body(nh, me_ref, refs[:count], *refs[count : -blocks - 1], refs[-blocks - 1 : -1], refs[-1])


def output_body(
    nh, me_ref, map_refs, at_ref, bt_ref, w_ref, reach_ref, u_ref, score_ref, gate_ref, gain_ref, wout_ref,
    sin_ref, fresh_ref, core_ref, gated_ref, branch_refs, all_ref,
):
    nc = w_ref.shape[0]
    states = []
    for h in range(nh):
        state = jnp.zeros((128, 128), f32)
        for distance in range(len(map_refs), 0, -1):
            map_ref = map_refs[distance - 1]
            passed = split(map_ref[h, :128].astype(f32))
            state = mm3(split(state), passed) + map_ref[h, 128:].astype(f32)
            state = jnp.where(me_ref[2] >= distance, state, 0.0)
        states.append(state)

    def chain(c, states):
        out = []
        for h in range(nh):
            sin_ref[c, h] = states[h]
            out.append(mm3(split(states[h]), split(at_ref[c, h])) + bt_ref[c, h])
        return tuple(out)

    copies.need(at_ref, bt_ref)
    states = lax.fori_loop(0, nc, chain, tuple(states))
    for h in range(nh):
        sin_ref[nc, h] = states[h]
    copies.done(sin_ref)
    copies.need(w_ref, reach_ref, u_ref, score_ref, gate_ref)

    def outputs(group, carry):
        for c, h in [(group * OUTPUT + i, h) for i in range(OUTPUT) for h in range(nh)]:
            rows = rows_of(c)
            cols = slice(h * 128, (h + 1) * 128)
            state2 = split(sin_ref[c, h])
            probe = jnp.concatenate([w_ref[c, h], reach_ref[c, h]], 0)
            seen = mm3(split(probe), state2, NT)
            fresh = u_ref[c, h] - seen[: 2 * CT]
            fresh_ref[c, h] = fresh
            core = seen[2 * CT :] + mm3(split(score_ref[c, h]), split(fresh))
            core_ref[rows, cols] = core
            unit = core * lax.rsqrt(jnp.mean(core * core, -1, keepdims=True) + EPS)
            gate = gate_ref[rows, cols]
            gated_ref[rows, cols] = (
                unit * gain_ref[:, cols] * (gate * jax.nn.sigmoid(gate))
            ).astype(bf16)
        copies.done(fresh_ref, at=pl.ds(group * OUTPUT, OUTPUT))
        copies.done(core_ref, gated_ref, at=rows_of(group, OUTPUT * CT))
        return carry

    lax.fori_loop(0, nc // OUTPUT, outputs, 0)
    copies.need(wout_ref)
    all_ref[...] = mm(gated_ref[...], wout_ref[...]).astype(bf16)
    count = len(branch_refs)
    each = branch_refs[0].shape[0]
    for shift, branch_ref in enumerate(branch_refs):
        place = lax.rem(me_ref[0] + shift, count) * each
        branch_ref[...] = all_ref[pl.ds(pl.multiple_of(place, 16), each), :]
        copies.done(branch_ref)


def adjoint_kernel(nh, count, me_ref, *refs):
    adjoint_body(nh, me_ref, refs[:count], *refs[count:])


def adjoint_body(
    nh, me_ref, g_refs, wout_ref, core_ref, gate_ref, gain_ref, score_ref, reach_ref, w_ref, at_ref,
    dcore_ref, dt_ref, dgate_ref, dgain_ref, local_ref, dgated_ref, all_ref,
):
    nc = w_ref.shape[0]
    count = len(g_refs)
    each = g_refs[0].shape[0]
    for shift, g_ref in enumerate(g_refs):
        place = lax.rem(me_ref[0] + (count - shift), count) * each
        all_ref[pl.ds(pl.multiple_of(place, 16), each), :] = g_ref[...]
    copies.need(wout_ref)
    dgated_ref[...] = mm(all_ref[...], wout_ref[...], NT)
    copies.need(core_ref, gate_ref, score_ref, reach_ref, w_ref)

    def chunks(group, dgain):
        for i in range(ADJOINT):
            dgain = dgain + chunk(group * ADJOINT + i)
        copies.done(dt_ref, at=pl.ds(group * ADJOINT, ADJOINT))
        copies.done(dcore_ref, dgate_ref, at=rows_of(group, ADJOINT * CT))
        return dgain

    def chunk(c):
        rows = rows_of(c)
        sums = []
        for h in range(nh):
            cols = slice(h * 128, (h + 1) * 128)
            core = core_ref[rows, cols]
            scale = lax.rsqrt(jnp.mean(core * core, -1, keepdims=True) + EPS)
            unit = core * scale
            gate = gate_ref[rows, cols]
            sig = jax.nn.sigmoid(gate)
            silu = gate * sig
            gain = gain_ref[:, cols]
            grad = dgated_ref[rows, cols]
            sums.append(jnp.sum(grad * unit * silu, 0, keepdims=True))
            dgate_ref[rows, cols] = (
                grad * unit * gain * (sig * (1.0 + gate * (1.0 - sig)))
            ).astype(bf16)
            dunit = grad * gain * silu
            dcore = scale * (dunit - unit * jnp.mean(dunit * unit, -1, keepdims=True))
            dcore_ref[rows, cols] = dcore
            across = jnp.transpose(dcore)
            dft = mm3(split(across), split(score_ref[c, h]))
            left = jnp.concatenate([-dft, across], 1)
            right = jnp.concatenate([w_ref[c, h], reach_ref[c, h]], 0)
            dt_ref[c, h] = mm3(split(left), split(right))
        return jnp.concatenate(sums, 1)

    dgain_ref[...] = lax.fori_loop(0, nc // ADJOINT, chunks, jnp.zeros(dgain_ref.shape, f32))

    copies.need(at_ref)

    def chain(i, carry):
        c = nc - 1 - i
        return tuple(
            mm3(split(carry[h]), split(at_ref[c, h]), NT) + dt_ref[c, h] for h in range(nh)
        )

    start = tuple(dt_ref[nc - 1, h] for h in range(nh))
    total = lax.fori_loop(1, nc, chain, start)
    for h in range(nh):
        local_ref[h] = total[h].astype(bf16)


def normed_back(count, place_ref, gp_ref, weights, normed_ref, gain_ref, mlp_ref, out_refs, all_ref):
    each = out_refs[0].shape[0] - RIM
    length = all_ref.shape[0] - RIM
    total = jnp.zeros(gain_ref.shape, f32)
    for start in range(0, length, 256):
        rows = slice(start + (RIM if start else 0), start + 256 + RIM)
        first = 0
        grad = None
        for weight in weights:
            width = weight.shape[1]
            term = mm(gp_ref[rows, first : first + width], weight[...], NT)
            grad = term if grad is None else grad + term
            first += width
        all_ref[rows, :] = grad.astype(bf16)
        total = total + jnp.sum(grad * normed_ref[rows, :].astype(f32), 0, keepdims=True)
    rim = all_ref[0:RIM, :].astype(f32)
    row = iota2((RIM, 1), 0)
    gains = [*split(total / gain_ref[...]), *split(mlp_ref[...])]
    for n, gain in enumerate(gains):
        rim = jnp.where(row == n, gain.astype(f32), rim)
    rim = rim.astype(bf16)
    for shift, out_ref in enumerate(out_refs):
        place = lax.rem(place_ref[0] + shift, count) * each + RIM
        out_ref[0:each, :] = all_ref[pl.ds(pl.multiple_of(place, 16), each), :]
        out_ref[each:, :] = rim
        copies.done(out_ref)


def turn(left_ref, turned_ref):
    tokens, width = left_ref.shape
    for n in range(width // 128):
        turned_ref[n * 128 : (n + 1) * 128, :tokens] = jnp.transpose(
            left_ref[:, n * 128 : (n + 1) * 128]
        )


def two_halves(place_ref, turned, right, own_ref, given_ref, cols):
    half = turned.shape[0] // 2
    for core, out_ref in ((place_ref[1], own_ref), (1 - place_ref[1], given_ref)):
        rows = pl.ds(pl.multiple_of(core * half, 16), half)
        out_ref[0:half, cols] = mm(turned[rows, : right.shape[0]], right[...]).astype(out_ref.dtype)


def two_parts(value):
    high, low = split(value)
    return jnp.concatenate([high, low], 0)


def backward_kernel(nh, count, blocks, *refs):
    at = 2 * count + 1
    maps, local_sums, place, refs = refs[:count], refs[count : at - 1], refs[at - 1], refs[at:]
    inputs, refs = refs[:21], refs[21:]
    dgate, weights, (normed, gain, mlp, dgain), refs = refs[0], refs[1:6], refs[6:10], refs[10:]
    gated, grads, refs = refs[0], refs[1 : blocks + 1], refs[blocks + 1 :]
    out_refs, (own, given), refs = refs[:blocks], refs[blocks : blocks + 2], refs[blocks + 2 :]
    gp, taps, dlog, dconv, small, ends, everything, turned, turned_grad, sums = refs
    half, width = own.shape[0] - 16, gp.shape[1]
    wide, nq = own.shape[1], gated.shape[1]
    gp[0:RIM, width - nq :] = jnp.zeros((RIM, nq), bf16)
    backward_body(nh, maps, local_sums, *inputs, gp, taps, dlog, dconv, small, ends)
    copies.need(dgate, normed, gated, *grads)
    gp[RIM:, width - nq :] = dgate[...]
    turn(normed, turned)
    two_halves(place, turned, gp, own, given, slice(0, width))
    each = grads[0].shape[0]
    for shift, grad in enumerate(grads):
        at = pl.multiple_of(lax.rem(place[0] + (blocks - shift), blocks) * each, 128)
        for n in range(grad.shape[1] // 128):
            turned_grad[n * 128 : (n + 1) * 128, pl.ds(at, each)] = jnp.transpose(
                grad[:, n * 128 : (n + 1) * 128]
            )
    two_halves(place, turned_grad, gated, own, given, slice(width, wide))
    sums[...] = jnp.zeros(sums.shape, f32)
    sums[0:4, : taps.shape[1]] = taps[...]
    sums[4:5, :128] = dlog[...]
    sums[4:5, 128 : 128 + dgain.shape[1]] = dgain[...]
    own[half:, :] = two_parts(sums[...])
    given[half:, :] = own[half:, :]
    copies.done(given, own)
    copies.need(*weights)
    normed_back(blocks, place, gp, weights, normed, gain, mlp, out_refs, everything)


def backward_body(
    nh, map_refs, local_refs, at_ref, dt_ref, score_ref, dcore_ref, t_ref, fresh_ref, sin_ref,
    q_ref, k_ref, v_ref, beta_ref, gam_ref, dec_ref, conv_ref, pre_ref, info_ref, tq_ref, tk_ref, tv_ref,
    rate_ref, glog_ref,
    gp_ref, taps_ref, dlog_ref,
    dconv_ref, small_ref, ends_ref,
):
    length = q_ref.shape[0]
    nc = length // CT
    nq = nh * 128
    width = 5 * nq
    ends = []
    for h in range(nh):
        end = local_refs[0][h].astype(f32)
        for map_ref, local_ref in zip(map_refs[1:], local_refs[1:]):
            passed = split(map_ref[h, :128].astype(f32))
            end = mm3(split(end), passed, NT) + local_ref[h].astype(f32)
        ends.append(end)
    row, col, later, same_token = step_order()
    before = (later > 0) | same_token
    last_row = (iota2((CT, 1), 0) == CT - 1).astype(f32)
    dconv_ref[0:RIM, :] = jnp.zeros((RIM, width), f32)
    dconv_ref[RIM + length :, :] = jnp.zeros((RIM, width), f32)
    lane = iota2((CT, 128), 1)
    upper = (iota2((CT, CT), 0) <= iota2((CT, CT), 1)).astype(f32)

    def chain(i, ends):
        c = nc - 1 - i
        out = []
        for h in range(nh):
            ends_ref[c, h] = ends[h]
            out.append(mm3(split(ends[h]), split(at_ref[c, h]), NT) + dt_ref[c, h])
        return tuple(out)

    copies.need(at_ref, dt_ref)
    lax.fori_loop(0, nc, chain, tuple(ends))
    copies.need(score_ref, dcore_ref, t_ref, fresh_ref, sin_ref, q_ref, k_ref, v_ref, dec_ref, conv_ref)

    def chunks(group, carry):
        for i in range(BACKWARD):
            chunk(group * BACKWARD + i)
        return carry

    def chunk(c):
        rows = rows_of(c)
        store = rows_of(c, CT, RIM)
        info = info_ref[store, :]
        small = jnp.zeros((CT, 128), f32)
        dgam = jnp.zeros((CT, 128), f32)
        for h in range(nh):
            cols = slice(h * 128, (h + 1) * 128)
            end = ends_ref[c, h]
            end2 = split(end)
            _, carried, tail, _ = decays(gam_ref, info, rows, h, nh)
            carried2, tail2 = twice(carried), twice(tail)
            key = head_steps(k_ref, rows, h)
            value = head_steps(v_ref, rows, h)
            query = q_ref[rows, cols]
            beta = jnp.concatenate(
                [beta_ref[rows, 2 * h + j : 2 * h + j + 1] for j in range(2)], 0
            )
            wide = dec_ref[c, h]
            full = jnp.where(before, twice(wide), 0.0)
            state = sin_ref[c, h]
            fresh = fresh_ref[c, h]
            fresh2 = split(fresh)
            dcore = dcore_ref[rows, cols]
            dft = mm3(split(jnp.transpose(dcore)), split(score_ref[c, h])) + mm3(
                end2, split(key * tail2), NT
            )
            solved = jnp.transpose(mm3(split(dft), split(t_ref[c, h])))
            both = split(jnp.concatenate([solved, dcore], 0))
            through = mm3(both, split(state))
            pairs = mm3(both, fresh2, NT)
            dtail = mm3(fresh2, end2)
            em = -pairs[: 2 * CT] * full
            ps = pairs[2 * CT :] * wide
            mixed = mm3(split(jnp.concatenate([em, ps], 0)), split(key))
            turned = jnp.transpose(jnp.concatenate([beta * em, ps], 0))
            dkb = mm3(split(turned), split(jnp.concatenate([key, query], 0))) + tail2 * dtail
            x1 = mixed[: 2 * CT] - carried2 * through[: 2 * CT]
            dka = beta * x1
            dkey = dka + dkb
            dbeta = jnp.sum(key * x1 + solved * value, -1, keepdims=True)
            dvalue = beta * solved
            dquery = mixed[2 * CT :] + carried * through[2 * CT :]
            turn = jnp.sum(key * (dka - dkb), -1, keepdims=True)
            closing = jnp.sum(
                jnp.sum(end * sin_ref[c + 1, h], -1, keepdims=True), 0, keepdims=True
            )
            dg = (
                jnp.sum(query * dquery, -1, keepdims=True)
                + turn[:CT]
                + turn[CT:]
                + last_row * closing
            )
            dgam = jnp.where(lane == 2 * nh + h, dg, dgam)
            for j in range(2):
                small = jnp.where(lane == 2 * h + j, dbeta[j * CT : (j + 1) * CT], small)
            pre = conv_ref[rows, cols]
            sig = jax.nn.sigmoid(pre)
            dconv_ref[store, cols] = dquery * (sig * (1.0 + pre * (1.0 - sig)))
            for j in range(2):
                kcols = slice(nq + (2 * h + j) * 128, nq + (2 * h + j + 1) * 128)
                pre = conv_ref[rows, kcols]
                sig = jax.nn.sigmoid(pre)
                act = pre * sig
                scale = lax.rsqrt(jnp.sum(act * act, -1, keepdims=True) + EPS)
                unit = key[j * CT : (j + 1) * CT]
                grad = dkey[j * CT : (j + 1) * CT]
                grad = scale * (grad - unit * jnp.sum(unit * grad, -1, keepdims=True))
                dconv_ref[store, kcols] = grad * (sig * (1.0 + pre * (1.0 - sig)))
                vcols = slice(3 * nq + (2 * h + j) * 128, 3 * nq + (2 * h + j + 1) * 128)
                pre = conv_ref[rows, vcols]
                sig = jax.nn.sigmoid(pre)
                dconv_ref[store, vcols] = dvalue[j * CT : (j + 1) * CT] * (
                    sig * (1.0 + pre * (1.0 - sig))
                )
        dglog = exact(upper, dgam)
        small_ref[rows, :] = jnp.where(lane < 2 * nh, small, dglog)

    lax.fori_loop(0, nc // BACKWARD, chunks, 0)

    copies.need(pre_ref, glog_ref)
    beta = beta_ref[...]
    small = small_ref[...]
    lanes = iota2(beta.shape, 1)
    grads = small * beta * jnp.where(lanes < 2 * nh, 1.0 - beta, rate_ref[...])
    dlog_ref[...] = jnp.sum(small * glog_ref[...], 0, keepdims=True)
    gp_ref[0:RIM, 0 : width + 128] = jnp.zeros((RIM, width + 128), bf16)
    gp_ref[RIM:, width : width + 128] = grads.astype(bf16)
    groups = ((tq_ref, 0, nh), (tk_ref, nq, 2 * nh), (tv_ref, 3 * nq, 2 * nh))

    def turned_back(grad, masks, taps, count):
        total = grad[:count] * taps[0:1]
        size = grad.shape[0]
        for m in range(1, 4):
            moved = pltpu.roll(grad * masks[:, m : m + 1], size - m, 0)
            total = total + moved[:count] * taps[m : m + 1]
        return total

    def conv_back(c, sums):
        info = info_ref[near(c, RIM), :]
        new = []
        for tap_ref, first, count in groups:
            for j in range(count):
                cols = slice(first + j * 128, first + (j + 1) * 128)
                taps = tap_ref[:, j * 128 : (j + 1) * 128].astype(f32)
                grad = dconv_ref[near(c, RIM), cols]
                gp_ref[rows_of(c, CT, RIM), cols] = turned_back(grad, info, taps, CT).astype(bf16)
                block = pre_ref[near(c, RIM - 8), cols]
                parts = [jnp.sum(grad[:CT] * block[8:], 0, keepdims=True)]
                for m in range(1, 4):
                    moved = pltpu.roll(block, m, 0)[8:]
                    parts.append(
                        jnp.sum(grad[:CT] * info[:CT, m : m + 1] * moved, 0, keepdims=True)
                    )
                new.append(jnp.concatenate(parts, 0))
        return sums + jnp.concatenate(new, 1)

    taps_ref[...] = lax.fori_loop(0, nc, conv_back, jnp.zeros((4, width), f32))
    for tap_ref, first, count in groups:
        cols = slice(first, first + count * 128)
        taps = tap_ref[...].astype(f32)
        early = slice(8, 24)
        rim = turned_back(dconv_ref[early, cols], info_ref[early, :], taps, 8)
        gp_ref[0:RIM, cols] = jnp.concatenate([jnp.zeros_like(rim), rim], 0).astype(bf16)


VMEM = pl.BlockSpec(memory_space=pltpu.VMEM)
SMEM = pl.BlockSpec(memory_space=pltpu.SMEM)
ANY = pl.BlockSpec(memory_space=pl.ANY)


class Late:
    def __init__(self, value):
        self.value = value


def late(*values):
    return [Late(value) for value in values]


class Copies:
    def __init__(self):
        self.coming, self.going = {}, {}

    def need(self, *refs):
        for ref in refs:
            copy = self.coming.pop(id(ref), None)
            if copy is not None:
                copy.wait()

    def done(self, *refs, at=None):
        for ref in refs:
            entry = self.going.get(id(ref))
            if entry is None:
                continue
            target, sem, _ = entry
            source = ref
            if at is not None:
                source, target = ref.at[at], target.at[at]
            pltpu.make_async_copy(source, target, sem).start()
            self.going[id(ref)] = (entry[0], sem, True)

    def finish(self, refs):
        for copy in self.coming.values():
            copy.wait()
        self.coming = {}
        for ref in refs:
            if id(ref) in self.going and not self.going[id(ref)][2]:
                self.done(ref)
        for ref in refs:
            if id(ref) in self.going:
                target, sem, _ = self.going.pop(id(ref))
                pltpu.make_async_copy(ref, target, sem).wait()


copies = Copies()


def kernel_call(body, name, args, outs, scratch=(), after=(), hbm=(), mib=24, cost=2):
    late_in = [n for n, a in enumerate(args) if isinstance(a, Late)]
    late_out = [n for n, s in enumerate(outs) if isinstance(s, Late)]
    args = [a.value if isinstance(a, Late) else a for a in args]
    outs = [s.value if isinstance(s, Late) else s for s in outs]
    extra, n_in, n_out, n_scratch = len(after), len(args), len(outs), len(scratch)
    buffers = [pltpu.VMEM(args[n].shape, args[n].dtype) for n in late_in]
    buffers += [pltpu.VMEM(outs[n].shape, outs[n].dtype) for n in late_out]
    sems = [pltpu.SemaphoreType.DMA((len(late_in) + len(late_out),))] if buffers else []

    def run(*refs):
        in_refs, refs = list(refs[:n_in]), refs[n_in + extra :]
        out_refs, refs = list(refs[:n_out]), refs[n_out:]
        own_scratch, refs = refs[:n_scratch], refs[n_scratch:]
        held = []
        for k, n in enumerate(late_in):
            copy = pltpu.make_async_copy(in_refs[n], refs[k], refs[-1].at[k])
            copy.start()
            copies.coming[id(refs[k])] = copy
            in_refs[n] = refs[k]
        for k, n in enumerate(late_out, len(late_in)):
            copies.going[id(refs[k])] = (out_refs[n], refs[-1].at[k], False)
            out_refs[n] = refs[k]
            held.append(refs[k])
        body(*in_refs, *out_refs, *own_scratch)
        copies.finish(held)

    in_specs = [SMEM if a.dtype == i32 else VMEM for a in args]
    out_specs = [VMEM] * n_out
    for n in (*late_in, *hbm):
        in_specs[n] = ANY
    for n in late_out:
        out_specs[n] = ANY
    return pl.pallas_call(
        run,
        name=name,
        in_specs=in_specs + [ANY] * extra,
        out_specs=out_specs,
        out_shape=outs,
        scratch_shapes=[*scratch, *buffers, *sems],
        compiler_params=pltpu.CompilerParams(vmem_limit_bytes=mib * MIB),
        cost_estimate=pl.CostEstimate(flops=cost * 10**9, bytes_accessed=0, transcendentals=0),
    )(*args, *after)


def sds(*shape, dtype=f32):
    return jax.ShapeDtypeStruct(shape, dtype)


def mixer_forward(me, tokens, rim, norm_gain, weights, taps, info, doc_rows, rate):
    length, width = tokens[0].shape
    length *= len(tokens)
    w_query, w_key, w_value, w_outgate, w_small = weights
    nh = w_query.shape[1] // 128
    nc, nq = length // CT, nh * 128
    per = (nc, nh)
    outs = dict(
        normed=sds(RIM + length, width, dtype=bf16),
        pre=sds(RIM + length, 5 * nq),
        conv=sds(length, 5 * nq),
        gate=sds(length, nq),
        q=sds(length, nq),
        k=sds(length, 2 * nq),
        v=sds(length, 2 * nq),
        beta=sds(length, 128),
        glog=sds(length, 128),
        gam=sds(length, 128),
        dec=sds(*per, CT, 128),
        t=sds(*per, 128, 128),
        w=sds(*per, 128, 128),
        u=sds(*per, 128, 128),
        reach=sds(*per, CT, 128),
        score=sds(*per, CT, 128),
        at=sds(*per, 128, 128),
        bt=sds(*per, 128, 128),
        info=sds(length + 2 * RIM, 8),
        low=sds(nh, 256, 128, dtype=bf16),
    )
    args = (
        me, *tokens, rim, norm_gain, *late(w_query, w_key, w_value, w_outgate, w_small), *taps, info, doc_rows,
        rate,
    )
    res = kernel_call(
        functools.partial(forward_kernel, nh, len(tokens)), "mixer_forward", args,
        [s if n in ("info", "low") else Late(s) for n, s in outs.items()],
        cost=25, mib=60,
        scratch=[pltpu.VMEM((nh, 256, 128), f32)],
    )
    return dict(zip(outs, res))


def mixer_output(me, maps, fwd, out_gain, w_out, blocks, after=()):
    nc, nh = fwd["w"].shape[:2]
    length = nc * CT
    outs = dict(
        sin=sds(nc + 1, nh, 128, 128),
        fresh=sds(nc, nh, 128, 128),
        core=sds(length, nh * 128),
        gated=sds(length, nh * 128, dtype=bf16),
    )
    parts = [sds(length // blocks, w_out.shape[1], dtype=bf16)] * blocks
    names = ("at", "bt", "w", "reach", "u", "score", "gate")
    args = (me, *maps, *late(*(fwd[n] for n in names)), out_gain, *late(w_out))
    res = kernel_call(
        functools.partial(output_kernel, nh, len(maps), blocks), "mixer_output", args,
        late(*outs.values(), *parts), cost=10, mib=60,
        scratch=[pltpu.VMEM((length, w_out.shape[1]), bf16)],
        after=after,
    )
    return dict(zip(outs, res), branch=res[len(outs) :])


def mixer_adjoint(me, grad, w_out, fwd, out, out_gain, after=()):
    nc, nh = fwd["w"].shape[:2]
    length = nc * CT
    outs = dict(
        dcore=sds(length, nh * 128),
        dt=sds(nc, nh, 128, 128),
        dgate=sds(length, nh * 128, dtype=bf16),
        dgain=sds(1, nh * 128),
        local=sds(nh, 128, 128, dtype=bf16),
    )
    args = (
        me, *grad, w_out, out["core"], fwd["gate"], out_gain,
        *(fwd[n] for n in ("score", "reach", "w", "at")),
    )
    res = kernel_call(
        functools.partial(adjoint_kernel, nh, len(grad)), "mixer_adjoint", args,
        [s if n in ("dgain", "local") else Late(s) for n, s in outs.items()],
        cost=10, mib=24,
        scratch=[pltpu.VMEM((length, nh * 128), f32), pltpu.VMEM((length, w_out.shape[1]), bf16)],
        after=after,
    )
    return dict(zip(outs, res))


def mixer_backward(
    place, maps, local_sums, fwd, out, adj, taps, rate, weights, gain, mlp, grad, after=()
):
    nc, nh = fwd["w"].shape[:2]
    length, nq = nc * CT, nh * 128
    width = 5 * nq
    model = gain.shape[1]
    blocks = len(grad)
    parts = [sds(RIM + length // blocks, model, dtype=bf16)] * blocks
    columns = width + 128 + 2 * nq
    halves = [sds(model // 2 + 16, columns, dtype=bf16)] * 2
    args = (
        *maps, *local_sums, place,
        *late(
            fwd["at"], adj["dt"], fwd["score"], adj["dcore"], fwd["t"], out["fresh"], out["sin"],
            *(fwd[n] for n in ("q", "k", "v")),
        ),
        fwd["beta"], fwd["gam"], *late(fwd["dec"], fwd["conv"], fwd["pre"]), fwd["info"], *taps, rate,
        *late(fwd["glog"], adj["dgate"], *weights, fwd["normed"]), gain, mlp, adj["dgain"],
        *late(out["gated"], *grad),
    )
    *res, own, given = kernel_call(
        functools.partial(backward_kernel, nh, len(maps), blocks), "mixer_backward", args,
        late(*parts, *halves), cost=300, mib=60,
        scratch=[
            pltpu.VMEM((RIM + length, width + 128 + nq), bf16), pltpu.VMEM((4, width), f32),
            pltpu.VMEM((1, 128), f32),
            pltpu.VMEM((length + 2 * RIM, width), f32), pltpu.VMEM((length, 128), f32),
            pltpu.VMEM((nc, nh, 128, 128), f32), pltpu.VMEM((RIM + length, model), bf16),
            pltpu.VMEM((model, RIM + length), bf16), pltpu.VMEM((model, length), bf16),
            pltpu.VMEM((8, columns), f32),
        ],
        after=after,
    )
    return res, (own, given)


def token_info(doc_ids):
    ids = doc_ids.astype(f32)
    length = ids.shape[0]
    extended = jnp.concatenate([ids[:3], ids])
    masks = [(extended[3 - m : 3 - m + length] == ids).astype(f32) for m in range(4)]
    blocks = ids.reshape(-1, CT)
    last = blocks[:, -1:]
    previous = jnp.concatenate([blocks[:1, :1], last[:-1]], 0)
    columns = masks + [
        (blocks == previous).astype(f32).reshape(-1),
        (blocks == last).astype(f32).reshape(-1),
        ids,
        jnp.zeros_like(ids),
    ]
    info = jnp.pad(jnp.stack(columns, 1), ((RIM, RIM), (0, 0)))
    return info, blocks[:, None, :]


def middle_kernel(count, tok_ref, *refs):
    parts, (gain_ref, middle_ref, normed_ref) = refs[:count], refs[count:]
    middle = tok_ref[...].astype(f32)
    total = parts[0][...].astype(f32)
    for part in parts[1:]:
        total = total + part[...].astype(f32)
    middle = middle + total
    middle_ref[...] = middle
    scale = lax.rsqrt(jnp.mean(middle * middle, -1, keepdims=True) + EPS)
    normed_ref[...] = (middle * scale * gain_ref[...]).astype(bf16)


def feed_kernel(hidden, place_ref, *refs):
    x_refs, cot_refs, weights, refs = refs[:4], refs[4:8], refs[8:11], refs[11:]
    norm_refs, block_refs, cols_ref, refs = refs[:4], refs[4:8], refs[8], refs[9:]
    gate_w, up_w, down_w, sems = refs
    width = gate_w.shape[1]
    each = x_refs[0].shape[0]
    start = pl.multiple_of(place_ref[3], 128)
    window = pl.ds(start, width)
    copies = [
        pltpu.make_async_copy(weights[0].at[:, window], gate_w, sems.at[0]),
        pltpu.make_async_copy(weights[1].at[:, window], up_w, sems.at[1]),
        pltpu.make_async_copy(weights[2].at[window, :], down_w, sems.at[2]),
    ]
    for copy in copies:
        copy.start()
    lane = iota2((1, width), 1) - place_ref[4]
    mask = ((lane >= 0) & (lane < hidden)).astype(f32)
    for n, pair in enumerate(((1, 3), (0, 2))):
        x = jnp.concatenate([x_refs[p][...] for p in pair], 0)
        cot = jnp.concatenate([cot_refs[p][...] for p in pair], 0)
        if n == 0:
            copies[0].wait()
        gate = mm(x, gate_w[...])
        if n == 0:
            copies[1].wait()
        up = mm(x, up_w[...]) * mask
        sig = jax.nn.sigmoid(gate)
        silu = gate * sig * mask
        act = (silu * up).astype(bf16)
        if n == 0:
            copies[2].wait()
        grad = mm(cot, down_w[...], NT)
        ggate = (grad * up * sig * (1.0 + gate * (1.0 - sig))).astype(bf16)
        gup = (grad * silu).astype(bf16)
        gnorm = (mm(ggate, gate_w[...], NT) + mm(gup, up_w[...], NT)).astype(bf16)
        block = mm(act, down_w[...]).astype(bf16)
        for n, p in enumerate(pair):
            half, at = slice(n * each, (n + 1) * each), slice(p * each, (p + 1) * each)
            norm_refs[p][...] = gnorm[half]
            block_refs[p][...] = block[half]
            for k, value in enumerate((ggate, gup, act)):
                cols_ref[k, at, :] = value[half]


def with_bit(index, position, bit):
    low = index & ((1 << position) - 1)
    return ((index >> position) << (position + 1)) + bit * (1 << position) + low


def seq_bit(place_ref, bit):
    return lax.rem(lax.div(place_ref[2], 1 << bit), 2)


def feed_grads_kernel(bits, place_ref, *refs):
    x_refs, cot_refs, cols_ref, refs = refs[:4], refs[4:8], refs[8], refs[9:]
    out_refs, (turned_ref, full_ref) = refs[:-2], refs[-2:]
    each = x_refs[0].shape[0]
    half = full_ref.shape[0]
    rows = half >> bits
    for n, blocks in enumerate((x_refs, cot_refs)):
        for p, ref in enumerate(blocks):
            turned_ref[n, :, p * each : (p + 1) * each] = jnp.transpose(ref[...])
    for k in range(3):
        for b in range(2):
            left = turned_ref[k // 2, b * half : (b + 1) * half, :]
            copies.need(cols_ref)
            full_ref[...] = mm(left, cols_ref[k]).astype(bf16)
            position = (bits - 1) * b
            mine = seq_bit(place_ref, position)
            for n, bit in enumerate((mine, 1 - mine)):
                out_ref = out_refs[2 * b + n]
                for i in range(1 << (bits - 1)):
                    at = with_bit(i, position, bit) * rows
                    first = (k * (1 << (bits - 1)) + i) * rows
                    out_ref[first : first + rows, :] = full_ref[
                        pl.ds(pl.multiple_of(at, rows), rows), :
                    ]


def feed_seq_kernel(bits, left, place_ref, *refs):
    in_refs, out_refs, (sum_ref,) = refs[:4], refs[4:8], refs[8:]
    for b in range(2):
        sum_ref[...] = in_refs[2 * b][...].astype(f32) + in_refs[2 * b + 1][...].astype(f32)
        rows = sum_ref.shape[0] // (3 << left)
        position = (left - 1) * b
        mine = seq_bit(place_ref, bits - left if b == 0 else left - 1)
        for n, bit in enumerate((mine, 1 - mine)):
            out_ref = out_refs[2 * b + n]
            for k in range(3):
                for i in range(1 << (left - 1)):
                    at = ((k << left) + with_bit(i, position, bit)) * rows
                    first = ((k << (left - 1)) + i) * rows
                    out_ref[first : first + rows, :] = sum_ref[
                        pl.ds(pl.multiple_of(at, rows), rows), :
                    ].astype(bf16)


def feed_head_kernel(pairs, place_ref, *refs):
    in_refs, out_refs, (sum_ref,) = refs[:4], refs[4:-1], refs[-1:]
    size = in_refs[0].shape[0]
    for b in range(2):
        sum_ref[b * size : (b + 1) * size, :] = in_refs[2 * b][...].astype(f32) + in_refs[
            2 * b + 1
        ][...].astype(f32)
    rows = out_refs[0].shape[0] // 6
    for shift, out_ref in enumerate(out_refs):
        at = lax.rem(lax.div(place_ref[0], 2) + shift, pairs) * rows
        for n in range(6):
            piece = sum_ref[pl.ds(pl.multiple_of(at + n * rows * pairs, rows), rows), :]
            out_ref[n * rows : (n + 1) * rows, :] = piece.astype(bf16)


def feed_pair_kernel(count, place_ref, *refs):
    parts, out_refs, (sum_ref,) = refs[:count], refs[count:-1], refs[-1:]
    sum_ref[...] = add_up([part[...] for part in parts])
    rows = out_refs[0].shape[0] // 6
    for other, out_ref in enumerate(out_refs):
        odd = lax.rem(place_ref[0] + other, 2) == 1
        for n in range(2):
            core = lax.rem(place_ref[1] + n, 2)
            for k in range(3):
                both = sum_ref[pl.ds(pl.multiple_of((core * 3 + k) * 2 * rows, 2 * rows), 2 * rows), :]
                first = (n * 3 + k) * rows
                value = jnp.where(odd, both[rows:], both[:rows])
                out_ref[first : first + rows, :] = value.astype(bf16)


def feed_out_kernel(hidden, place_ref, *refs):
    parts, (gate_ref, up_ref, down_ref) = refs[:4], refs[4:]
    rows = parts[0].shape[0] // 6
    own = lax.rem(place_ref[0], 2) * 2 + place_ref[1]
    for k, out_ref in enumerate((gate_ref, up_ref, down_ref)):
        values = [
            part[(n % 2 * 3 + k) * rows : (n % 2 * 3 + k + 1) * rows, :].astype(f32)
            for n, part in enumerate(parts)
        ]
        for g in range(4):
            value = values[0]
            for n in range(1, 4):
                value = jnp.where(own == (g ^ n), values[n], value)
            start = g * hidden % 128
            value = value[:, start : start + hidden]
            out_ref[:, g * hidden : (g + 1) * hidden] = value


def mixer_blocks_kernel(place_ref, own_ref, got_ref, *out_refs):
    count = len(out_refs)
    half = own_ref.shape[0] - 16
    rows = half // count
    small = two_parts(joined_parts(own_ref, half, 8) + joined_parts(got_ref, half, 8))
    for shift, out_ref in enumerate(out_refs):
        at = pl.ds(pl.multiple_of(lax.rem(place_ref[2] + shift, count) * rows, 16), rows)
        out_ref[0:rows, :] = (own_ref[at, :].astype(f32) + got_ref[at, :].astype(f32)).astype(bf16)
        out_ref[rows:, :] = small
        copies.done(out_ref)


def joined_parts(ref, start, extra):
    both = ref[start : start + 2 * extra, :].astype(f32)
    return both[:extra] + both[extra:]


def mixer_sum_kernel(count, nh, *refs):
    parts, out_refs = refs[:count], refs[count:]
    weight_refs, conv_refs, (decay_ref, gain_ref) = out_refs[:7], out_refs[7:10], out_refs[10:]
    rows = weight_refs[0].shape[0]
    nq = nh * 128
    starts = (0, nq, 3 * nq, 5 * nq, 5 * nq + 2 * nh, 5 * nq + 128, 6 * nq + 128)
    for n, (start, out_ref) in enumerate(zip(starts, weight_refs)):
        turned = n in (3, 4, 6)
        width = out_ref.shape[0] if turned else out_ref.shape[1]
        total = add_up([part[0:rows, start : start + width] for part in parts])
        out_ref[...] = jnp.transpose(total) if turned else total
    small = add_up([joined_parts(part, rows, 8) for part in parts])
    for start, out_ref in zip(starts, conv_refs):
        out_ref[...] = small[0:4, start : start + out_ref.shape[1]]
    decay_ref[...] = small[4:5, 2 * nh : 3 * nh]
    gain_ref[...] = small[4:5, 128 : 128 + nq]


def norm_back(grad_normed, rows, gain):
    scale = lax.rsqrt(jnp.mean(rows * rows, -1, keepdims=True) + EPS)
    unit = rows * scale
    scaled = grad_normed * gain
    grad_rows = scale * (scaled - unit * jnp.mean(scaled * unit, -1, keepdims=True))
    return grad_rows, jnp.sum(grad_normed * unit, 0, keepdims=True)


def middle_back_kernel(a_ref, b_ref, c_ref, middle_ref, cot_ref, gain_ref, grad_ref, low_ref, sum_ref):
    total = a_ref[...].astype(f32) + b_ref[...].astype(f32) + c_ref[...].astype(f32)
    rows, sum_ref[...] = norm_back(total, middle_ref[...], gain_ref[...])
    grad = cot_ref[...].astype(f32) + rows
    grad_ref[...] = grad
    low_ref[...] = grad.astype(bf16)


def extra_rows_kernel(count, *refs):
    parts, (rim_ref, gains_ref) = refs[:count], refs[count:]
    each = parts[0].shape[0] - RIM
    total = add_up([part[each:, :] for part in parts])
    row = iota2((RIM, 1), 0)
    rim_ref[...] = jnp.where(row >= RIM - 3, total, 0.0).astype(bf16)
    gains_ref[...] = jnp.zeros(gains_ref.shape, f32)
    for n in range(2):
        gains_ref[n : n + 1, :] = total[2 * n : 2 * n + 1] + total[2 * n + 1 : 2 * n + 2]


def tokens_back_kernel(count, *refs):
    parts, (rim_ref, tok_ref, gain_ref, middle_ref, grad_ref) = refs[:count], refs[count:]
    each = tok_ref.shape[0]
    total = add_up([part[0:each, :] for part in parts])
    rim = rim_ref[...].astype(f32)
    total = total + jnp.concatenate([jnp.zeros((each - RIM, rim.shape[1]), f32), rim], 0)
    rows, _ = norm_back(total, tok_ref[...].astype(f32), gain_ref[...])
    grad_ref[...] = middle_ref[...] + rows


HEAD = ("pair", "half")


def axis_size(axis):
    return lax.axis_size(axis) if isinstance(axis, str) else lax.psum(1, axis)


def ring(value, axis):
    count = axis_size(axis)
    return [value] + [
        lax.ppermute(value, axis, [(i, (i + shift) % count) for i in range(count)])
        for shift in range(1, count)
    ]


def along(value, axis, shift):
    count = axis_size(axis)
    pairs = [(i, i + shift) for i in range(count) if 0 <= i + shift < count]
    return lax.ppermute(value, axis, pairs)


def crossed(value, axis, bit=0):
    return lax.ppermute(value, axis, [(i, i ^ (1 << bit)) for i in range(axis_size(axis))])


def spread(blocks, axis):
    count = axis_size(axis)
    return [blocks[0]] + [
        lax.ppermute(blocks[shift], axis, [(i, (i + shift) % count) for i in range(count)])
        for shift in range(1, count)
    ]


def add_up(parts):
    total = parts[0].astype(f32)
    for part in parts[1:]:
        total = total + part.astype(f32)
    return total


def sum_over(value, axis):
    return add_up(ring(value, axis))


def tied(*values):
    return lax.optimization_barrier(values)


def on_device(
    tokens, doc_ids, norm_gain, w_query, w_key, w_value, w_beta, w_decay, w_outgate, conv_query,
    conv_key, conv_value, decay_log, out_gain, w_out, mlp_gain, w_gate, w_up, w_down, cotangent,
):
    head_n, seq_n, batch_n = (axis_size(a) for a in (HEAD, "seq", "batch"))
    me = lax.axis_index(HEAD)
    nh = w_decay.shape[1]
    nq = nh * 128
    each, model = tokens.shape
    length = each * head_n
    me_array = me.astype(i32).reshape(1)

    head_last = head_n - 1
    blocks = ring(tokens, HEAD)
    seq_place = lax.axis_index("seq")
    core = lax.axis_index("batch")
    ways = 2 * batch_n
    hidden = w_gate.shape[1] // ways
    mine = ((me & 1) * batch_n + core) * hidden
    place = jnp.stack([me, core, seq_place, mine // 128 * 128, mine % 128]).astype(i32)
    window = -(-(hidden + 64) // 128) * 128
    ids = jnp.broadcast_to(doc_ids[-RIM:, None], (RIM, 128)).astype(bf16)
    tail = tied(jnp.concatenate([tokens[-RIM:], ids], 1), blocks[1])[0]
    rim = add_up(
        [
            lax.ppermute(
                tail,
                ("seq", *HEAD),
                [(s * head_n + head_last, (s + 1) * head_n + h) for s in range(seq_n - 1)],
            )
            for h in range(head_n)
        ]
    ).astype(bf16)
    info, doc_rows = token_info(doc_ids)
    w_small = jnp.pad(jnp.concatenate([w_beta, w_decay], 1), ((0, 0), (0, 128 - 3 * nh)))
    rate = jnp.pad(-jnp.exp(decay_log), (2 * nh, 128 - 3 * nh))[None]
    weights = (w_query, w_key, w_value, w_outgate, w_small)
    taps = (conv_query, conv_key, conv_value)
    gain = norm_gain[None]
    fwd = mixer_forward(me_array, blocks, rim, gain, weights, taps, info, doc_rows, rate)

    states = ring(fwd["low"], "seq")
    cot_sent = tied(cotangent, fwd["low"])[0]
    cot_near = crossed(cot_sent, HEAD)
    cots = [cotangent, cot_near, *[crossed(value, "batch") for value in (cot_sent, cot_near)]]
    out = mixer_output(place, states[1:], fwd, out_gain[None], w_out, head_n)

    low = lambda *shape: sds(*shape, dtype=bf16)
    parts = spread(out["branch"], HEAD)
    middle, normed_mid = kernel_call(
        functools.partial(middle_kernel, len(parts)), "middle",
        (tokens, *parts, mlp_gain[None]), [sds(each, model), low(each, model)],
        after=cots[1:],
    )
    near = crossed(normed_mid, HEAD)
    rows = [normed_mid, near, crossed(normed_mid, "batch"), crossed(near, "batch")]
    fed = pl.pallas_call(
        functools.partial(feed_kernel, hidden),
        name="feed",
        in_specs=[SMEM] + [VMEM] * 8 + [ANY] * 3,
        out_specs=[VMEM] * 9,
        out_shape=[low(each, model)] * 8 + [low(3, 4 * each, window)],
        scratch_shapes=[
            pltpu.VMEM((model, window), bf16), pltpu.VMEM((model, window), bf16),
            pltpu.VMEM((window, model), bf16), pltpu.SemaphoreType.DMA((3,)),
        ],
        compiler_params=pltpu.CompilerParams(vmem_limit_bytes=40 * MIB),
        cost_estimate=pl.CostEstimate(flops=10**10, bytes_accessed=0, transcendentals=0),
    )(place, *rows, *cots, w_gate, w_up, w_down)

    def own_parts(blocks):
        given = (blocks[1].astype(f32) + crossed(blocks[3], "batch").astype(f32)).astype(bf16)
        return given, (blocks[0], crossed(blocks[2], "batch"), crossed(given, HEAD))

    given, norm_parts = own_parts(fed[:4])
    block_own = crossed(fed[6], "batch")
    block_given = (fed[5].astype(f32) + crossed(fed[7], "batch").astype(f32)).astype(bf16)

    seq_rows = model // (batch_n * seq_n)
    seq_bits = seq_n.bit_length() - 1
    size = 3 * model // 4
    feed_kept = kernel_call(
        functools.partial(feed_grads_kernel, seq_bits), "feed_grads",
        (place, *rows, *cots, *late(fed[8])), late(*[low(size, window)] * 4),
        scratch=[
            pltpu.VMEM((2, model, 4 * each), bf16), pltpu.VMEM((model // 2, window), bf16),
        ],
        after=[given],
    )

    def exchanged(values, step):
        bits = (step, seq_bits - 1 - step)
        return [
            value
            for b in range(2)
            for value in (values[2 * b], crossed(values[2 * b + 1], "seq", bits[b]))
        ]

    grad_middle, grad_branch, grad_mlp_gain = kernel_call(
        middle_back_kernel, "middle_back",
        (*norm_parts, middle, cotangent, mlp_gain[None]),
        [sds(each, model), low(each, model), sds(1, model)],
        after=feed_kept[1::2], cost=100,
    )
    feed_grads = exchanged(feed_kept, 0)
    grad_blocks = ring(grad_branch, HEAD)

    for step in range(1, seq_bits):
        size //= 2
        feed_kept = kernel_call(
            functools.partial(feed_seq_kernel, seq_bits, seq_bits - step), "feed_seq",
            (place, *feed_grads), late(*[low(size, window)] * 4),
            scratch=[pltpu.VMEM((2 * size, window), f32)],
            after=grad_blocks[1:2],
        )
        feed_grads = exchanged(feed_kept, step)
    adj = mixer_adjoint(
        me_array, grad_blocks, w_out, fwd, out, out_gain[None],
        after=[block_given, block_own, feed_kept[1]],
    )
    later = [along(adj["local"], "seq", -s) for s in range(seq_n - 1, 0, -1)]

    own_rows = model // (batch_n * seq_n * head_n)
    seq_rows = own_rows * head_n
    pairs = head_n // 2
    feed_kept = kernel_call(
        functools.partial(feed_head_kernel, pairs), "feed_head", (place, *feed_grads),
        late(*[low(12 * own_rows, window)] * pairs),
        scratch=[pltpu.VMEM((6 * seq_rows, window), f32)],
        after=[adj["local"]],
    )
    normed_parts, wide = mixer_backward(
        place, states[1:], later, fwd, out, adj, taps, rate,
        (w_query, w_key, w_value, w_small, w_outgate), gain, grad_mlp_gain, grad_blocks,
        after=[feed_kept[-1]],
    )
    feed_grads = [feed_kept[0]] + [
        lax.ppermute(
            feed_kept[shift], HEAD, [(i, (i + 2 * shift) % head_n) for i in range(head_n)]
        )
        for shift in range(1, pairs)
    ]
    block_given = crossed(tied(feed_kept[0], block_given)[1], HEAD)
    block_out = (middle + add_up([fed[4], block_own, block_given])).astype(bf16)
    normed_parts = spread(normed_parts, HEAD)

    columns = wide[0].shape[1]
    wide_blocks = kernel_call(
        mixer_blocks_kernel, "mixer_blocks",
        (place, wide[0], crossed(tied(wide[1], block_given, *feed_grads[1:])[0], "batch")),
        late(*[low(seq_rows + 16, columns)] * seq_n),
    )
    wide_parts = spread(wide_blocks, "seq")
    extra, gains = kernel_call(
        functools.partial(extra_rows_kernel, head_n), "extra_rows", normed_parts,
        [low(RIM, model), sds(8, model)],
        after=wide_parts[1:2],
    )
    gains = add_up([gains, crossed(gains, "batch")])
    gain_parts = ring(gains, "seq")
    rim_part = lax.ppermute(
        extra,
        ("seq", *HEAD),
        [(s * head_n + head_last, (s - 1) * head_n + head_last) for s in range(1, seq_n)],
    )
    group_own, group_sent = kernel_call(
        functools.partial(feed_pair_kernel, pairs), "feed_pair", (place, *feed_grads),
        [low(6 * own_rows, window)] * 2,
        scratch=[pltpu.VMEM((12 * own_rows, window), f32)],
        after=[extra],
    )
    group_got = crossed(group_sent, HEAD)
    group = [group_own, crossed(group_own, "batch"), group_got, crossed(group_got, "batch")]
    grad_gate, grad_up, grad_down = kernel_call(
        functools.partial(feed_out_kernel, hidden), "feed_out", (place, *group),
        [sds(own_rows, ways * hidden)] * 3,
    )
    (grad_tokens,) = kernel_call(
        functools.partial(tokens_back_kernel, head_n), "tokens_back",
        (*normed_parts, rim_part, tokens, gain, grad_middle),
        [sds(each, model)],
    )
    *sums, grad_decay, grad_out_gain = kernel_call(
        functools.partial(mixer_sum_kernel, seq_n, nh), "mixer_sum", wide_parts,
        [sds(seq_rows, w) for w in (nq, 2 * nq, 2 * nq)] + [sds(w, seq_rows) for w in (2 * nh, nh)]
        + [sds(seq_rows, nq), sds(nq, seq_rows)]
        + [sds(4, w) for w in (nq, 2 * nq, 2 * nq)] + [sds(1, nh), sds(1, nq)],
    )
    grad_q, grad_k, grad_v, grad_b, grad_d, grad_g, grad_out, *grad_convs = sums
    gains = add_up(gain_parts)
    index = (core * seq_n + seq_place) * head_n + me
    gains = lax.dynamic_slice_in_dim(gains, index * own_rows, own_rows, 1)
    return (
        block_out, grad_tokens, gains[0], grad_q, grad_k, grad_v, grad_b.T, grad_d.T, grad_g,
        *grad_convs, grad_decay[0], grad_out_gain[0], grad_out, gains[1], grad_gate, grad_up,
        grad_down.T,
    )


def solution(mesh):
    batch, seq, head = mesh.devices.shape
    split_mesh = Mesh(mesh.devices.reshape(batch, seq, head // 2, 2), ("batch", "seq", *HEAD))
    return jax.shard_map(
        on_device,
        mesh=split_mesh,
        in_specs=(
            P(("batch", "seq", *HEAD), None),
            P(("batch", "seq")),
            P(),
            P(None, HEAD),
            P(None, HEAD),
            P(None, HEAD),
            P(None, HEAD),
            P(None, HEAD),
            P(None, HEAD),
            P(None, HEAD),
            P(None, HEAD),
            P(None, HEAD),
            P(HEAD),
            P(HEAD),
            P(HEAD, None),
            P(),
            P(),
            P(),
            P(),
            P(("batch", "seq", *HEAD), None),
        ),
        out_specs=(
            P(("batch", "seq", *HEAD), None),
            P(("batch", "seq", *HEAD), None),
            P(("batch", "seq", *HEAD)),
            P(("batch", "seq"), HEAD),
            P(("batch", "seq"), HEAD),
            P(("batch", "seq"), HEAD),
            P(("batch", "seq"), HEAD),
            P(("batch", "seq"), HEAD),
            P(("batch", "seq"), HEAD),
            P(None, HEAD),
            P(None, HEAD),
            P(None, HEAD),
            P(HEAD),
            P(HEAD),
            P(HEAD, ("batch", "seq")),
            P(("batch", "seq", *HEAD)),
            P(("batch", "seq", *HEAD), None),
            P(("batch", "seq", *HEAD), None),
            P(None, ("batch", "seq", *HEAD)),
        ),
        check_vma=False,
    )
```

```python
import functools

import jax
import jax.numpy as jnp
from jax import lax
from jax.experimental import pallas as pl
from jax.experimental.pallas import tpu as pltpu
from jax.sharding import Mesh
from jax.sharding import PartitionSpec as P

bf16, f32, i32 = jnp.bfloat16, jnp.float32, jnp.int32
EPS = 1e-06
CT = 64
RIM = 16
NN = ((1,), (0,))
NT = ((1,), (1,))
MIB = 1 << 20
FORWARD, OUTPUT, ADJOINT, BACKWARD = 4, 4, 8, 8


def mm(a, b, dims=NN):
    return lax.dot_general(a, b, (dims, ((), ())), preferred_element_type=f32)


def split(x):
    high = x.astype(bf16)
    return high, (x - high.astype(f32)).astype(bf16)


def mm3(a, b, dims=NN):
    return mm(a[0], b[0], dims) + (mm(a[0], b[1], dims) + mm(a[1], b[0], dims))


def mm3_deep(a, b, dims=NN):
    if a[0].shape[1] % 128:
        return mm3(a, b, dims)
    left = jnp.concatenate([a[0], a[1]], 1)
    right = jnp.concatenate([b[0], b[0]], 1 if dims == NT else 0)
    return mm(left, right, dims) + mm(a[0], b[1], dims)


def exact(a, b):
    return lax.dot_general(
        a, b, (NN, ((), ())), precision=lax.Precision.HIGHEST, preferred_element_type=f32
    )


def iota2(shape, dim):
    return lax.broadcasted_iota(i32, shape, dim)


def rows_of(c, size=CT, start=0):
    return pl.ds(pl.multiple_of(c * size + start, 16), size)


def near(c, start):
    return pl.ds(pl.multiple_of(c * CT + start, 8), CT + 8)


def step_order():
    size = 2 * CT
    row, col = iota2((size, size), 0), iota2((size, size), 1)
    row_tok, col_tok = row & (CT - 1), col & (CT - 1)
    later = jnp.where(row_tok > col_tok, row_tok ^ col_tok, 0)
    same_token = (row_tok == col_tok) & (row >= CT) & (col < CT)
    return row, col, later, same_token


def twice(x):
    return jnp.concatenate([x, x], 0)


def head_steps(ref, rows, h):
    return jnp.concatenate(
        [ref[rows, (2 * h + j) * 128 : (2 * h + j + 1) * 128] for j in range(2)], 0
    )


def decays(gam_ref, info, rows, h, nh):
    gcol = gam_ref[rows, 2 * nh + h : 2 * nh + h + 1]
    glast = gcol[CT - 1 : CT, :]
    carried = jnp.exp(gcol) * info[:, 4:5]
    tail = jnp.exp(jnp.minimum(glast - gcol, 0.0)) * info[:, 5:6]
    keep = carried[CT - 1 : CT, :]
    return gcol, carried, tail, keep


def forward_kernel(
    nh, count, me_ref, *refs
):
    tok_refs, refs = refs[:count], refs[count:]
    forward_body(nh, me_ref, tok_refs, *refs)


def forward_body(
    nh, me_ref, tok_refs, rim_ref, ng_ref, wq_ref, wk_ref, wv_ref, wg_ref, ws_ref, tq_ref, tk_ref, tv_ref,
    flags_ref, drow_ref, rate_ref,
    normed_ref, pre_ref, conv_ref, gate_ref, q_ref, k_ref, v_ref, beta_ref, glog_ref, gam_ref, dec_ref,
    t_ref, w_ref, u_ref, reach_ref, score_ref, at_ref, bt_ref, info_ref, low_ref, st_ref,
):
    length = pre_ref.shape[0] - RIM
    nc = length // CT
    gain = ng_ref[...]
    count = len(tok_refs)
    each = tok_refs[0].shape[0]

    def normal(x):
        x = x.astype(f32)
        scale = lax.rsqrt(jnp.mean(x * x, -1, keepdims=True) + EPS)
        return (x * scale * gain).astype(bf16)

    model = ng_ref.shape[1]
    normed_ref[0:RIM, :] = normal(rim_ref[:, :model])
    info_ref[...] = flags_ref[...]
    first = flags_ref[RIM : RIM + 8, :]
    ids = jnp.concatenate([rim_ref[8:, model : model + 8].astype(f32), first[:, 6:7] + jnp.zeros((8, 8), f32)], 0)
    row, col = iota2((8, 8), 0), iota2((8, 8), 1)
    for m in range(1, 4):
        same = (pltpu.roll(ids, m, 0)[8:] == ids[8:]).astype(f32)
        first = jnp.where((col == m) & (row < m), same, first)
    info_ref[RIM : RIM + 8, :] = first

    for shift, tok_ref in enumerate(tok_refs):
        place = lax.rem(me_ref[0] + (count - shift), count) * each

        def norm_rows(c, carry):
            target = pl.ds(pl.multiple_of(place + c * CT + RIM, 16), CT)
            normed_ref[target, :] = normal(tok_ref[rows_of(c), :])
            return carry

        lax.fori_loop(0, each // CT, norm_rows, 0)
    copies.done(normed_ref)
    copies.need(wq_ref, wk_ref, wv_ref, wg_ref, ws_ref)
    nq = nh * 128
    groups = ((wq_ref, 0, nq), (wk_ref, nq, 2 * nq), (wv_ref, 3 * nq, 2 * nq))

    for weight, first, width in groups:
        pre_ref[0:RIM, first : first + width] = (
            mm(normed_ref[0:RIM, :], weight[...]).astype(bf16).astype(f32)
        )

    def project(i, carry):
        rows = rows_of(i, 256, RIM)
        block = normed_ref[rows, :]
        for weight, first, width in groups:
            pre_ref[rows, first : first + width] = mm(block, weight[...]).astype(bf16).astype(f32)
        plain = rows_of(i, 256)
        gate_ref[plain, :] = mm(block, wg_ref[...])
        glog_ref[plain, :] = mm(block, ws_ref[...])
        return carry

    lax.fori_loop(0, length // 256, project, 0)
    copies.done(pre_ref, gate_ref)
    logits = glog_ref[...]
    beta_ref[...] = jax.nn.sigmoid(logits)
    soft = jnp.maximum(logits, 0.0) + jnp.log1p(jnp.exp(-jnp.abs(logits)))
    glog = rate_ref[...] * soft
    glog_ref[...] = glog
    tri = (iota2((CT, CT), 0) >= iota2((CT, CT), 1)).astype(f32)
    for c in range(nc):
        gam_ref[c * CT : (c + 1) * CT, :] = exact(tri, glog[c * CT : (c + 1) * CT, :])

    def conv_rows(c, carry):
        rows = rows_of(c)
        info = info_ref[rows_of(c, CT, RIM), :]
        mask = [info[:, m : m + 1] for m in range(4)]
        for tap_ref, first, count, kind in (
            (tq_ref, 0, nh, "q"), (tk_ref, nq, 2 * nh, "k"), (tv_ref, 3 * nq, 2 * nh, "v")
        ):
            for j in range(count):
                cols = slice(first + j * 128, first + (j + 1) * 128)
                mine = slice(j * 128, (j + 1) * 128)
                taps = tap_ref[:, mine].astype(f32)
                block = pre_ref[near(c, RIM - 8), cols]
                total = block[8:] * taps[0:1]
                for m in range(1, 4):
                    total = total + pltpu.roll(block, m, 0)[8:] * mask[m] * taps[m : m + 1]
                conv_ref[rows, cols] = total
                out = total * jax.nn.sigmoid(total)
                if kind == "k":
                    out = out * lax.rsqrt(jnp.sum(out * out, -1, keepdims=True) + EPS)
                {"q": q_ref, "k": k_ref, "v": v_ref}[kind][rows, mine] = out
        return carry

    lax.fori_loop(0, nc, conv_rows, 0)
    copies.done(conv_ref, q_ref, k_ref, v_ref, beta_ref, glog_ref, gam_ref)

    row, col, later, same_token = step_order()
    eye = (row == col).astype(f32)
    small_row, small_col = iota2((CT, CT), 0), iota2((CT, CT), 1)

    def prepare(group, carry):
        items = [(group * FORWARD + i, h) for i in range(FORWARD) for h in range(nh)]
        systems, rhs, tails, keeps = [], [], [], []
        for c, h in items:
            rows = rows_of(c)
            info = info_ref[rows_of(c, CT, RIM), :]
            same = (info[:, 6:7] == drow_ref[c]) & (small_row >= small_col)
            gcol, carried, tail, keep = decays(gam_ref, info, rows, h, nh)
            grow = jnp.sum(jnp.where(small_row == small_col, gcol, 0.0), 0, keepdims=True)
            decay = jnp.where(same, jnp.exp(jnp.minimum(gcol - grow, 0.0)), 0.0)
            wide = jnp.concatenate([decay, decay], 1)
            dec_ref[c, h] = wide
            key = head_steps(k_ref, rows, h)
            value = head_steps(v_ref, rows, h)
            beta = jnp.concatenate(
                [beta_ref[rows, 2 * h + j : 2 * h + j + 1] for j in range(2)], 0
            )
            key2 = split(key)
            query = q_ref[rows, h * 128 : (h + 1) * 128]
            query2 = split(query)
            pairs = mm3([jnp.concatenate(x, 0) for x in zip(key2, query2)], key2, NT)
            score_ref[c, h] = pairs[2 * CT :] * wide
            reach_ref[c, h] = query * carried
            systems.append(
                jnp.where((later > 0) | same_token, beta * pairs[: 2 * CT] * twice(wide), 0.0)
            )
            rhs.append(jnp.concatenate([beta * twice(carried) * key, beta * value], 1))
            tails.append(key * twice(tail))
            keeps.append(keep)
        inverse = [eye - jnp.where(same_token, n, 0.0) for n in systems]
        for level in range(6):
            part = (later >> level) == 1
            blocks = [split(jnp.where(part, n, 0.0)) for n in systems]
            inverse2 = [split(x) for x in inverse]
            first = [split(mm3(b, x)) for b, x in zip(blocks, inverse2)]
            inverse = [x - mm3(x2, y) for x, x2, y in zip(inverse, inverse2, first)]
        mixed = [mm3(split(x), split(r)) for x, r in zip(inverse, rhs)]
        products = [mm3(split(jnp.transpose(m)), split(t)) for m, t in zip(mixed, tails)]
        for n, (c, h) in enumerate(items):
            t_ref[c, h] = inverse[n]
            w_ref[c, h] = mixed[n][:, :128]
            u_ref[c, h] = mixed[n][:, 128:]
            at_ref[c, h] = keeps[n] * eye - products[n][:128]
            bt_ref[c, h] = products[n][128:]
        part = pl.ds(group * FORWARD, FORWARD)
        copies.done(dec_ref, score_ref, reach_ref, t_ref, w_ref, u_ref, at_ref, bt_ref, at=part)
        return carry

    lax.fori_loop(0, nc // FORWARD, prepare, 0)

    for h in range(nh):
        st_ref[h, :128] = at_ref[0, h]
        st_ref[h, 128:] = bt_ref[0, h]

    def chain(c, carry):
        for h in range(nh):
            after = mm3(split(st_ref[h]), split(at_ref[c, h]))
            st_ref[h, :128] = after[:128]
            st_ref[h, 128:] = after[128:] + bt_ref[c, h]
        return carry

    lax.fori_loop(1, nc, chain, 0)
    low_ref[...] = st_ref[...].astype(bf16)


def output_kernel(nh, count, blocks, me_ref, *refs):
    output_body(nh, me_ref, refs[:count], *refs[count : -blocks - 1], refs[-blocks - 1 : -1], refs[-1])


def output_body(
    nh, me_ref, map_refs, at_ref, bt_ref, w_ref, reach_ref, u_ref, score_ref, gate_ref, gain_ref, wout_ref,
    sin_ref, fresh_ref, core_ref, gated_ref, branch_refs, all_ref,
):
    nc = w_ref.shape[0]
    states = []
    for h in range(nh):
        state = jnp.zeros((128, 128), f32)
        for distance in range(len(map_refs), 0, -1):
            map_ref = map_refs[distance - 1]
            passed = split(map_ref[h, :128].astype(f32))
            state = mm3(split(state), passed) + map_ref[h, 128:].astype(f32)
            state = jnp.where(me_ref[2] >= distance, state, 0.0)
        states.append(state)

    def chain(c, states):
        out = []
        for h in range(nh):
            sin_ref[c, h] = states[h]
            out.append(mm3(split(states[h]), split(at_ref[c, h])) + bt_ref[c, h])
        return tuple(out)

    copies.need(at_ref, bt_ref)
    states = lax.fori_loop(0, nc, chain, tuple(states))
    for h in range(nh):
        sin_ref[nc, h] = states[h]
    copies.done(sin_ref)
    copies.need(w_ref, reach_ref, u_ref, score_ref, gate_ref)

    def outputs(group, carry):
        for c, h in [(group * OUTPUT + i, h) for i in range(OUTPUT) for h in range(nh)]:
            rows = rows_of(c)
            cols = slice(h * 128, (h + 1) * 128)
            state2 = split(sin_ref[c, h])
            probe = jnp.concatenate([w_ref[c, h], reach_ref[c, h]], 0)
            seen = mm3(split(probe), state2, NT)
            fresh = u_ref[c, h] - seen[: 2 * CT]
            fresh_ref[c, h] = fresh
            core = seen[2 * CT :] + mm3(split(score_ref[c, h]), split(fresh))
            core_ref[rows, cols] = core
            unit = core * lax.rsqrt(jnp.mean(core * core, -1, keepdims=True) + EPS)
            gate = gate_ref[rows, cols]
            gated_ref[rows, cols] = (
                unit * gain_ref[:, cols] * (gate * jax.nn.sigmoid(gate))
            ).astype(bf16)
        copies.done(fresh_ref, at=pl.ds(group * OUTPUT, OUTPUT))
        copies.done(core_ref, gated_ref, at=rows_of(group, OUTPUT * CT))
        return carry

    lax.fori_loop(0, nc // OUTPUT, outputs, 0)
    copies.need(wout_ref)
    all_ref[...] = mm(gated_ref[...], wout_ref[...]).astype(bf16)
    count = len(branch_refs)
    each = branch_refs[0].shape[0]
    for shift, branch_ref in enumerate(branch_refs):
        place = lax.rem(me_ref[0] + shift, count) * each
        branch_ref[...] = all_ref[pl.ds(pl.multiple_of(place, 16), each), :]
        copies.done(branch_ref)


def adjoint_kernel(nh, count, me_ref, *refs):
    adjoint_body(nh, me_ref, refs[:count], *refs[count:])


def adjoint_body(
    nh, me_ref, g_refs, wout_ref, core_ref, gate_ref, gain_ref, score_ref, reach_ref, w_ref, at_ref,
    dcore_ref, dt_ref, dgate_ref, dgain_ref, local_ref, dgated_ref, all_ref,
):
    nc = w_ref.shape[0]
    count = len(g_refs)
    each = g_refs[0].shape[0]
    for shift, g_ref in enumerate(g_refs):
        place = lax.rem(me_ref[0] + (count - shift), count) * each
        all_ref[pl.ds(pl.multiple_of(place, 16), each), :] = g_ref[...]
    copies.need(wout_ref)
    dgated_ref[...] = mm(all_ref[...], wout_ref[...], NT)
    copies.need(core_ref, gate_ref, score_ref, reach_ref, w_ref)

    def chunks(group, dgain):
        for i in range(ADJOINT):
            dgain = dgain + chunk(group * ADJOINT + i)
        copies.done(dt_ref, at=pl.ds(group * ADJOINT, ADJOINT))
        copies.done(dcore_ref, dgate_ref, at=rows_of(group, ADJOINT * CT))
        return dgain

    def chunk(c):
        rows = rows_of(c)
        sums = []
        for h in range(nh):
            cols = slice(h * 128, (h + 1) * 128)
            core = core_ref[rows, cols]
            scale = lax.rsqrt(jnp.mean(core * core, -1, keepdims=True) + EPS)
            unit = core * scale
            gate = gate_ref[rows, cols]
            sig = jax.nn.sigmoid(gate)
            silu = gate * sig
            gain = gain_ref[:, cols]
            grad = dgated_ref[rows, cols]
            sums.append(jnp.sum(grad * unit * silu, 0, keepdims=True))
            dgate_ref[rows, cols] = (
                grad * unit * gain * (sig * (1.0 + gate * (1.0 - sig)))
            ).astype(bf16)
            dunit = grad * gain * silu
            dcore = scale * (dunit - unit * jnp.mean(dunit * unit, -1, keepdims=True))
            dcore_ref[rows, cols] = dcore
            across = jnp.transpose(dcore)
            dft = mm3_deep(split(across), split(score_ref[c, h]))
            left = jnp.concatenate([-dft, across], 1)
            right = jnp.concatenate([w_ref[c, h], reach_ref[c, h]], 0)
            dt_ref[c, h] = mm3_deep(split(left), split(right))
        return jnp.concatenate(sums, 1)

    dgain_ref[...] = lax.fori_loop(0, nc // ADJOINT, chunks, jnp.zeros(dgain_ref.shape, f32))

    copies.need(at_ref)

    def chain(i, carry):
        c = nc - 1 - i
        return tuple(
            mm3_deep(split(carry[h]), split(at_ref[c, h]), NT) + dt_ref[c, h] for h in range(nh)
        )

    start = tuple(dt_ref[nc - 1, h] for h in range(nh))
    total = lax.fori_loop(1, nc, chain, start)
    for h in range(nh):
        local_ref[h] = total[h].astype(bf16)


def normed_back(count, place_ref, gp_ref, weights, normed_ref, gain_ref, mlp_ref, out_refs, all_ref):
    each = out_refs[0].shape[0] - RIM
    length = all_ref.shape[0] - RIM
    total = jnp.zeros(gain_ref.shape, f32)
    for start in range(0, length, 256):
        rows = slice(start + (RIM if start else 0), start + 256 + RIM)
        first = 0
        grad = None
        for weight in weights:
            width = weight.shape[1]
            term = mm(gp_ref[rows, first : first + width], weight[...], NT)
            grad = term if grad is None else grad + term
            first += width
        all_ref[rows, :] = grad.astype(bf16)
        total = total + jnp.sum(grad * normed_ref[rows, :].astype(f32), 0, keepdims=True)
    rim = all_ref[0:RIM, :].astype(f32)
    row = iota2((RIM, 1), 0)
    gains = [*split(total / gain_ref[...]), *split(mlp_ref[...])]
    for n, gain in enumerate(gains):
        rim = jnp.where(row == n, gain.astype(f32), rim)
    rim = rim.astype(bf16)
    for shift, out_ref in enumerate(out_refs):
        place = lax.rem(place_ref[0] + shift, count) * each + RIM
        out_ref[0:each, :] = all_ref[pl.ds(pl.multiple_of(place, 16), each), :]
        out_ref[each:, :] = rim
        copies.done(out_ref)


def turn(left_ref, turned_ref):
    tokens, width = left_ref.shape
    for n in range(width // 128):
        turned_ref[n * 128 : (n + 1) * 128, :tokens] = jnp.transpose(
            left_ref[:, n * 128 : (n + 1) * 128]
        )


def two_halves(place_ref, turned, right, own_ref, given_ref, cols):
    half = turned.shape[0] // 2
    for core, out_ref in ((place_ref[1], own_ref), (1 - place_ref[1], given_ref)):
        rows = pl.ds(pl.multiple_of(core * half, 16), half)
        out_ref[0:half, cols] = mm(turned[rows, : right.shape[0]], right[...]).astype(out_ref.dtype)


def two_parts(value):
    high, low = split(value)
    return jnp.concatenate([high, low], 0)


def backward_kernel(nh, count, blocks, *refs):
    at = 2 * count + 1
    maps, local_sums, place, refs = refs[:count], refs[count : at - 1], refs[at - 1], refs[at:]
    inputs, refs = refs[:21], refs[21:]
    dgate, weights, (normed, gain, mlp, dgain), refs = refs[0], refs[1:6], refs[6:10], refs[10:]
    gated, grads, refs = refs[0], refs[1 : blocks + 1], refs[blocks + 1 :]
    out_refs, (own, given), refs = refs[:blocks], refs[blocks : blocks + 2], refs[blocks + 2 :]
    gp, taps, dlog, dconv, small, ends, everything, turned, turned_grad, sums = refs
    half, width = own.shape[0] - 16, gp.shape[1]
    wide, nq = own.shape[1], gated.shape[1]
    gp[0:RIM, width - nq :] = jnp.zeros((RIM, nq), bf16)
    backward_body(nh, maps, local_sums, *inputs, gp, taps, dlog, dconv, small, ends)
    copies.need(dgate, normed, gated, *grads)
    gp[RIM:, width - nq :] = dgate[...]
    turn(normed, turned)
    two_halves(place, turned, gp, own, given, slice(0, width))
    each = grads[0].shape[0]
    for shift, grad in enumerate(grads):
        at = pl.multiple_of(lax.rem(place[0] + (blocks - shift), blocks) * each, 128)
        for n in range(grad.shape[1] // 128):
            turned_grad[n * 128 : (n + 1) * 128, pl.ds(at, each)] = jnp.transpose(
                grad[:, n * 128 : (n + 1) * 128]
            )
    two_halves(place, turned_grad, gated, own, given, slice(width, wide))
    sums[...] = jnp.zeros(sums.shape, f32)
    sums[0:4, : taps.shape[1]] = taps[...]
    sums[4:5, :128] = dlog[...]
    sums[4:5, 128 : 128 + dgain.shape[1]] = dgain[...]
    own[half:, :] = two_parts(sums[...])
    given[half:, :] = own[half:, :]
    copies.done(given, own)
    copies.need(*weights)
    normed_back(blocks, place, gp, weights, normed, gain, mlp, out_refs, everything)


def backward_body(
    nh, map_refs, local_refs, at_ref, dt_ref, score_ref, dcore_ref, t_ref, fresh_ref, sin_ref,
    q_ref, k_ref, v_ref, beta_ref, gam_ref, dec_ref, conv_ref, pre_ref, info_ref, tq_ref, tk_ref, tv_ref,
    rate_ref, glog_ref,
    gp_ref, taps_ref, dlog_ref,
    dconv_ref, small_ref, ends_ref,
):
    length = q_ref.shape[0]
    nc = length // CT
    nq = nh * 128
    width = 5 * nq
    ends = []
    for h in range(nh):
        end = local_refs[0][h].astype(f32)
        for map_ref, local_ref in zip(map_refs[1:], local_refs[1:]):
            passed = split(map_ref[h, :128].astype(f32))
            end = mm3_deep(split(end), passed, NT) + local_ref[h].astype(f32)
        ends.append(end)
    row, col, later, same_token = step_order()
    before = (later > 0) | same_token
    last_row = (iota2((CT, 1), 0) == CT - 1).astype(f32)
    dconv_ref[0:RIM, :] = jnp.zeros((RIM, width), f32)
    dconv_ref[RIM + length :, :] = jnp.zeros((RIM, width), f32)
    lane = iota2((CT, 128), 1)
    upper = (iota2((CT, CT), 0) <= iota2((CT, CT), 1)).astype(f32)

    def chain(i, ends):
        c = nc - 1 - i
        out = []
        for h in range(nh):
            ends_ref[c, h] = ends[h]
            out.append(mm3_deep(split(ends[h]), split(at_ref[c, h]), NT) + dt_ref[c, h])
        return tuple(out)

    copies.need(at_ref, dt_ref)
    lax.fori_loop(0, nc, chain, tuple(ends))
    copies.need(score_ref, dcore_ref, t_ref, fresh_ref, sin_ref, q_ref, k_ref, v_ref, dec_ref, conv_ref)

    def chunks(group, carry):
        for i in range(BACKWARD):
            chunk(group * BACKWARD + i)
        return carry

    def chunk(c):
        rows = rows_of(c)
        store = rows_of(c, CT, RIM)
        info = info_ref[store, :]
        small = jnp.zeros((CT, 128), f32)
        dgam = jnp.zeros((CT, 128), f32)
        for h in range(nh):
            cols = slice(h * 128, (h + 1) * 128)
            end = ends_ref[c, h]
            end2 = split(end)
            _, carried, tail, _ = decays(gam_ref, info, rows, h, nh)
            carried2, tail2 = twice(carried), twice(tail)
            key = head_steps(k_ref, rows, h)
            value = head_steps(v_ref, rows, h)
            query = q_ref[rows, cols]
            beta = jnp.concatenate(
                [beta_ref[rows, 2 * h + j : 2 * h + j + 1] for j in range(2)], 0
            )
            wide = dec_ref[c, h]
            full = jnp.where(before, twice(wide), 0.0)
            state = sin_ref[c, h]
            fresh = fresh_ref[c, h]
            fresh2 = split(fresh)
            dcore = dcore_ref[rows, cols]
            dft = mm3_deep(split(jnp.transpose(dcore)), split(score_ref[c, h])) + mm3_deep(
                end2, split(key * tail2), NT
            )
            solved = jnp.transpose(mm3_deep(split(dft), split(t_ref[c, h])))
            both = split(jnp.concatenate([solved, dcore], 0))
            through = mm3_deep(both, split(state))
            pairs = mm3_deep(both, fresh2, NT)
            dtail = mm3_deep(fresh2, end2)
            em = -pairs[: 2 * CT] * full
            ps = pairs[2 * CT :] * wide
            mixed = mm3_deep(split(jnp.concatenate([em, ps], 0)), split(key))
            turned = jnp.transpose(jnp.concatenate([beta * em, ps], 0))
            dkb = mm3_deep(split(turned), split(jnp.concatenate([key, query], 0))) + tail2 * dtail
            x1 = mixed[: 2 * CT] - carried2 * through[: 2 * CT]
            dka = beta * x1
            dkey = dka + dkb
            dbeta = jnp.sum(key * x1 + solved * value, -1, keepdims=True)
            dvalue = beta * solved
            dquery = mixed[2 * CT :] + carried * through[2 * CT :]
            turn = jnp.sum(key * (dka - dkb), -1, keepdims=True)
            closing = jnp.sum(
                jnp.sum(end * sin_ref[c + 1, h], -1, keepdims=True), 0, keepdims=True
            )
            dg = (
                jnp.sum(query * dquery, -1, keepdims=True)
                + turn[:CT]
                + turn[CT:]
                + last_row * closing
            )
            dgam = jnp.where(lane == 2 * nh + h, dg, dgam)
            for j in range(2):
                small = jnp.where(lane == 2 * h + j, dbeta[j * CT : (j + 1) * CT], small)
            pre = conv_ref[rows, cols]
            sig = jax.nn.sigmoid(pre)
            dconv_ref[store, cols] = dquery * (sig * (1.0 + pre * (1.0 - sig)))
            for j in range(2):
                kcols = slice(nq + (2 * h + j) * 128, nq + (2 * h + j + 1) * 128)
                pre = conv_ref[rows, kcols]
                sig = jax.nn.sigmoid(pre)
                act = pre * sig
                scale = lax.rsqrt(jnp.sum(act * act, -1, keepdims=True) + EPS)
                unit = key[j * CT : (j + 1) * CT]
                grad = dkey[j * CT : (j + 1) * CT]
                grad = scale * (grad - unit * jnp.sum(unit * grad, -1, keepdims=True))
                dconv_ref[store, kcols] = grad * (sig * (1.0 + pre * (1.0 - sig)))
                vcols = slice(3 * nq + (2 * h + j) * 128, 3 * nq + (2 * h + j + 1) * 128)
                pre = conv_ref[rows, vcols]
                sig = jax.nn.sigmoid(pre)
                dconv_ref[store, vcols] = dvalue[j * CT : (j + 1) * CT] * (
                    sig * (1.0 + pre * (1.0 - sig))
                )
        dglog = exact(upper, dgam)
        small_ref[rows, :] = jnp.where(lane < 2 * nh, small, dglog)

    lax.fori_loop(0, nc // BACKWARD, chunks, 0)

    copies.need(pre_ref, glog_ref)
    beta = beta_ref[...]
    small = small_ref[...]
    lanes = iota2(beta.shape, 1)
    grads = small * beta * jnp.where(lanes < 2 * nh, 1.0 - beta, rate_ref[...])
    dlog_ref[...] = jnp.sum(small * glog_ref[...], 0, keepdims=True)
    gp_ref[0:RIM, 0 : width + 128] = jnp.zeros((RIM, width + 128), bf16)
    gp_ref[RIM:, width : width + 128] = grads.astype(bf16)
    groups = ((tq_ref, 0, nh), (tk_ref, nq, 2 * nh), (tv_ref, 3 * nq, 2 * nh))

    def turned_back(grad, masks, taps, count):
        total = grad[:count] * taps[0:1]
        size = grad.shape[0]
        for m in range(1, 4):
            moved = pltpu.roll(grad * masks[:, m : m + 1], size - m, 0)
            total = total + moved[:count] * taps[m : m + 1]
        return total

    def conv_back(c, sums):
        info = info_ref[near(c, RIM), :]
        new = []
        for tap_ref, first, count in groups:
            for j in range(count):
                cols = slice(first + j * 128, first + (j + 1) * 128)
                taps = tap_ref[:, j * 128 : (j + 1) * 128].astype(f32)
                grad = dconv_ref[near(c, RIM), cols]
                gp_ref[rows_of(c, CT, RIM), cols] = turned_back(grad, info, taps, CT).astype(bf16)
                block = pre_ref[near(c, RIM - 8), cols]
                parts = [jnp.sum(grad[:CT] * block[8:], 0, keepdims=True)]
                for m in range(1, 4):
                    moved = pltpu.roll(block, m, 0)[8:]
                    parts.append(
                        jnp.sum(grad[:CT] * info[:CT, m : m + 1] * moved, 0, keepdims=True)
                    )
                new.append(jnp.concatenate(parts, 0))
        return sums + jnp.concatenate(new, 1)

    taps_ref[...] = lax.fori_loop(0, nc, conv_back, jnp.zeros((4, width), f32))
    for tap_ref, first, count in groups:
        cols = slice(first, first + count * 128)
        taps = tap_ref[...].astype(f32)
        early = slice(8, 24)
        rim = turned_back(dconv_ref[early, cols], info_ref[early, :], taps, 8)
        gp_ref[0:RIM, cols] = jnp.concatenate([jnp.zeros_like(rim), rim], 0).astype(bf16)


VMEM = pl.BlockSpec(memory_space=pltpu.VMEM)
SMEM = pl.BlockSpec(memory_space=pltpu.SMEM)
ANY = pl.BlockSpec(memory_space=pl.ANY)


class Late:
    def __init__(self, value):
        self.value = value


def late(*values):
    return [Late(value) for value in values]


class Copies:
    def __init__(self):
        self.coming, self.going = {}, {}

    def need(self, *refs):
        for ref in refs:
            copy = self.coming.pop(id(ref), None)
            if copy is not None:
                copy.wait()

    def done(self, *refs, at=None):
        for ref in refs:
            entry = self.going.get(id(ref))
            if entry is None:
                continue
            target, sem, _ = entry
            source = ref
            if at is not None:
                source, target = ref.at[at], target.at[at]
            pltpu.make_async_copy(source, target, sem).start()
            self.going[id(ref)] = (entry[0], sem, True)

    def finish(self, refs):
        for copy in self.coming.values():
            copy.wait()
        self.coming = {}
        for ref in refs:
            if id(ref) in self.going and not self.going[id(ref)][2]:
                self.done(ref)
        for ref in refs:
            if id(ref) in self.going:
                target, sem, _ = self.going.pop(id(ref))
                pltpu.make_async_copy(ref, target, sem).wait()


copies = Copies()


def kernel_call(body, name, args, outs, scratch=(), after=(), hbm=(), mib=24, cost=2):
    late_in = [n for n, a in enumerate(args) if isinstance(a, Late)]
    late_out = [n for n, s in enumerate(outs) if isinstance(s, Late)]
    args = [a.value if isinstance(a, Late) else a for a in args]
    outs = [s.value if isinstance(s, Late) else s for s in outs]
    extra, n_in, n_out, n_scratch = len(after), len(args), len(outs), len(scratch)
    buffers = [pltpu.VMEM(args[n].shape, args[n].dtype) for n in late_in]
    buffers += [pltpu.VMEM(outs[n].shape, outs[n].dtype) for n in late_out]
    sems = [pltpu.SemaphoreType.DMA((len(late_in) + len(late_out),))] if buffers else []

    def run(*refs):
        in_refs, refs = list(refs[:n_in]), refs[n_in + extra :]
        out_refs, refs = list(refs[:n_out]), refs[n_out:]
        own_scratch, refs = refs[:n_scratch], refs[n_scratch:]
        held = []
        for k, n in enumerate(late_in):
            copy = pltpu.make_async_copy(in_refs[n], refs[k], refs[-1].at[k])
            copy.start()
            copies.coming[id(refs[k])] = copy
            in_refs[n] = refs[k]
        for k, n in enumerate(late_out, len(late_in)):
            copies.going[id(refs[k])] = (out_refs[n], refs[-1].at[k], False)
            out_refs[n] = refs[k]
            held.append(refs[k])
        body(*in_refs, *out_refs, *own_scratch)
        copies.finish(held)

    in_specs = [SMEM if a.dtype == i32 else VMEM for a in args]
    out_specs = [VMEM] * n_out
    for n in (*late_in, *hbm):
        in_specs[n] = ANY
    for n in late_out:
        out_specs[n] = ANY
    return pl.pallas_call(
        run,
        name=name,
        in_specs=in_specs + [ANY] * extra,
        out_specs=out_specs,
        out_shape=outs,
        scratch_shapes=[*scratch, *buffers, *sems],
        compiler_params=pltpu.CompilerParams(vmem_limit_bytes=mib * MIB),
        cost_estimate=pl.CostEstimate(flops=cost * 10**9, bytes_accessed=0, transcendentals=0),
    )(*args, *after)


def sds(*shape, dtype=f32):
    return jax.ShapeDtypeStruct(shape, dtype)


def mixer_forward(me, tokens, rim, norm_gain, weights, taps, info, doc_rows, rate):
    length, width = tokens[0].shape
    length *= len(tokens)
    w_query, w_key, w_value, w_outgate, w_small = weights
    nh = w_query.shape[1] // 128
    nc, nq = length // CT, nh * 128
    per = (nc, nh)
    outs = dict(
        normed=sds(RIM + length, width, dtype=bf16),
        pre=sds(RIM + length, 5 * nq),
        conv=sds(length, 5 * nq),
        gate=sds(length, nq),
        q=sds(length, nq),
        k=sds(length, 2 * nq),
        v=sds(length, 2 * nq),
        beta=sds(length, 128),
        glog=sds(length, 128),
        gam=sds(length, 128),
        dec=sds(*per, CT, 128),
        t=sds(*per, 128, 128),
        w=sds(*per, 128, 128),
        u=sds(*per, 128, 128),
        reach=sds(*per, CT, 128),
        score=sds(*per, CT, 128),
        at=sds(*per, 128, 128),
        bt=sds(*per, 128, 128),
        info=sds(length + 2 * RIM, 8),
        low=sds(nh, 256, 128, dtype=bf16),
    )
    args = (
        me, *tokens, rim, norm_gain, *late(w_query, w_key, w_value, w_outgate, w_small), *taps, info, doc_rows,
        rate,
    )
    res = kernel_call(
        functools.partial(forward_kernel, nh, len(tokens)), "mixer_forward", args,
        [s if n in ("info", "low") else Late(s) for n, s in outs.items()],
        cost=25, mib=60,
        scratch=[pltpu.VMEM((nh, 256, 128), f32)],
    )
    return dict(zip(outs, res))


def mixer_output(me, maps, fwd, out_gain, w_out, blocks, after=()):
    nc, nh = fwd["w"].shape[:2]
    length = nc * CT
    outs = dict(
        sin=sds(nc + 1, nh, 128, 128),
        fresh=sds(nc, nh, 128, 128),
        core=sds(length, nh * 128),
        gated=sds(length, nh * 128, dtype=bf16),
    )
    parts = [sds(length // blocks, w_out.shape[1], dtype=bf16)] * blocks
    names = ("at", "bt", "w", "reach", "u", "score", "gate")
    args = (me, *maps, *late(*(fwd[n] for n in names)), out_gain, *late(w_out))
    res = kernel_call(
        functools.partial(output_kernel, nh, len(maps), blocks), "mixer_output", args,
        late(*outs.values(), *parts), cost=10, mib=60,
        scratch=[pltpu.VMEM((length, w_out.shape[1]), bf16)],
        after=after,
    )
    return dict(zip(outs, res), branch=res[len(outs) :])


def mixer_adjoint(me, grad, w_out, fwd, out, out_gain, after=()):
    nc, nh = fwd["w"].shape[:2]
    length = nc * CT
    outs = dict(
        dcore=sds(length, nh * 128),
        dt=sds(nc, nh, 128, 128),
        dgate=sds(length, nh * 128, dtype=bf16),
        dgain=sds(1, nh * 128),
        local=sds(nh, 128, 128, dtype=bf16),
    )
    args = (
        me, *grad, w_out, out["core"], fwd["gate"], out_gain,
        *(fwd[n] for n in ("score", "reach", "w", "at")),
    )
    res = kernel_call(
        functools.partial(adjoint_kernel, nh, len(grad)), "mixer_adjoint", args,
        [s if n in ("dgain", "local") else Late(s) for n, s in outs.items()],
        cost=10, mib=24,
        scratch=[pltpu.VMEM((length, nh * 128), f32), pltpu.VMEM((length, w_out.shape[1]), bf16)],
        after=after,
    )
    return dict(zip(outs, res))


def mixer_backward(
    place, maps, local_sums, fwd, out, adj, taps, rate, weights, gain, mlp, grad, after=()
):
    nc, nh = fwd["w"].shape[:2]
    length, nq = nc * CT, nh * 128
    width = 5 * nq
    model = gain.shape[1]
    blocks = len(grad)
    parts = [sds(RIM + length // blocks, model, dtype=bf16)] * blocks
    columns = width + 128 + 2 * nq
    halves = [sds(model // 2 + 16, columns, dtype=bf16)] * 2
    args = (
        *maps, *local_sums, place,
        *late(
            fwd["at"], adj["dt"], fwd["score"], adj["dcore"], fwd["t"], out["fresh"], out["sin"],
            *(fwd[n] for n in ("q", "k", "v")),
        ),
        fwd["beta"], fwd["gam"], *late(fwd["dec"], fwd["conv"], fwd["pre"]), fwd["info"], *taps, rate,
        *late(fwd["glog"], adj["dgate"], *weights, fwd["normed"]), gain, mlp, adj["dgain"],
        *late(out["gated"], *grad),
    )
    *res, own, given = kernel_call(
        functools.partial(backward_kernel, nh, len(maps), blocks), "mixer_backward", args,
        late(*parts, *halves), cost=300, mib=60,
        scratch=[
            pltpu.VMEM((RIM + length, width + 128 + nq), bf16), pltpu.VMEM((4, width), f32),
            pltpu.VMEM((1, 128), f32),
            pltpu.VMEM((length + 2 * RIM, width), f32), pltpu.VMEM((length, 128), f32),
            pltpu.VMEM((nc, nh, 128, 128), f32), pltpu.VMEM((RIM + length, model), bf16),
            pltpu.VMEM((model, RIM + length), bf16), pltpu.VMEM((model, length), bf16),
            pltpu.VMEM((8, columns), f32),
        ],
        after=after,
    )
    return res, (own, given)


def token_info(doc_ids):
    ids = doc_ids.astype(f32)
    length = ids.shape[0]
    extended = jnp.concatenate([ids[:3], ids])
    masks = [(extended[3 - m : 3 - m + length] == ids).astype(f32) for m in range(4)]
    blocks = ids.reshape(-1, CT)
    last = blocks[:, -1:]
    previous = jnp.concatenate([blocks[:1, :1], last[:-1]], 0)
    columns = masks + [
        (blocks == previous).astype(f32).reshape(-1),
        (blocks == last).astype(f32).reshape(-1),
        ids,
        jnp.zeros_like(ids),
    ]
    info = jnp.pad(jnp.stack(columns, 1), ((RIM, RIM), (0, 0)))
    return info, blocks[:, None, :]


def middle_kernel(count, tok_ref, *refs):
    parts, (gain_ref, middle_ref, normed_ref) = refs[:count], refs[count:]
    middle = tok_ref[...].astype(f32)
    total = parts[0][...].astype(f32)
    for part in parts[1:]:
        total = total + part[...].astype(f32)
    middle = middle + total
    middle_ref[...] = middle
    scale = lax.rsqrt(jnp.mean(middle * middle, -1, keepdims=True) + EPS)
    normed_ref[...] = (middle * scale * gain_ref[...]).astype(bf16)


def feed_kernel(hidden, place_ref, *refs):
    x_refs, cot_refs, weights, refs = refs[:2], refs[2:4], refs[4:7], refs[-9:]
    norm_refs, block_refs, cols_ref, refs = refs[:2], refs[2:4], refs[4], refs[5:]
    gate_w, up_w, down_w, sems = refs
    width = gate_w.shape[1]
    each = x_refs[0].shape[0]
    window = pl.ds(pl.multiple_of(place_ref[3], 128), width)
    moves = [
        pltpu.make_async_copy(weights[0].at[:, window], gate_w, sems.at[0]),
        pltpu.make_async_copy(weights[1].at[:, window], up_w, sems.at[1]),
        pltpu.make_async_copy(weights[2].at[window, :], down_w, sems.at[2]),
    ]
    for move in moves:
        move.start()
    lane = iota2((1, width), 1) - place_ref[4]
    mask = ((lane >= 0) & (lane < hidden)).astype(f32)
    x = jnp.concatenate([ref[...] for ref in x_refs], 0)
    cot = jnp.concatenate([ref[...] for ref in cot_refs], 0)
    moves[0].wait()
    gate = mm(x, gate_w[...])
    moves[1].wait()
    up = mm(x, up_w[...]) * mask
    sig = jax.nn.sigmoid(gate)
    silu = gate * sig * mask
    act = (silu * up).astype(bf16)
    moves[2].wait()
    grad = mm(cot, down_w[...], NT)
    ggate = (grad * up * sig * (1.0 + gate * (1.0 - sig))).astype(bf16)
    gup = (grad * silu).astype(bf16)
    gnorm = (mm(ggate, gate_w[...], NT) + mm(gup, up_w[...], NT)).astype(bf16)
    block = mm(act, down_w[...]).astype(bf16)
    for n in range(2):
        half = slice(n * each, (n + 1) * each)
        norm_refs[n][...] = gnorm[half]
        block_refs[n][...] = block[half]
    for n, value in enumerate((ggate, gup, act)):
        cols_ref[n] = value


def with_bit(index, position, bit):
    low = index & ((1 << position) - 1)
    return ((index >> position) << (position + 1)) + bit * (1 << position) + low


def seq_bit(place_ref, bit):
    return lax.rem(lax.div(place_ref[2], 1 << bit), 2)


def feed_grads_kernel(bits, place_ref, *refs):
    x_refs, cot_refs, cols_refs, refs = refs[:4], refs[4:8], refs[8:10], refs[10:]
    out_refs, (turned_ref, full_ref) = refs[:-2], refs[-2:]
    each = x_refs[0].shape[0]
    half = full_ref.shape[0]
    rows = half >> bits
    for n, blocks in enumerate((x_refs, cot_refs)):
        for p, ref in enumerate(blocks):
            turned_ref[n, :, p * each : (p + 1) * each] = jnp.transpose(ref[...])
    for k in range(3):
        for b in range(2):
            left = turned_ref[k // 2, b * half : (b + 1) * half, :]
            if not (k or b):
                copies.need(*cols_refs)
            full_ref[...] = (
                mm(left[:, : 2 * each], cols_refs[0][k]) + mm(left[:, 2 * each :], cols_refs[1][k])
            ).astype(bf16)
            position = (bits - 1) * b
            mine = seq_bit(place_ref, position)
            for n, bit in enumerate((mine, 1 - mine)):
                out_ref = out_refs[2 * b + n]
                for i in range(1 << (bits - 1)):
                    at = with_bit(i, position, bit) * rows
                    first = (k * (1 << (bits - 1)) + i) * rows
                    out_ref[first : first + rows, :] = full_ref[
                        pl.ds(pl.multiple_of(at, rows), rows), :
                    ]


def feed_seq_kernel(bits, left, place_ref, *refs):
    in_refs, out_refs, (sum_ref,) = refs[:4], refs[4:8], refs[8:]
    for b in range(2):
        sum_ref[...] = in_refs[2 * b][...].astype(f32) + in_refs[2 * b + 1][...].astype(f32)
        rows = sum_ref.shape[0] // (3 << left)
        position = (left - 1) * b
        mine = seq_bit(place_ref, bits - left if b == 0 else left - 1)
        for n, bit in enumerate((mine, 1 - mine)):
            out_ref = out_refs[2 * b + n]
            for k in range(3):
                for i in range(1 << (left - 1)):
                    at = ((k << left) + with_bit(i, position, bit)) * rows
                    first = ((k << (left - 1)) + i) * rows
                    out_ref[first : first + rows, :] = sum_ref[
                        pl.ds(pl.multiple_of(at, rows), rows), :
                    ].astype(bf16)


def feed_head_kernel(pairs, place_ref, *refs):
    in_refs, out_refs, (sum_ref,) = refs[:4], refs[4:-1], refs[-1:]
    size = in_refs[0].shape[0]
    for b in range(2):
        sum_ref[b * size : (b + 1) * size, :] = in_refs[2 * b][...].astype(f32) + in_refs[
            2 * b + 1
        ][...].astype(f32)
    rows = out_refs[0].shape[0] // 6
    for shift, out_ref in enumerate(out_refs):
        at = lax.rem(lax.div(place_ref[0], 2) + shift, pairs) * rows
        for n in range(6):
            piece = sum_ref[pl.ds(pl.multiple_of(at + n * rows * pairs, rows), rows), :]
            out_ref[n * rows : (n + 1) * rows, :] = piece.astype(bf16)


def feed_pair_kernel(count, place_ref, *refs):
    parts, out_refs, (sum_ref,) = refs[:count], refs[count:-1], refs[-1:]
    sum_ref[...] = add_up([part[...] for part in parts])
    rows = out_refs[0].shape[0] // 6
    for other, out_ref in enumerate(out_refs):
        odd = lax.rem(place_ref[0] + other, 2) == 1
        for n in range(2):
            core = lax.rem(place_ref[1] + n, 2)
            for k in range(3):
                both = sum_ref[pl.ds(pl.multiple_of((core * 3 + k) * 2 * rows, 2 * rows), 2 * rows), :]
                first = (n * 3 + k) * rows
                value = jnp.where(odd, both[rows:], both[:rows])
                out_ref[first : first + rows, :] = value.astype(bf16)


def feed_out_kernel(hidden, place_ref, *refs):
    parts, (gate_ref, up_ref, down_ref) = refs[:4], refs[4:]
    rows = parts[0].shape[0] // 6
    own = lax.rem(place_ref[0], 2) * 2 + place_ref[1]
    for k, out_ref in enumerate((gate_ref, up_ref, down_ref)):
        values = [
            part[(n % 2 * 3 + k) * rows : (n % 2 * 3 + k + 1) * rows, :].astype(f32)
            for n, part in enumerate(parts)
        ]
        for g in range(4):
            value = values[0]
            for n in range(1, 4):
                value = jnp.where(own == (g ^ n), values[n], value)
            start = g * hidden % 128
            value = value[:, start : start + hidden]
            out_ref[:, g * hidden : (g + 1) * hidden] = value


def mixer_blocks_kernel(place_ref, own_ref, got_ref, *out_refs):
    count = len(out_refs)
    half = own_ref.shape[0] - 16
    rows = half // count
    small = two_parts(joined_parts(own_ref, half, 8) + joined_parts(got_ref, half, 8))
    for shift, out_ref in enumerate(out_refs):
        at = pl.ds(pl.multiple_of(lax.rem(place_ref[2] + shift, count) * rows, 16), rows)
        out_ref[0:rows, :] = (own_ref[at, :].astype(f32) + got_ref[at, :].astype(f32)).astype(bf16)
        out_ref[rows:, :] = small
        copies.done(out_ref)


def joined_parts(ref, start, extra):
    both = ref[start : start + 2 * extra, :].astype(f32)
    return both[:extra] + both[extra:]


def mixer_sum_kernel(count, nh, *refs):
    parts, out_refs = refs[:count], refs[count:]
    weight_refs, conv_refs, (decay_ref, gain_ref) = out_refs[:7], out_refs[7:10], out_refs[10:]
    rows = weight_refs[0].shape[0]
    nq = nh * 128
    starts = (0, nq, 3 * nq, 5 * nq, 5 * nq + 2 * nh, 5 * nq + 128, 6 * nq + 128)
    for n, (start, out_ref) in enumerate(zip(starts, weight_refs)):
        turned = n in (3, 4, 6)
        width = out_ref.shape[0] if turned else out_ref.shape[1]
        total = add_up([part[0:rows, start : start + width] for part in parts])
        out_ref[...] = jnp.transpose(total) if turned else total
    small = add_up([joined_parts(part, rows, 8) for part in parts])
    for start, out_ref in zip(starts, conv_refs):
        out_ref[...] = small[0:4, start : start + out_ref.shape[1]]
    decay_ref[...] = small[4:5, 2 * nh : 3 * nh]
    gain_ref[...] = small[4:5, 128 : 128 + nq]


def norm_back(grad_normed, rows, gain):
    scale = lax.rsqrt(jnp.mean(rows * rows, -1, keepdims=True) + EPS)
    unit = rows * scale
    scaled = grad_normed * gain
    grad_rows = scale * (scaled - unit * jnp.mean(scaled * unit, -1, keepdims=True))
    return grad_rows, jnp.sum(grad_normed * unit, 0, keepdims=True)


def middle_back_kernel(a_ref, b_ref, c_ref, middle_ref, cot_ref, gain_ref, grad_ref, low_ref, sum_ref):
    total = a_ref[...].astype(f32) + b_ref[...].astype(f32) + c_ref[...].astype(f32)
    rows, sum_ref[...] = norm_back(total, middle_ref[...], gain_ref[...])
    grad = cot_ref[...].astype(f32) + rows
    grad_ref[...] = grad
    low_ref[...] = grad.astype(bf16)


def extra_rows_kernel(count, *refs):
    parts, (rim_ref, gains_ref) = refs[:count], refs[count:]
    each = parts[0].shape[0] - RIM
    total = add_up([part[each:, :] for part in parts])
    row = iota2((RIM, 1), 0)
    rim_ref[...] = jnp.where(row >= RIM - 3, total, 0.0).astype(bf16)
    gains_ref[...] = jnp.zeros(gains_ref.shape, f32)
    for n in range(2):
        gains_ref[n : n + 1, :] = total[2 * n : 2 * n + 1] + total[2 * n + 1 : 2 * n + 2]


def tokens_back_kernel(count, *refs):
    parts, (rim_ref, tok_ref, gain_ref, middle_ref, grad_ref) = refs[:count], refs[count:]
    each = tok_ref.shape[0]
    total = add_up([part[0:each, :] for part in parts])
    rim = rim_ref[...].astype(f32)
    total = total + jnp.concatenate([jnp.zeros((each - RIM, rim.shape[1]), f32), rim], 0)
    rows, _ = norm_back(total, tok_ref[...].astype(f32), gain_ref[...])
    grad_ref[...] = middle_ref[...] + rows


HEAD = ("pair", "half")


def axis_size(axis):
    return lax.axis_size(axis) if isinstance(axis, str) else lax.psum(1, axis)


def ring(value, axis):
    count = axis_size(axis)
    return [value] + [
        lax.ppermute(value, axis, [(i, (i + shift) % count) for i in range(count)])
        for shift in range(1, count)
    ]


def along(value, axis, shift):
    count = axis_size(axis)
    pairs = [(i, i + shift) for i in range(count) if 0 <= i + shift < count]
    return lax.ppermute(value, axis, pairs)


def crossed(value, axis, bit=0):
    return lax.ppermute(value, axis, [(i, i ^ (1 << bit)) for i in range(axis_size(axis))])


def spread(blocks, axis):
    count = axis_size(axis)
    return [blocks[0]] + [
        lax.ppermute(blocks[shift], axis, [(i, (i + shift) % count) for i in range(count)])
        for shift in range(1, count)
    ]


def add_up(parts):
    total = parts[0].astype(f32)
    for part in parts[1:]:
        total = total + part.astype(f32)
    return total


def sum_over(value, axis):
    return add_up(ring(value, axis))


def tied(*values):
    return lax.optimization_barrier(values)


def on_device(
    tokens, doc_ids, norm_gain, w_query, w_key, w_value, w_beta, w_decay, w_outgate, conv_query,
    conv_key, conv_value, decay_log, out_gain, w_out, mlp_gain, w_gate, w_up, w_down, cotangent,
):
    head_n, seq_n, batch_n = (axis_size(a) for a in (HEAD, "seq", "batch"))
    me = lax.axis_index(HEAD)
    nh = w_decay.shape[1]
    nq = nh * 128
    each, model = tokens.shape
    length = each * head_n
    me_array = me.astype(i32).reshape(1)

    head_last = head_n - 1
    blocks = ring(tokens, HEAD)
    seq_place = lax.axis_index("seq")
    core = lax.axis_index("batch")
    ways = 2 * batch_n
    hidden = w_gate.shape[1] // ways
    mine = ((me & 1) * batch_n + core) * hidden
    place = jnp.stack([me, core, seq_place, mine // 128 * 128, mine % 128]).astype(i32)
    window = -(-(hidden + 64) // 128) * 128
    ids = jnp.broadcast_to(doc_ids[-RIM:, None], (RIM, 128)).astype(bf16)
    tail = tied(jnp.concatenate([tokens[-RIM:], ids], 1), blocks[-1])[0]
    rim = add_up(
        [
            lax.ppermute(
                tail,
                ("seq", *HEAD),
                [(s * head_n + head_last, (s + 1) * head_n + h) for s in range(seq_n - 1)],
            )
            for h in range(head_n)
        ]
    ).astype(bf16)
    info, doc_rows = token_info(doc_ids)
    w_small = jnp.pad(jnp.concatenate([w_beta, w_decay], 1), ((0, 0), (0, 128 - 3 * nh)))
    rate = jnp.pad(-jnp.exp(decay_log), (2 * nh, 128 - 3 * nh))[None]
    weights = (w_query, w_key, w_value, w_outgate, w_small)
    taps = (conv_query, conv_key, conv_value)
    gain = norm_gain[None]
    fwd = mixer_forward(me_array, blocks, rim, gain, weights, taps, info, doc_rows, rate)

    states = ring(fwd["low"], "seq")
    cot_sent = tied(cotangent, fwd["low"])[0]
    cot_near = crossed(cot_sent, HEAD)
    cots = [cotangent, cot_near, *[crossed(value, "batch") for value in (cot_sent, cot_near)]]
    out = mixer_output(place, states[1:], fwd, out_gain[None], w_out, head_n)

    low = lambda *shape: sds(*shape, dtype=bf16)
    parts = spread(out["branch"], HEAD)
    middle, normed_mid = kernel_call(
        functools.partial(middle_kernel, len(parts)), "middle",
        (tokens, *parts, mlp_gain[None]), [sds(each, model), low(each, model)],
        after=cots[1:],
    )
    near = crossed(normed_mid, HEAD)

    def feed(rows, cots, after=()):
        return pl.pallas_call(
            functools.partial(feed_kernel, hidden),
            name="feed",
            in_specs=[SMEM] + [VMEM] * 4 + [ANY] * (3 + len(after)),
            out_specs=[VMEM] * 5,
            out_shape=[low(each, model)] * 4 + [low(3, 2 * each, window)],
            scratch_shapes=[
                pltpu.VMEM((model, window), bf16), pltpu.VMEM((model, window), bf16),
                pltpu.VMEM((window, model), bf16), pltpu.SemaphoreType.DMA((3,)),
            ],
            compiler_params=pltpu.CompilerParams(vmem_limit_bytes=40 * MIB),
            cost_estimate=pl.CostEstimate(flops=5 * 10**9, bytes_accessed=0, transcendentals=0),
        )(place, *rows, *cots, w_gate, w_up, w_down, *after)

    rows = [normed_mid, crossed(normed_mid, "batch")]
    cots = [cots[0], cots[2], cots[1], cots[3]]
    first = feed(rows, cots[:2])
    near_sent = tied(near, first[0])[0]
    rows += [near, crossed(near_sent, "batch")]
    second = feed(rows[2:], cots[2:], after=first[:1])
    fed = [first[0], second[0], first[1], second[1], first[2], second[2], first[3], second[3]]
    fed += [first[4], second[4]]

    def own_parts(blocks):
        given = (blocks[1].astype(f32) + crossed(blocks[3], "batch").astype(f32)).astype(bf16)
        return given, (blocks[0], crossed(blocks[2], "batch"), crossed(given, HEAD))

    given, norm_parts = own_parts(fed[:4])
    block_own = crossed(fed[6], "batch")
    block_given = (fed[5].astype(f32) + crossed(fed[7], "batch").astype(f32)).astype(bf16)

    seq_rows = model // (batch_n * seq_n)
    seq_bits = seq_n.bit_length() - 1
    size = 3 * model // 4
    feed_kept = kernel_call(
        functools.partial(feed_grads_kernel, seq_bits), "feed_grads",
        (place, *rows, *cots, *late(*fed[8:])), late(*[low(size, window)] * 4),
        scratch=[
            pltpu.VMEM((2, model, 4 * each), bf16), pltpu.VMEM((model // 2, window), bf16),
        ],
        after=[given],
    )

    def exchanged(values, step):
        bits = (step, seq_bits - 1 - step)
        return [
            value
            for b in range(2)
            for value in (values[2 * b], crossed(values[2 * b + 1], "seq", bits[b]))
        ]

    grad_middle, grad_branch, grad_mlp_gain = kernel_call(
        middle_back_kernel, "middle_back",
        (*norm_parts, middle, cotangent, mlp_gain[None]),
        [sds(each, model), low(each, model), sds(1, model)],
        after=feed_kept[1::2], cost=100,
    )
    feed_grads = exchanged(feed_kept, 0)
    grad_blocks = ring(grad_branch, HEAD)

    for step in range(1, seq_bits):
        size //= 2
        feed_kept = kernel_call(
            functools.partial(feed_seq_kernel, seq_bits, seq_bits - step), "feed_seq",
            (place, *feed_grads), late(*[low(size, window)] * 4),
            scratch=[pltpu.VMEM((2 * size, window), f32)],
            after=grad_blocks[1:2],
        )
        feed_grads = exchanged(feed_kept, step)
    adj = mixer_adjoint(
        me_array, grad_blocks, w_out, fwd, out, out_gain[None],
        after=[block_given, block_own, feed_kept[1]],
    )
    later = [along(adj["local"], "seq", -s) for s in range(seq_n - 1, 0, -1)]

    own_rows = model // (batch_n * seq_n * head_n)
    seq_rows = own_rows * head_n
    pairs = head_n // 2
    feed_kept = kernel_call(
        functools.partial(feed_head_kernel, pairs), "feed_head", (place, *feed_grads),
        late(*[low(12 * own_rows, window)] * pairs),
        scratch=[pltpu.VMEM((6 * seq_rows, window), f32)],
        after=[adj["local"]],
    )
    normed_parts, wide = mixer_backward(
        place, states[1:], later, fwd, out, adj, taps, rate,
        (w_query, w_key, w_value, w_small, w_outgate), gain, grad_mlp_gain, grad_blocks,
        after=[feed_kept[-1]],
    )
    feed_grads = [feed_kept[0]] + [
        lax.ppermute(
            feed_kept[shift], HEAD, [(i, (i + 2 * shift) % head_n) for i in range(head_n)]
        )
        for shift in range(1, pairs)
    ]
    block_given = crossed(tied(feed_kept[0], block_given)[1], HEAD)
    block_out = (middle + add_up([fed[4], block_own, block_given])).astype(bf16)
    normed_parts = spread(normed_parts, HEAD)

    columns = wide[0].shape[1]
    wide_blocks = kernel_call(
        mixer_blocks_kernel, "mixer_blocks",
        (place, wide[0], crossed(tied(wide[1], block_given, *feed_grads[1:])[0], "batch")),
        late(*[low(seq_rows + 16, columns)] * seq_n),
    )
    wide_parts = spread(wide_blocks, "seq")
    extra, gains = kernel_call(
        functools.partial(extra_rows_kernel, head_n), "extra_rows", normed_parts,
        [low(RIM, model), sds(8, model)],
        after=wide_parts[1:2],
    )
    gains = add_up([gains, crossed(gains, "batch")])
    gain_parts = ring(gains, "seq")
    rim_part = lax.ppermute(
        extra,
        ("seq", *HEAD),
        [(s * head_n + head_last, (s - 1) * head_n + head_last) for s in range(1, seq_n)],
    )
    group_own, group_sent = kernel_call(
        functools.partial(feed_pair_kernel, pairs), "feed_pair", (place, *feed_grads),
        [low(6 * own_rows, window)] * 2,
        scratch=[pltpu.VMEM((12 * own_rows, window), f32)],
        after=[extra],
    )
    group_got = crossed(group_sent, HEAD)
    group = [group_own, crossed(group_own, "batch"), group_got, crossed(group_got, "batch")]
    grad_gate, grad_up, grad_down = kernel_call(
        functools.partial(feed_out_kernel, hidden), "feed_out", (place, *group),
        [sds(own_rows, ways * hidden)] * 3,
    )
    (grad_tokens,) = kernel_call(
        functools.partial(tokens_back_kernel, head_n), "tokens_back",
        (*normed_parts, rim_part, tokens, gain, grad_middle),
        [sds(each, model)],
    )
    *sums, grad_decay, grad_out_gain = kernel_call(
        functools.partial(mixer_sum_kernel, seq_n, nh), "mixer_sum", wide_parts,
        [sds(seq_rows, w) for w in (nq, 2 * nq, 2 * nq)] + [sds(w, seq_rows) for w in (2 * nh, nh)]
        + [sds(seq_rows, nq), sds(nq, seq_rows)]
        + [sds(4, w) for w in (nq, 2 * nq, 2 * nq)] + [sds(1, nh), sds(1, nq)],
    )
    grad_q, grad_k, grad_v, grad_b, grad_d, grad_g, grad_out, *grad_convs = sums
    gains = add_up(gain_parts)
    index = (core * seq_n + seq_place) * head_n + me
    gains = lax.dynamic_slice_in_dim(gains, index * own_rows, own_rows, 1)
    return (
        block_out, grad_tokens, gains[0], grad_q, grad_k, grad_v, grad_b.T, grad_d.T, grad_g,
        *grad_convs, grad_decay[0], grad_out_gain[0], grad_out, gains[1], grad_gate, grad_up,
        grad_down.T,
    )


def solution(mesh):
    batch, seq, head = mesh.devices.shape
    split_mesh = Mesh(mesh.devices.reshape(batch, seq, head // 2, 2), ("batch", "seq", *HEAD))
    return jax.shard_map(
        on_device,
        mesh=split_mesh,
        in_specs=(
            P(("batch", "seq", *HEAD), None),
            P(("batch", "seq")),
            P(),
            P(None, HEAD),
            P(None, HEAD),
            P(None, HEAD),
            P(None, HEAD),
            P(None, HEAD),
            P(None, HEAD),
            P(None, HEAD),
            P(None, HEAD),
            P(None, HEAD),
            P(HEAD),
            P(HEAD),
            P(HEAD, None),
            P(),
            P(),
            P(),
            P(),
            P(("batch", "seq", *HEAD), None),
        ),
        out_specs=(
            P(("batch", "seq", *HEAD), None),
            P(("batch", "seq", *HEAD), None),
            P(("batch", "seq", *HEAD)),
            P(("batch", "seq"), HEAD),
            P(("batch", "seq"), HEAD),
            P(("batch", "seq"), HEAD),
            P(("batch", "seq"), HEAD),
            P(("batch", "seq"), HEAD),
            P(("batch", "seq"), HEAD),
            P(None, HEAD),
            P(None, HEAD),
            P(None, HEAD),
            P(HEAD),
            P(HEAD),
            P(HEAD, ("batch", "seq")),
            P(("batch", "seq", *HEAD)),
            P(("batch", "seq", *HEAD), None),
            P(("batch", "seq", *HEAD), None),
            P(None, ("batch", "seq", *HEAD)),
        ),
        check_vma=False,
    )
```

```python
import functools

import jax
import jax.numpy as jnp
from jax import lax
from jax.experimental import pallas as pl
from jax.experimental.pallas import tpu as pltpu
from jax.sharding import Mesh
from jax.sharding import PartitionSpec as P

bf16, f32, i32 = jnp.bfloat16, jnp.float32, jnp.int32
EPS = 1e-06
CT = 64
RIM = 16
NN = ((1,), (0,))
NT = ((1,), (1,))
MIB = 1 << 20
FORWARD, OUTPUT, ADJOINT, BACKWARD = 4, 4, 8, 8


def mm(a, b, dims=NN):
    return lax.dot_general(a, b, (dims, ((), ())), preferred_element_type=f32)


def split(x):
    high = x.astype(bf16)
    return high, (x - high.astype(f32)).astype(bf16)


def mm3(a, b, dims=NN):
    return mm(a[0], b[0], dims) + (mm(a[0], b[1], dims) + mm(a[1], b[0], dims))


def mm3_deep(a, b, dims=NN):
    if a[0].shape[1] % 128:
        return mm3(a, b, dims)
    left = jnp.concatenate([a[0], a[1]], 1)
    right = jnp.concatenate([b[0], b[0]], 1 if dims == NT else 0)
    return mm(left, right, dims) + mm(a[0], b[1], dims)


def exact(a, b):
    return lax.dot_general(
        a, b, (NN, ((), ())), precision=lax.Precision.HIGHEST, preferred_element_type=f32
    )


def iota2(shape, dim):
    return lax.broadcasted_iota(i32, shape, dim)


def rows_of(c, size=CT, start=0):
    return pl.ds(pl.multiple_of(c * size + start, 16), size)


def near(c, start):
    return pl.ds(pl.multiple_of(c * CT + start, 8), CT + 8)


def step_order():
    size = 2 * CT
    row, col = iota2((size, size), 0), iota2((size, size), 1)
    row_tok, col_tok = row & (CT - 1), col & (CT - 1)
    later = jnp.where(row_tok > col_tok, row_tok ^ col_tok, 0)
    same_token = (row_tok == col_tok) & (row >= CT) & (col < CT)
    return row, col, later, same_token


def twice(x):
    return jnp.concatenate([x, x], 0)


def head_steps(ref, rows, h):
    return jnp.concatenate(
        [ref[rows, (2 * h + j) * 128 : (2 * h + j + 1) * 128] for j in range(2)], 0
    )


def decays(gam_ref, info, rows, h, nh):
    gcol = gam_ref[rows, 2 * nh + h : 2 * nh + h + 1]
    glast = gcol[CT - 1 : CT, :]
    carried = jnp.exp(gcol) * info[:, 4:5]
    tail = jnp.exp(jnp.minimum(glast - gcol, 0.0)) * info[:, 5:6]
    keep = carried[CT - 1 : CT, :]
    return gcol, carried, tail, keep


def forward_kernel(
    nh, count, me_ref, *refs
):
    tok_refs, refs = refs[:count], refs[count:]
    forward_body(nh, me_ref, tok_refs, *refs)


def forward_body(
    nh, me_ref, tok_refs, rim_ref, ng_ref, wq_ref, wk_ref, wv_ref, wg_ref, ws_ref, tq_ref, tk_ref, tv_ref,
    flags_ref, drow_ref, rate_ref,
    normed_ref, pre_ref, conv_ref, gate_ref, q_ref, k_ref, v_ref, beta_ref, glog_ref, gam_ref, dec_ref,
    t_ref, w_ref, u_ref, reach_ref, score_ref, at_ref, bt_ref, info_ref, low_ref, st_ref,
):
    length = pre_ref.shape[0] - RIM
    nc = length // CT
    gain = ng_ref[...]
    count = len(tok_refs)
    each = tok_refs[0].shape[0]

    def normal(x):
        x = x.astype(f32)
        scale = lax.rsqrt(jnp.mean(x * x, -1, keepdims=True) + EPS)
        return (x * scale * gain).astype(bf16)

    model = ng_ref.shape[1]
    normed_ref[0:RIM, :] = normal(rim_ref[:, :model])
    info_ref[...] = flags_ref[...]
    first = flags_ref[RIM : RIM + 8, :]
    ids = jnp.concatenate([rim_ref[8:, model : model + 8].astype(f32), first[:, 6:7] + jnp.zeros((8, 8), f32)], 0)
    row, col = iota2((8, 8), 0), iota2((8, 8), 1)
    for m in range(1, 4):
        same = (pltpu.roll(ids, m, 0)[8:] == ids[8:]).astype(f32)
        first = jnp.where((col == m) & (row < m), same, first)
    info_ref[RIM : RIM + 8, :] = first

    for shift, tok_ref in enumerate(tok_refs):
        place = lax.rem(me_ref[0] + (count - shift), count) * each

        def norm_rows(c, carry):
            target = pl.ds(pl.multiple_of(place + c * CT + RIM, 16), CT)
            normed_ref[target, :] = normal(tok_ref[rows_of(c), :])
            return carry

        lax.fori_loop(0, each // CT, norm_rows, 0)
    copies.done(normed_ref)
    copies.need(wq_ref, wk_ref, wv_ref, wg_ref, ws_ref)
    nq = nh * 128
    groups = ((wq_ref, 0, nq), (wk_ref, nq, 2 * nq), (wv_ref, 3 * nq, 2 * nq))

    for weight, first, width in groups:
        pre_ref[0:RIM, first : first + width] = (
            mm(normed_ref[0:RIM, :], weight[...]).astype(bf16).astype(f32)
        )

    def project(i, carry):
        rows = rows_of(i, 256, RIM)
        block = normed_ref[rows, :]
        for weight, first, width in groups:
            pre_ref[rows, first : first + width] = mm(block, weight[...]).astype(bf16).astype(f32)
        plain = rows_of(i, 256)
        gate_ref[plain, :] = mm(block, wg_ref[...])
        glog_ref[plain, :] = mm(block, ws_ref[...])
        return carry

    lax.fori_loop(0, length // 256, project, 0)
    copies.done(pre_ref, gate_ref)
    logits = glog_ref[...]
    beta_ref[...] = jax.nn.sigmoid(logits)
    soft = jnp.maximum(logits, 0.0) + jnp.log1p(jnp.exp(-jnp.abs(logits)))
    glog = rate_ref[...] * soft
    glog_ref[...] = glog
    tri = (iota2((CT, CT), 0) >= iota2((CT, CT), 1)).astype(f32)
    for c in range(nc):
        gam_ref[c * CT : (c + 1) * CT, :] = exact(tri, glog[c * CT : (c + 1) * CT, :])

    def conv_rows(c, carry):
        rows = rows_of(c)
        info = info_ref[rows_of(c, CT, RIM), :]
        mask = [info[:, m : m + 1] for m in range(4)]
        for tap_ref, first, count, kind in (
            (tq_ref, 0, nh, "q"), (tk_ref, nq, 2 * nh, "k"), (tv_ref, 3 * nq, 2 * nh, "v")
        ):
            for j in range(count):
                cols = slice(first + j * 128, first + (j + 1) * 128)
                mine = slice(j * 128, (j + 1) * 128)
                taps = tap_ref[:, mine].astype(f32)
                block = pre_ref[near(c, RIM - 8), cols]
                total = block[8:] * taps[0:1]
                for m in range(1, 4):
                    total = total + pltpu.roll(block, m, 0)[8:] * mask[m] * taps[m : m + 1]
                conv_ref[rows, cols] = total
                out = total * jax.nn.sigmoid(total)
                if kind == "k":
                    out = out * lax.rsqrt(jnp.sum(out * out, -1, keepdims=True) + EPS)
                {"q": q_ref, "k": k_ref, "v": v_ref}[kind][rows, mine] = out
        return carry

    lax.fori_loop(0, nc, conv_rows, 0)
    copies.done(conv_ref, q_ref, k_ref, v_ref, beta_ref, glog_ref, gam_ref)

    row, col, later, same_token = step_order()
    eye = (row == col).astype(f32)
    small_row, small_col = iota2((CT, CT), 0), iota2((CT, CT), 1)

    def prepare(group, carry):
        items = [(group * FORWARD + i, h) for i in range(FORWARD) for h in range(nh)]
        systems, rhs, tails, keeps = [], [], [], []
        for c, h in items:
            rows = rows_of(c)
            info = info_ref[rows_of(c, CT, RIM), :]
            same = (info[:, 6:7] == drow_ref[c]) & (small_row >= small_col)
            gcol, carried, tail, keep = decays(gam_ref, info, rows, h, nh)
            grow = jnp.sum(jnp.where(small_row == small_col, gcol, 0.0), 0, keepdims=True)
            decay = jnp.where(same, jnp.exp(jnp.minimum(gcol - grow, 0.0)), 0.0)
            wide = jnp.concatenate([decay, decay], 1)
            dec_ref[c, h] = wide
            key = head_steps(k_ref, rows, h)
            value = head_steps(v_ref, rows, h)
            beta = jnp.concatenate(
                [beta_ref[rows, 2 * h + j : 2 * h + j + 1] for j in range(2)], 0
            )
            key2 = split(key)
            query = q_ref[rows, h * 128 : (h + 1) * 128]
            query2 = split(query)
            pairs = mm3([jnp.concatenate(x, 0) for x in zip(key2, query2)], key2, NT)
            score_ref[c, h] = pairs[2 * CT :] * wide
            reach_ref[c, h] = query * carried
            systems.append(
                jnp.where((later > 0) | same_token, beta * pairs[: 2 * CT] * twice(wide), 0.0)
            )
            rhs.append(jnp.concatenate([beta * twice(carried) * key, beta * value], 1))
            tails.append(key * twice(tail))
            keeps.append(keep)
        inverse = [eye - jnp.where(same_token, n, 0.0) for n in systems]
        for level in range(6):
            part = (later >> level) == 1
            blocks = [split(jnp.where(part, n, 0.0)) for n in systems]
            inverse2 = [split(x) for x in inverse]
            first = [split(mm3(b, x)) for b, x in zip(blocks, inverse2)]
            inverse = [x - mm3(x2, y) for x, x2, y in zip(inverse, inverse2, first)]
        mixed = [mm3(split(x), split(r)) for x, r in zip(inverse, rhs)]
        products = [mm3(split(jnp.transpose(m)), split(t)) for m, t in zip(mixed, tails)]
        for n, (c, h) in enumerate(items):
            t_ref[c, h] = inverse[n]
            w_ref[c, h] = mixed[n][:, :128]
            u_ref[c, h] = mixed[n][:, 128:]
            at_ref[c, h] = keeps[n] * eye - products[n][:128]
            bt_ref[c, h] = products[n][128:]
        part = pl.ds(group * FORWARD, FORWARD)
        copies.done(dec_ref, score_ref, reach_ref, t_ref, w_ref, u_ref, at_ref, bt_ref, at=part)
        return carry

    lax.fori_loop(0, nc // FORWARD, prepare, 0)

    for h in range(nh):
        st_ref[h, :128] = at_ref[0, h]
        st_ref[h, 128:] = bt_ref[0, h]

    def chain(c, carry):
        for h in range(nh):
            after = mm3(split(st_ref[h]), split(at_ref[c, h]))
            st_ref[h, :128] = after[:128]
            st_ref[h, 128:] = after[128:] + bt_ref[c, h]
        return carry

    lax.fori_loop(1, nc, chain, 0)
    low_ref[...] = st_ref[...].astype(bf16)


def output_kernel(nh, count, blocks, me_ref, *refs):
    output_body(nh, me_ref, refs[:count], *refs[count : -blocks - 1], refs[-blocks - 1 : -1], refs[-1])


def output_body(
    nh, me_ref, map_refs, at_ref, bt_ref, w_ref, reach_ref, u_ref, score_ref, gate_ref, gain_ref, wout_ref,
    sin_ref, fresh_ref, core_ref, gated_ref, branch_refs, all_ref,
):
    nc = w_ref.shape[0]
    states = []
    for h in range(nh):
        state = jnp.zeros((128, 128), f32)
        for distance in range(len(map_refs), 0, -1):
            map_ref = map_refs[distance - 1]
            passed = split(map_ref[h, :128].astype(f32))
            state = mm3(split(state), passed) + map_ref[h, 128:].astype(f32)
            state = jnp.where(me_ref[2] >= distance, state, 0.0)
        states.append(state)

    def chain(c, states):
        out = []
        for h in range(nh):
            sin_ref[c, h] = states[h]
            out.append(mm3(split(states[h]), split(at_ref[c, h])) + bt_ref[c, h])
        return tuple(out)

    copies.need(at_ref, bt_ref)
    states = lax.fori_loop(0, nc, chain, tuple(states))
    for h in range(nh):
        sin_ref[nc, h] = states[h]
    copies.done(sin_ref)
    copies.need(w_ref, reach_ref, u_ref, score_ref, gate_ref)

    def outputs(group, carry):
        for c, h in [(group * OUTPUT + i, h) for i in range(OUTPUT) for h in range(nh)]:
            rows = rows_of(c)
            cols = slice(h * 128, (h + 1) * 128)
            state2 = split(sin_ref[c, h])
            probe = jnp.concatenate([w_ref[c, h], reach_ref[c, h]], 0)
            seen = mm3(split(probe), state2, NT)
            fresh = u_ref[c, h] - seen[: 2 * CT]
            fresh_ref[c, h] = fresh
            core = seen[2 * CT :] + mm3(split(score_ref[c, h]), split(fresh))
            core_ref[rows, cols] = core
            unit = core * lax.rsqrt(jnp.mean(core * core, -1, keepdims=True) + EPS)
            gate = gate_ref[rows, cols]
            gated_ref[rows, cols] = (
                unit * gain_ref[:, cols] * (gate * jax.nn.sigmoid(gate))
            ).astype(bf16)
        copies.done(fresh_ref, at=pl.ds(group * OUTPUT, OUTPUT))
        copies.done(core_ref, gated_ref, at=rows_of(group, OUTPUT * CT))
        return carry

    lax.fori_loop(0, nc // OUTPUT, outputs, 0)
    copies.need(wout_ref)
    all_ref[...] = mm(gated_ref[...], wout_ref[...]).astype(bf16)
    count = len(branch_refs)
    each = branch_refs[0].shape[0]
    for shift, branch_ref in enumerate(branch_refs):
        place = lax.rem(me_ref[0] + shift, count) * each
        branch_ref[...] = all_ref[pl.ds(pl.multiple_of(place, 16), each), :]
        copies.done(branch_ref)


def adjoint_kernel(nh, count, me_ref, *refs):
    adjoint_body(nh, me_ref, refs[:count], *refs[count:])


def adjoint_body(
    nh, me_ref, g_refs, wout_ref, core_ref, gate_ref, gain_ref, score_ref, reach_ref, w_ref, at_ref,
    dcore_ref, dt_ref, dgate_ref, dgain_ref, local_ref, dgated_ref, all_ref,
):
    nc = w_ref.shape[0]
    count = len(g_refs)
    each = g_refs[0].shape[0]
    for shift, g_ref in enumerate(g_refs):
        place = lax.rem(me_ref[0] + (count - shift), count) * each
        all_ref[pl.ds(pl.multiple_of(place, 16), each), :] = g_ref[...]
    copies.need(wout_ref)
    dgated_ref[...] = mm(all_ref[...], wout_ref[...], NT)
    copies.need(core_ref, gate_ref, score_ref, reach_ref, w_ref)

    def chunks(group, dgain):
        for i in range(ADJOINT):
            dgain = dgain + chunk(group * ADJOINT + i)
        copies.done(dt_ref, at=pl.ds(group * ADJOINT, ADJOINT))
        copies.done(dcore_ref, dgate_ref, at=rows_of(group, ADJOINT * CT))
        return dgain

    def chunk(c):
        rows = rows_of(c)
        sums = []
        for h in range(nh):
            cols = slice(h * 128, (h + 1) * 128)
            core = core_ref[rows, cols]
            scale = lax.rsqrt(jnp.mean(core * core, -1, keepdims=True) + EPS)
            unit = core * scale
            gate = gate_ref[rows, cols]
            sig = jax.nn.sigmoid(gate)
            silu = gate * sig
            gain = gain_ref[:, cols]
            grad = dgated_ref[rows, cols]
            sums.append(jnp.sum(grad * unit * silu, 0, keepdims=True))
            dgate_ref[rows, cols] = (
                grad * unit * gain * (sig * (1.0 + gate * (1.0 - sig)))
            ).astype(bf16)
            dunit = grad * gain * silu
            dcore = scale * (dunit - unit * jnp.mean(dunit * unit, -1, keepdims=True))
            dcore_ref[rows, cols] = dcore
            across = jnp.transpose(dcore)
            dft = mm3_deep(split(across), split(score_ref[c, h]))
            left = jnp.concatenate([-dft, across], 1)
            right = jnp.concatenate([w_ref[c, h], reach_ref[c, h]], 0)
            dt_ref[c, h] = mm3_deep(split(left), split(right))
        return jnp.concatenate(sums, 1)

    dgain_ref[...] = lax.fori_loop(0, nc // ADJOINT, chunks, jnp.zeros(dgain_ref.shape, f32))

    copies.need(at_ref)

    def chain(i, carry):
        c = nc - 1 - i
        return tuple(
            mm3_deep(split(carry[h]), split(at_ref[c, h]), NT) + dt_ref[c, h] for h in range(nh)
        )

    start = tuple(dt_ref[nc - 1, h] for h in range(nh))
    total = lax.fori_loop(1, nc, chain, start)
    for h in range(nh):
        local_ref[h] = total[h].astype(bf16)


def normed_back(count, place_ref, gp_ref, weights, normed_ref, gain_ref, mlp_ref, out_refs, all_ref):
    each = out_refs[0].shape[0] - RIM
    length = all_ref.shape[0] - RIM
    total = jnp.zeros(gain_ref.shape, f32)
    for start in range(0, length, 256):
        rows = slice(start + (RIM if start else 0), start + 256 + RIM)
        first = 0
        grad = None
        for weight in weights:
            width = weight.shape[1]
            term = mm(gp_ref[rows, first : first + width], weight[...], NT)
            grad = term if grad is None else grad + term
            first += width
        all_ref[rows, :] = grad.astype(bf16)
        total = total + jnp.sum(grad * normed_ref[rows, :].astype(f32), 0, keepdims=True)
    rim = all_ref[0:RIM, :].astype(f32)
    row = iota2((RIM, 1), 0)
    gains = [*split(total / gain_ref[...]), *split(mlp_ref[...])]
    for n, gain in enumerate(gains):
        rim = jnp.where(row == n, gain.astype(f32), rim)
    rim = rim.astype(bf16)
    for shift, out_ref in enumerate(out_refs):
        place = lax.rem(place_ref[0] + shift, count) * each + RIM
        out_ref[0:each, :] = all_ref[pl.ds(pl.multiple_of(place, 16), each), :]
        out_ref[each:, :] = rim
        copies.done(out_ref)


def turn(left_ref, turned_ref):
    tokens, width = left_ref.shape
    for n in range(width // 128):
        turned_ref[n * 128 : (n + 1) * 128, :tokens] = jnp.transpose(
            left_ref[:, n * 128 : (n + 1) * 128]
        )


def two_halves(place_ref, turned, right, own_ref, given_ref, cols):
    half = turned.shape[0] // 2
    for core, out_ref in ((place_ref[1], own_ref), (1 - place_ref[1], given_ref)):
        rows = pl.ds(pl.multiple_of(core * half, 16), half)
        out_ref[0:half, cols] = mm(turned[rows, : right.shape[0]], right[...]).astype(out_ref.dtype)


def two_parts(value):
    high, low = split(value)
    return jnp.concatenate([high, low], 0)


def backward_kernel(nh, count, blocks, *refs):
    at = 2 * count + 1
    maps, local_sums, place, refs = refs[:count], refs[count : at - 1], refs[at - 1], refs[at:]
    inputs, refs = refs[:21], refs[21:]
    dgate, weights, (normed, gain, mlp, dgain), refs = refs[0], refs[1:6], refs[6:10], refs[10:]
    gated, grads, refs = refs[0], refs[1 : blocks + 1], refs[blocks + 1 :]
    out_refs, (own, given), refs = refs[:blocks], refs[blocks : blocks + 2], refs[blocks + 2 :]
    gp, taps, dlog, dconv, small, ends, everything, turned, turned_grad, sums = refs
    half, width = own.shape[0] - 16, gp.shape[1]
    wide, nq = own.shape[1], gated.shape[1]
    gp[0:RIM, width - nq :] = jnp.zeros((RIM, nq), bf16)
    backward_body(nh, maps, local_sums, *inputs, gp, taps, dlog, dconv, small, ends)
    copies.need(dgate, normed, gated, *grads)
    gp[RIM:, width - nq :] = dgate[...]
    turn(normed, turned)
    two_halves(place, turned, gp, own, given, slice(0, width))
    each = grads[0].shape[0]
    for shift, grad in enumerate(grads):
        at = pl.multiple_of(lax.rem(place[0] + (blocks - shift), blocks) * each, 128)
        for n in range(grad.shape[1] // 128):
            turned_grad[n * 128 : (n + 1) * 128, pl.ds(at, each)] = jnp.transpose(
                grad[:, n * 128 : (n + 1) * 128]
            )
    two_halves(place, turned_grad, gated, own, given, slice(width, wide))
    sums[...] = jnp.zeros(sums.shape, f32)
    sums[0:4, : taps.shape[1]] = taps[...]
    sums[4:5, :128] = dlog[...]
    sums[4:5, 128 : 128 + dgain.shape[1]] = dgain[...]
    own[half:, :] = two_parts(sums[...])
    given[half:, :] = own[half:, :]
    copies.done(given, own)
    copies.need(*weights)
    normed_back(blocks, place, gp, weights, normed, gain, mlp, out_refs, everything)


def backward_body(
    nh, map_refs, local_refs, at_ref, dt_ref, score_ref, dcore_ref, t_ref, fresh_ref, sin_ref,
    q_ref, k_ref, v_ref, beta_ref, gam_ref, dec_ref, conv_ref, pre_ref, info_ref, tq_ref, tk_ref, tv_ref,
    rate_ref, glog_ref,
    gp_ref, taps_ref, dlog_ref,
    dconv_ref, small_ref, ends_ref,
):
    length = q_ref.shape[0]
    nc = length // CT
    nq = nh * 128
    width = 5 * nq
    ends = []
    for h in range(nh):
        end = local_refs[0][h].astype(f32)
        for map_ref, local_ref in zip(map_refs[1:], local_refs[1:]):
            passed = split(map_ref[h, :128].astype(f32))
            end = mm3_deep(split(end), passed, NT) + local_ref[h].astype(f32)
        ends.append(end)
    row, col, later, same_token = step_order()
    before = (later > 0) | same_token
    last_row = (iota2((CT, 1), 0) == CT - 1).astype(f32)
    dconv_ref[0:RIM, :] = jnp.zeros((RIM, width), f32)
    dconv_ref[RIM + length :, :] = jnp.zeros((RIM, width), f32)
    lane = iota2((CT, 128), 1)
    upper = (iota2((CT, CT), 0) <= iota2((CT, CT), 1)).astype(f32)

    def chain(i, ends):
        c = nc - 1 - i
        out = []
        for h in range(nh):
            ends_ref[c, h] = ends[h]
            out.append(mm3_deep(split(ends[h]), split(at_ref[c, h]), NT) + dt_ref[c, h])
        return tuple(out)

    copies.need(at_ref, dt_ref)
    lax.fori_loop(0, nc, chain, tuple(ends))
    copies.need(score_ref, dcore_ref, t_ref, fresh_ref, sin_ref, q_ref, k_ref, v_ref, dec_ref, conv_ref)

    def chunks(group, carry):
        for i in range(BACKWARD):
            chunk(group * BACKWARD + i)
        return carry

    def chunk(c):
        rows = rows_of(c)
        store = rows_of(c, CT, RIM)
        info = info_ref[store, :]
        small = jnp.zeros((CT, 128), f32)
        dgam = jnp.zeros((CT, 128), f32)
        for h in range(nh):
            cols = slice(h * 128, (h + 1) * 128)
            end = ends_ref[c, h]
            end2 = split(end)
            _, carried, tail, _ = decays(gam_ref, info, rows, h, nh)
            carried2, tail2 = twice(carried), twice(tail)
            key = head_steps(k_ref, rows, h)
            value = head_steps(v_ref, rows, h)
            query = q_ref[rows, cols]
            beta = jnp.concatenate(
                [beta_ref[rows, 2 * h + j : 2 * h + j + 1] for j in range(2)], 0
            )
            wide = dec_ref[c, h]
            full = jnp.where(before, twice(wide), 0.0)
            state = sin_ref[c, h]
            fresh = fresh_ref[c, h]
            fresh2 = split(fresh)
            dcore = dcore_ref[rows, cols]
            dft = mm3_deep(split(jnp.transpose(dcore)), split(score_ref[c, h])) + mm3_deep(
                end2, split(key * tail2), NT
            )
            solved = jnp.transpose(mm3_deep(split(dft), split(t_ref[c, h])))
            both = split(jnp.concatenate([solved, dcore], 0))
            through = mm3_deep(both, split(state))
            pairs = mm3_deep(both, fresh2, NT)
            dtail = mm3_deep(fresh2, end2)
            em = -pairs[: 2 * CT] * full
            ps = pairs[2 * CT :] * wide
            mixed = mm3_deep(split(jnp.concatenate([em, ps], 0)), split(key))
            turned = jnp.transpose(jnp.concatenate([beta * em, ps], 0))
            dkb = mm3_deep(split(turned), split(jnp.concatenate([key, query], 0))) + tail2 * dtail
            x1 = mixed[: 2 * CT] - carried2 * through[: 2 * CT]
            dka = beta * x1
            dkey = dka + dkb
            dbeta = jnp.sum(key * x1 + solved * value, -1, keepdims=True)
            dvalue = beta * solved
            dquery = mixed[2 * CT :] + carried * through[2 * CT :]
            turn = jnp.sum(key * (dka - dkb), -1, keepdims=True)
            closing = jnp.sum(
                jnp.sum(end * sin_ref[c + 1, h], -1, keepdims=True), 0, keepdims=True
            )
            dg = (
                jnp.sum(query * dquery, -1, keepdims=True)
                + turn[:CT]
                + turn[CT:]
                + last_row * closing
            )
            dgam = jnp.where(lane == 2 * nh + h, dg, dgam)
            for j in range(2):
                small = jnp.where(lane == 2 * h + j, dbeta[j * CT : (j + 1) * CT], small)
            pre = conv_ref[rows, cols]
            sig = jax.nn.sigmoid(pre)
            dconv_ref[store, cols] = dquery * (sig * (1.0 + pre * (1.0 - sig)))
            for j in range(2):
                kcols = slice(nq + (2 * h + j) * 128, nq + (2 * h + j + 1) * 128)
                pre = conv_ref[rows, kcols]
                sig = jax.nn.sigmoid(pre)
                act = pre * sig
                scale = lax.rsqrt(jnp.sum(act * act, -1, keepdims=True) + EPS)
                unit = key[j * CT : (j + 1) * CT]
                grad = dkey[j * CT : (j + 1) * CT]
                grad = scale * (grad - unit * jnp.sum(unit * grad, -1, keepdims=True))
                dconv_ref[store, kcols] = grad * (sig * (1.0 + pre * (1.0 - sig)))
                vcols = slice(3 * nq + (2 * h + j) * 128, 3 * nq + (2 * h + j + 1) * 128)
                pre = conv_ref[rows, vcols]
                sig = jax.nn.sigmoid(pre)
                dconv_ref[store, vcols] = dvalue[j * CT : (j + 1) * CT] * (
                    sig * (1.0 + pre * (1.0 - sig))
                )
        dglog = exact(upper, dgam)
        small_ref[rows, :] = jnp.where(lane < 2 * nh, small, dglog)

    lax.fori_loop(0, nc // BACKWARD, chunks, 0)

    copies.need(pre_ref, glog_ref)
    beta = beta_ref[...]
    small = small_ref[...]
    lanes = iota2(beta.shape, 1)
    grads = small * beta * jnp.where(lanes < 2 * nh, 1.0 - beta, rate_ref[...])
    dlog_ref[...] = jnp.sum(small * glog_ref[...], 0, keepdims=True)
    gp_ref[0:RIM, 0 : width + 128] = jnp.zeros((RIM, width + 128), bf16)
    gp_ref[RIM:, width : width + 128] = grads.astype(bf16)
    groups = ((tq_ref, 0, nh), (tk_ref, nq, 2 * nh), (tv_ref, 3 * nq, 2 * nh))

    def turned_back(grad, masks, taps, count):
        total = grad[:count] * taps[0:1]
        size = grad.shape[0]
        for m in range(1, 4):
            moved = pltpu.roll(grad * masks[:, m : m + 1], size - m, 0)
            total = total + moved[:count] * taps[m : m + 1]
        return total

    def conv_back(c, sums):
        info = info_ref[near(c, RIM), :]
        new = []
        for tap_ref, first, count in groups:
            for j in range(count):
                cols = slice(first + j * 128, first + (j + 1) * 128)
                taps = tap_ref[:, j * 128 : (j + 1) * 128].astype(f32)
                grad = dconv_ref[near(c, RIM), cols]
                gp_ref[rows_of(c, CT, RIM), cols] = turned_back(grad, info, taps, CT).astype(bf16)
                block = pre_ref[near(c, RIM - 8), cols]
                parts = [jnp.sum(grad[:CT] * block[8:], 0, keepdims=True)]
                for m in range(1, 4):
                    moved = pltpu.roll(block, m, 0)[8:]
                    parts.append(
                        jnp.sum(grad[:CT] * info[:CT, m : m + 1] * moved, 0, keepdims=True)
                    )
                new.append(jnp.concatenate(parts, 0))
        return sums + jnp.concatenate(new, 1)

    taps_ref[...] = lax.fori_loop(0, nc, conv_back, jnp.zeros((4, width), f32))
    for tap_ref, first, count in groups:
        cols = slice(first, first + count * 128)
        taps = tap_ref[...].astype(f32)
        early = slice(8, 24)
        rim = turned_back(dconv_ref[early, cols], info_ref[early, :], taps, 8)
        gp_ref[0:RIM, cols] = jnp.concatenate([jnp.zeros_like(rim), rim], 0).astype(bf16)


VMEM = pl.BlockSpec(memory_space=pltpu.VMEM)
SMEM = pl.BlockSpec(memory_space=pltpu.SMEM)
ANY = pl.BlockSpec(memory_space=pl.ANY)


class Late:
    def __init__(self, value):
        self.value = value


def late(*values):
    return [Late(value) for value in values]


class Copies:
    def __init__(self):
        self.coming, self.going = {}, {}

    def need(self, *refs):
        for ref in refs:
            copy = self.coming.pop(id(ref), None)
            if copy is not None:
                copy.wait()

    def done(self, *refs, at=None):
        for ref in refs:
            entry = self.going.get(id(ref))
            if entry is None:
                continue
            target, sem, _ = entry
            source = ref
            if at is not None:
                source, target = ref.at[at], target.at[at]
            pltpu.make_async_copy(source, target, sem).start()
            self.going[id(ref)] = (entry[0], sem, True)

    def finish(self, refs):
        for copy in self.coming.values():
            copy.wait()
        self.coming = {}
        for ref in refs:
            if id(ref) in self.going and not self.going[id(ref)][2]:
                self.done(ref)
        for ref in refs:
            if id(ref) in self.going:
                target, sem, _ = self.going.pop(id(ref))
                pltpu.make_async_copy(ref, target, sem).wait()


copies = Copies()


def kernel_call(body, name, args, outs, scratch=(), after=(), hbm=(), mib=24, cost=2):
    late_in = [n for n, a in enumerate(args) if isinstance(a, Late)]
    late_out = [n for n, s in enumerate(outs) if isinstance(s, Late)]
    args = [a.value if isinstance(a, Late) else a for a in args]
    outs = [s.value if isinstance(s, Late) else s for s in outs]
    extra, n_in, n_out, n_scratch = len(after), len(args), len(outs), len(scratch)
    buffers = [pltpu.VMEM(args[n].shape, args[n].dtype) for n in late_in]
    buffers += [pltpu.VMEM(outs[n].shape, outs[n].dtype) for n in late_out]
    sems = [pltpu.SemaphoreType.DMA((len(late_in) + len(late_out),))] if buffers else []

    def run(*refs):
        in_refs, refs = list(refs[:n_in]), refs[n_in + extra :]
        out_refs, refs = list(refs[:n_out]), refs[n_out:]
        own_scratch, refs = refs[:n_scratch], refs[n_scratch:]
        held = []
        for k, n in enumerate(late_in):
            copy = pltpu.make_async_copy(in_refs[n], refs[k], refs[-1].at[k])
            copy.start()
            copies.coming[id(refs[k])] = copy
            in_refs[n] = refs[k]
        for k, n in enumerate(late_out, len(late_in)):
            copies.going[id(refs[k])] = (out_refs[n], refs[-1].at[k], False)
            out_refs[n] = refs[k]
            held.append(refs[k])
        body(*in_refs, *out_refs, *own_scratch)
        copies.finish(held)

    in_specs = [SMEM if a.dtype == i32 else VMEM for a in args]
    out_specs = [VMEM] * n_out
    for n in (*late_in, *hbm):
        in_specs[n] = ANY
    for n in late_out:
        out_specs[n] = ANY
    return pl.pallas_call(
        run,
        name=name,
        in_specs=in_specs + [ANY] * extra,
        out_specs=out_specs,
        out_shape=outs,
        scratch_shapes=[*scratch, *buffers, *sems],
        compiler_params=pltpu.CompilerParams(vmem_limit_bytes=mib * MIB),
        cost_estimate=pl.CostEstimate(flops=cost * 10**9, bytes_accessed=0, transcendentals=0),
    )(*args, *after)


def sds(*shape, dtype=f32):
    return jax.ShapeDtypeStruct(shape, dtype)


def mixer_forward(me, tokens, rim, norm_gain, weights, taps, info, doc_rows, rate):
    length, width = tokens[0].shape
    length *= len(tokens)
    w_query, w_key, w_value, w_outgate, w_small = weights
    nh = w_query.shape[1] // 128
    nc, nq = length // CT, nh * 128
    per = (nc, nh)
    outs = dict(
        normed=sds(RIM + length, width, dtype=bf16),
        pre=sds(RIM + length, 5 * nq),
        conv=sds(length, 5 * nq),
        gate=sds(length, nq),
        q=sds(length, nq),
        k=sds(length, 2 * nq),
        v=sds(length, 2 * nq),
        beta=sds(length, 128),
        glog=sds(length, 128),
        gam=sds(length, 128),
        dec=sds(*per, CT, 128),
        t=sds(*per, 128, 128),
        w=sds(*per, 128, 128),
        u=sds(*per, 128, 128),
        reach=sds(*per, CT, 128),
        score=sds(*per, CT, 128),
        at=sds(*per, 128, 128),
        bt=sds(*per, 128, 128),
        info=sds(length + 2 * RIM, 8),
        low=sds(nh, 256, 128, dtype=bf16),
    )
    args = (
        me, *tokens, rim, norm_gain, *late(w_query, w_key, w_value, w_outgate, w_small), *taps, info, doc_rows,
        rate,
    )
    res = kernel_call(
        functools.partial(forward_kernel, nh, len(tokens)), "mixer_forward", args,
        [s if n in ("info", "low") else Late(s) for n, s in outs.items()],
        cost=25, mib=60,
        scratch=[pltpu.VMEM((nh, 256, 128), f32)],
    )
    return dict(zip(outs, res))


def mixer_output(me, maps, fwd, out_gain, w_out, blocks, after=()):
    nc, nh = fwd["w"].shape[:2]
    length = nc * CT
    outs = dict(
        sin=sds(nc + 1, nh, 128, 128),
        fresh=sds(nc, nh, 128, 128),
        core=sds(length, nh * 128),
        gated=sds(length, nh * 128, dtype=bf16),
    )
    parts = [sds(length // blocks, w_out.shape[1], dtype=bf16)] * blocks
    names = ("at", "bt", "w", "reach", "u", "score", "gate")
    args = (me, *maps, *late(*(fwd[n] for n in names)), out_gain, *late(w_out))
    res = kernel_call(
        functools.partial(output_kernel, nh, len(maps), blocks), "mixer_output", args,
        late(*outs.values(), *parts), cost=10, mib=60,
        scratch=[pltpu.VMEM((length, w_out.shape[1]), bf16)],
        after=after,
    )
    return dict(zip(outs, res), branch=res[len(outs) :])


def mixer_adjoint(me, grad, w_out, fwd, out, out_gain, after=()):
    nc, nh = fwd["w"].shape[:2]
    length = nc * CT
    outs = dict(
        dcore=sds(length, nh * 128),
        dt=sds(nc, nh, 128, 128),
        dgate=sds(length, nh * 128, dtype=bf16),
        dgain=sds(1, nh * 128),
        local=sds(nh, 128, 128, dtype=bf16),
    )
    args = (
        me, *grad, w_out, out["core"], fwd["gate"], out_gain,
        *(fwd[n] for n in ("score", "reach", "w", "at")),
    )
    res = kernel_call(
        functools.partial(adjoint_kernel, nh, len(grad)), "mixer_adjoint", args,
        [s if n in ("dgain", "local") else Late(s) for n, s in outs.items()],
        cost=10, mib=24,
        scratch=[pltpu.VMEM((length, nh * 128), f32), pltpu.VMEM((length, w_out.shape[1]), bf16)],
        after=after,
    )
    return dict(zip(outs, res))


def mixer_backward(
    place, maps, local_sums, fwd, out, adj, taps, rate, weights, gain, mlp, grad, after=()
):
    nc, nh = fwd["w"].shape[:2]
    length, nq = nc * CT, nh * 128
    width = 5 * nq
    model = gain.shape[1]
    blocks = len(grad)
    parts = [sds(RIM + length // blocks, model, dtype=bf16)] * blocks
    columns = width + 128 + 2 * nq
    halves = [sds(model // 2 + 16, columns, dtype=bf16)] * 2
    args = (
        *maps, *local_sums, place,
        *late(
            fwd["at"], adj["dt"], fwd["score"], adj["dcore"], fwd["t"], out["fresh"], out["sin"],
            *(fwd[n] for n in ("q", "k", "v")),
        ),
        fwd["beta"], fwd["gam"], *late(fwd["dec"], fwd["conv"], fwd["pre"]), fwd["info"], *taps, rate,
        *late(fwd["glog"], adj["dgate"], *weights, fwd["normed"]), gain, mlp, adj["dgain"],
        *late(out["gated"], *grad),
    )
    *res, own, given = kernel_call(
        functools.partial(backward_kernel, nh, len(maps), blocks), "mixer_backward", args,
        late(*parts, *halves), cost=300, mib=60,
        scratch=[
            pltpu.VMEM((RIM + length, width + 128 + nq), bf16), pltpu.VMEM((4, width), f32),
            pltpu.VMEM((1, 128), f32),
            pltpu.VMEM((length + 2 * RIM, width), f32), pltpu.VMEM((length, 128), f32),
            pltpu.VMEM((nc, nh, 128, 128), f32), pltpu.VMEM((RIM + length, model), bf16),
            pltpu.VMEM((model, RIM + length), bf16), pltpu.VMEM((model, length), bf16),
            pltpu.VMEM((8, columns), f32),
        ],
        after=after,
    )
    return res, (own, given)


def token_info(doc_ids):
    ids = doc_ids.astype(f32)
    length = ids.shape[0]
    extended = jnp.concatenate([ids[:3], ids])
    masks = [(extended[3 - m : 3 - m + length] == ids).astype(f32) for m in range(4)]
    blocks = ids.reshape(-1, CT)
    last = blocks[:, -1:]
    previous = jnp.concatenate([blocks[:1, :1], last[:-1]], 0)
    columns = masks + [
        (blocks == previous).astype(f32).reshape(-1),
        (blocks == last).astype(f32).reshape(-1),
        ids,
        jnp.zeros_like(ids),
    ]
    info = jnp.pad(jnp.stack(columns, 1), ((RIM, RIM), (0, 0)))
    return info, blocks[:, None, :]


def middle_kernel(count, tok_ref, *refs):
    parts, (gain_ref, middle_ref, normed_ref) = refs[:count], refs[count:]
    middle = tok_ref[...].astype(f32)
    total = parts[0][...].astype(f32)
    for part in parts[1:]:
        total = total + part[...].astype(f32)
    middle = middle + total
    middle_ref[...] = middle
    scale = lax.rsqrt(jnp.mean(middle * middle, -1, keepdims=True) + EPS)
    normed_ref[...] = (middle * scale * gain_ref[...]).astype(bf16)


def feed_kernel(hidden, place_ref, *refs):
    x_refs, cot_refs, weights, refs = refs[:2], refs[2:4], refs[4:7], refs[-9:]
    norm_refs, block_refs, cols_ref, refs = refs[:2], refs[2:4], refs[4], refs[5:]
    gate_w, up_w, down_w, sems = refs
    width = gate_w.shape[1]
    each = x_refs[0].shape[0]
    window = pl.ds(pl.multiple_of(place_ref[3], 128), width)
    moves = [
        pltpu.make_async_copy(weights[0].at[:, window], gate_w, sems.at[0]),
        pltpu.make_async_copy(weights[1].at[:, window], up_w, sems.at[1]),
        pltpu.make_async_copy(weights[2].at[window, :], down_w, sems.at[2]),
    ]
    for move in moves:
        move.start()
    lane = iota2((1, width), 1) - place_ref[4]
    mask = ((lane >= 0) & (lane < hidden)).astype(f32)
    x = jnp.concatenate([ref[...] for ref in x_refs], 0)
    cot = jnp.concatenate([ref[...] for ref in cot_refs], 0)
    moves[0].wait()
    gate = mm(x, gate_w[...])
    moves[1].wait()
    up = mm(x, up_w[...]) * mask
    sig = jax.nn.sigmoid(gate)
    silu = gate * sig * mask
    act = (silu * up).astype(bf16)
    moves[2].wait()
    grad = mm(cot, down_w[...], NT)
    ggate = (grad * up * sig * (1.0 + gate * (1.0 - sig))).astype(bf16)
    gup = (grad * silu).astype(bf16)
    gnorm = (mm(ggate, gate_w[...], NT) + mm(gup, up_w[...], NT)).astype(bf16)
    block = mm(act, down_w[...]).astype(bf16)
    for n in range(2):
        half = slice(n * each, (n + 1) * each)
        norm_refs[n][...] = gnorm[half]
        block_refs[n][...] = block[half]
    for n, value in enumerate((ggate, gup, act)):
        cols_ref[n] = value


def with_bit(index, position, bit):
    low = index & ((1 << position) - 1)
    return ((index >> position) << (position + 1)) + bit * (1 << position) + low


def seq_bit(place_ref, bit):
    return lax.rem(lax.div(place_ref[2], 1 << bit), 2)


def feed_grads_kernel(bits, place_ref, *refs):
    x_refs, cot_refs, cols_refs, refs = refs[:4], refs[4:8], refs[8:10], refs[10:]
    out_refs, (turned_ref, full_ref) = refs[:-2], refs[-2:]
    each = x_refs[0].shape[0]
    half = full_ref.shape[0]
    rows = half >> bits
    for n, blocks in enumerate((x_refs, cot_refs)):
        for p, ref in enumerate(blocks):
            turned_ref[n, :, p * each : (p + 1) * each] = jnp.transpose(ref[...])
    for b in range(2):
        for k in range(3):
            left = turned_ref[k // 2, b * half : (b + 1) * half, :]
            if not (k or b):
                copies.need(*cols_refs)
            full_ref[...] = (
                mm(left[:, : 2 * each], cols_refs[0][k]) + mm(left[:, 2 * each :], cols_refs[1][k])
            ).astype(bf16)
            position = (bits - 1) * b
            mine = seq_bit(place_ref, position)
            for n, bit in enumerate((mine, 1 - mine)):
                out_ref = out_refs[2 * b + n]
                for i in range(1 << (bits - 1)):
                    at = with_bit(i, position, bit) * rows
                    first = (k * (1 << (bits - 1)) + i) * rows
                    out_ref[first : first + rows, :] = full_ref[
                        pl.ds(pl.multiple_of(at, rows), rows), :
                    ]
        copies.done(*out_refs[2 * b : 2 * b + 2])


def feed_seq_kernel(bits, left, place_ref, *refs):
    in_refs, out_refs, (sum_ref,) = refs[:4], refs[4:8], refs[8:]
    for b in range(2):
        sum_ref[...] = in_refs[2 * b][...].astype(f32) + in_refs[2 * b + 1][...].astype(f32)
        rows = sum_ref.shape[0] // (3 << left)
        position = (left - 1) * b
        mine = seq_bit(place_ref, bits - left if b == 0 else left - 1)
        for n, bit in enumerate((mine, 1 - mine)):
            out_ref = out_refs[2 * b + n]
            for k in range(3):
                for i in range(1 << (left - 1)):
                    at = ((k << left) + with_bit(i, position, bit)) * rows
                    first = ((k << (left - 1)) + i) * rows
                    out_ref[first : first + rows, :] = sum_ref[
                        pl.ds(pl.multiple_of(at, rows), rows), :
                    ].astype(bf16)
            copies.done(out_ref)


def feed_head_kernel(pairs, place_ref, *refs):
    in_refs, out_refs, (sum_ref,) = refs[:4], refs[4:-1], refs[-1:]
    size = in_refs[0].shape[0]
    for b in range(2):
        sum_ref[b * size : (b + 1) * size, :] = in_refs[2 * b][...].astype(f32) + in_refs[
            2 * b + 1
        ][...].astype(f32)
    rows = out_refs[0].shape[0] // 6
    for shift, out_ref in enumerate(out_refs):
        at = lax.rem(lax.div(place_ref[0], 2) + shift, pairs) * rows
        for n in range(6):
            piece = sum_ref[pl.ds(pl.multiple_of(at + n * rows * pairs, rows), rows), :]
            out_ref[n * rows : (n + 1) * rows, :] = piece.astype(bf16)


def feed_pair_kernel(count, place_ref, *refs):
    parts, out_refs, (sum_ref,) = refs[:count], refs[count:-1], refs[-1:]
    sum_ref[...] = add_up([part[...] for part in parts])
    rows = out_refs[0].shape[0] // 6
    for other, out_ref in enumerate(out_refs):
        odd = lax.rem(place_ref[0] + other, 2) == 1
        for n in range(2):
            core = lax.rem(place_ref[1] + n, 2)
            for k in range(3):
                both = sum_ref[pl.ds(pl.multiple_of((core * 3 + k) * 2 * rows, 2 * rows), 2 * rows), :]
                first = (n * 3 + k) * rows
                value = jnp.where(odd, both[rows:], both[:rows])
                out_ref[first : first + rows, :] = value.astype(bf16)


def feed_out_kernel(hidden, place_ref, *refs):
    parts, (gate_ref, up_ref, down_ref) = refs[:4], refs[4:]
    rows = parts[0].shape[0] // 6
    own = lax.rem(place_ref[0], 2) * 2 + place_ref[1]
    for k, out_ref in enumerate((gate_ref, up_ref, down_ref)):
        values = [
            part[(n % 2 * 3 + k) * rows : (n % 2 * 3 + k + 1) * rows, :].astype(f32)
            for n, part in enumerate(parts)
        ]
        for g in range(4):
            value = values[0]
            for n in range(1, 4):
                value = jnp.where(own == (g ^ n), values[n], value)
            start = g * hidden % 128
            value = value[:, start : start + hidden]
            out_ref[:, g * hidden : (g + 1) * hidden] = value


def mixer_blocks_kernel(place_ref, own_ref, got_ref, *out_refs):
    count = len(out_refs)
    half = own_ref.shape[0] - 16
    rows = half // count
    small = two_parts(joined_parts(own_ref, half, 8) + joined_parts(got_ref, half, 8))
    for shift, out_ref in enumerate(out_refs):
        at = pl.ds(pl.multiple_of(lax.rem(place_ref[2] + shift, count) * rows, 16), rows)
        out_ref[0:rows, :] = (own_ref[at, :].astype(f32) + got_ref[at, :].astype(f32)).astype(bf16)
        out_ref[rows:, :] = small
        copies.done(out_ref)


def joined_parts(ref, start, extra):
    both = ref[start : start + 2 * extra, :].astype(f32)
    return both[:extra] + both[extra:]


def mixer_sum_kernel(count, nh, *refs):
    parts, out_refs = refs[:count], refs[count:]
    weight_refs, conv_refs, (decay_ref, gain_ref) = out_refs[:7], out_refs[7:10], out_refs[10:]
    rows = weight_refs[0].shape[0]
    nq = nh * 128
    starts = (0, nq, 3 * nq, 5 * nq, 5 * nq + 2 * nh, 5 * nq + 128, 6 * nq + 128)
    for n, (start, out_ref) in enumerate(zip(starts, weight_refs)):
        turned = n in (3, 4, 6)
        width = out_ref.shape[0] if turned else out_ref.shape[1]
        total = add_up([part[0:rows, start : start + width] for part in parts])
        out_ref[...] = jnp.transpose(total) if turned else total
    small = add_up([joined_parts(part, rows, 8) for part in parts])
    for start, out_ref in zip(starts, conv_refs):
        out_ref[...] = small[0:4, start : start + out_ref.shape[1]]
    decay_ref[...] = small[4:5, 2 * nh : 3 * nh]
    gain_ref[...] = small[4:5, 128 : 128 + nq]


def norm_back(grad_normed, rows, gain):
    scale = lax.rsqrt(jnp.mean(rows * rows, -1, keepdims=True) + EPS)
    unit = rows * scale
    scaled = grad_normed * gain
    grad_rows = scale * (scaled - unit * jnp.mean(scaled * unit, -1, keepdims=True))
    return grad_rows, jnp.sum(grad_normed * unit, 0, keepdims=True)


def middle_back_kernel(a_ref, b_ref, c_ref, middle_ref, cot_ref, gain_ref, grad_ref, low_ref, sum_ref):
    total = a_ref[...].astype(f32) + b_ref[...].astype(f32) + c_ref[...].astype(f32)
    rows, sum_ref[...] = norm_back(total, middle_ref[...], gain_ref[...])
    grad = cot_ref[...].astype(f32) + rows
    grad_ref[...] = grad
    low_ref[...] = grad.astype(bf16)


def extra_rows_kernel(count, *refs):
    parts, (rim_ref, gains_ref) = refs[:count], refs[count:]
    each = parts[0].shape[0] - RIM
    total = add_up([part[each:, :] for part in parts])
    row = iota2((RIM, 1), 0)
    rim_ref[...] = jnp.where(row >= RIM - 3, total, 0.0).astype(bf16)
    gains_ref[...] = jnp.zeros(gains_ref.shape, f32)
    for n in range(2):
        gains_ref[n : n + 1, :] = total[2 * n : 2 * n + 1] + total[2 * n + 1 : 2 * n + 2]


def tokens_back_kernel(count, *refs):
    parts, (rim_ref, tok_ref, gain_ref, middle_ref, grad_ref) = refs[:count], refs[count:]
    each = tok_ref.shape[0]
    total = add_up([part[0:each, :] for part in parts])
    rim = rim_ref[...].astype(f32)
    total = total + jnp.concatenate([jnp.zeros((each - RIM, rim.shape[1]), f32), rim], 0)
    rows, _ = norm_back(total, tok_ref[...].astype(f32), gain_ref[...])
    grad_ref[...] = middle_ref[...] + rows


HEAD = ("pair", "half")


def axis_size(axis):
    return lax.axis_size(axis) if isinstance(axis, str) else lax.psum(1, axis)


def ring(value, axis):
    count = axis_size(axis)
    return [value] + [
        lax.ppermute(value, axis, [(i, (i + shift) % count) for i in range(count)])
        for shift in range(1, count)
    ]


def along(value, axis, shift):
    count = axis_size(axis)
    pairs = [(i, i + shift) for i in range(count) if 0 <= i + shift < count]
    return lax.ppermute(value, axis, pairs)


def crossed(value, axis, bit=0):
    return lax.ppermute(value, axis, [(i, i ^ (1 << bit)) for i in range(axis_size(axis))])


def spread(blocks, axis):
    count = axis_size(axis)
    return [blocks[0]] + [
        lax.ppermute(blocks[shift], axis, [(i, (i + shift) % count) for i in range(count)])
        for shift in range(1, count)
    ]


def add_up(parts):
    total = parts[0].astype(f32)
    for part in parts[1:]:
        total = total + part.astype(f32)
    return total


def sum_over(value, axis):
    return add_up(ring(value, axis))


def tied(*values):
    return lax.optimization_barrier(values)


def on_device(
    tokens, doc_ids, norm_gain, w_query, w_key, w_value, w_beta, w_decay, w_outgate, conv_query,
    conv_key, conv_value, decay_log, out_gain, w_out, mlp_gain, w_gate, w_up, w_down, cotangent,
):
    head_n, seq_n, batch_n = (axis_size(a) for a in (HEAD, "seq", "batch"))
    me = lax.axis_index(HEAD)
    nh = w_decay.shape[1]
    nq = nh * 128
    each, model = tokens.shape
    length = each * head_n
    me_array = me.astype(i32).reshape(1)

    head_last = head_n - 1
    blocks = ring(tokens, HEAD)
    seq_place = lax.axis_index("seq")
    core = lax.axis_index("batch")
    ways = 2 * batch_n
    hidden = w_gate.shape[1] // ways
    mine = ((me & 1) * batch_n + core) * hidden
    place = jnp.stack([me, core, seq_place, mine // 128 * 128, mine % 128]).astype(i32)
    window = -(-(hidden + 64) // 128) * 128
    ids = jnp.broadcast_to(doc_ids[-RIM:, None], (RIM, 128)).astype(bf16)
    tail = tied(jnp.concatenate([tokens[-RIM:], ids], 1), blocks[-1])[0]
    rim = add_up(
        [
            lax.ppermute(
                tail,
                ("seq", *HEAD),
                [(s * head_n + head_last, (s + 1) * head_n + h) for s in range(seq_n - 1)],
            )
            for h in range(head_n)
        ]
    ).astype(bf16)
    info, doc_rows = token_info(doc_ids)
    w_small = jnp.pad(jnp.concatenate([w_beta, w_decay], 1), ((0, 0), (0, 128 - 3 * nh)))
    rate = jnp.pad(-jnp.exp(decay_log), (2 * nh, 128 - 3 * nh))[None]
    weights = (w_query, w_key, w_value, w_outgate, w_small)
    taps = (conv_query, conv_key, conv_value)
    gain = norm_gain[None]
    fwd = mixer_forward(me_array, blocks, rim, gain, weights, taps, info, doc_rows, rate)

    states = ring(fwd["low"], "seq")
    cot_sent = tied(cotangent, fwd["low"])[0]
    cot_near = crossed(cot_sent, HEAD)
    cots = [cotangent, cot_near, *[crossed(value, "batch") for value in (cot_sent, cot_near)]]
    out = mixer_output(place, states[1:], fwd, out_gain[None], w_out, head_n)

    low = lambda *shape: sds(*shape, dtype=bf16)
    parts = spread(out["branch"], HEAD)
    middle, normed_mid = kernel_call(
        functools.partial(middle_kernel, len(parts)), "middle",
        (tokens, *parts, mlp_gain[None]), [sds(each, model), low(each, model)],
        after=cots[1:],
    )
    near = crossed(normed_mid, HEAD)

    def feed(rows, cots, after=()):
        return pl.pallas_call(
            functools.partial(feed_kernel, hidden),
            name="feed",
            in_specs=[SMEM] + [VMEM] * 4 + [ANY] * (3 + len(after)),
            out_specs=[VMEM] * 5,
            out_shape=[low(each, model)] * 4 + [low(3, 2 * each, window)],
            scratch_shapes=[
                pltpu.VMEM((model, window), bf16), pltpu.VMEM((model, window), bf16),
                pltpu.VMEM((window, model), bf16), pltpu.SemaphoreType.DMA((3,)),
            ],
            compiler_params=pltpu.CompilerParams(vmem_limit_bytes=40 * MIB),
            cost_estimate=pl.CostEstimate(flops=5 * 10**9, bytes_accessed=0, transcendentals=0),
        )(place, *rows, *cots, w_gate, w_up, w_down, *after)

    rows = [normed_mid, crossed(normed_mid, "batch")]
    cots = [cots[0], cots[2], cots[1], cots[3]]
    first = feed(rows, cots[:2])
    near_sent = tied(near, first[0])[0]
    rows += [near, crossed(near_sent, "batch")]
    second = feed(rows[2:], cots[2:], after=first[:1])
    fed = [first[0], second[0], first[1], second[1], first[2], second[2], first[3], second[3]]
    fed += [first[4], second[4]]

    def own_parts(blocks):
        given = (blocks[1].astype(f32) + crossed(blocks[3], "batch").astype(f32)).astype(bf16)
        return given, (blocks[0], crossed(blocks[2], "batch"), crossed(given, HEAD))

    given, norm_parts = own_parts(fed[:4])
    block_own = crossed(fed[6], "batch")
    block_given = (fed[5].astype(f32) + crossed(fed[7], "batch").astype(f32)).astype(bf16)

    seq_rows = model // (batch_n * seq_n)
    seq_bits = seq_n.bit_length() - 1
    size = 3 * model // 4
    feed_kept = kernel_call(
        functools.partial(feed_grads_kernel, seq_bits), "feed_grads",
        (place, *rows, *cots, *late(*fed[8:])), late(*[low(size, window)] * 4),
        scratch=[
            pltpu.VMEM((2, model, 4 * each), bf16), pltpu.VMEM((model // 2, window), bf16),
        ],
        after=[given],
    )

    def exchanged(values, step):
        bits = (step, seq_bits - 1 - step)
        return [
            value
            for b in range(2)
            for value in (values[2 * b], crossed(values[2 * b + 1], "seq", bits[b]))
        ]

    grad_middle, grad_branch, grad_mlp_gain = kernel_call(
        middle_back_kernel, "middle_back",
        (*norm_parts, middle, cotangent, mlp_gain[None]),
        [sds(each, model), low(each, model), sds(1, model)],
        after=feed_kept[1::2], cost=100,
    )
    feed_grads = exchanged(feed_kept, 0)
    grad_blocks = ring(grad_branch, HEAD)

    for step in range(1, seq_bits):
        size //= 2
        feed_kept = kernel_call(
            functools.partial(feed_seq_kernel, seq_bits, seq_bits - step), "feed_seq",
            (place, *feed_grads), late(*[low(size, window)] * 4),
            scratch=[pltpu.VMEM((2 * size, window), f32)],
            after=grad_blocks[1:2],
        )
        feed_grads = exchanged(feed_kept, step)
    adj = mixer_adjoint(
        me_array, grad_blocks, w_out, fwd, out, out_gain[None],
        after=[block_given, block_own, feed_kept[1]],
    )
    later = [along(adj["local"], "seq", -s) for s in range(seq_n - 1, 0, -1)]

    own_rows = model // (batch_n * seq_n * head_n)
    seq_rows = own_rows * head_n
    pairs = head_n // 2
    feed_kept = kernel_call(
        functools.partial(feed_head_kernel, pairs), "feed_head", (place, *feed_grads),
        late(*[low(12 * own_rows, window)] * pairs),
        scratch=[pltpu.VMEM((6 * seq_rows, window), f32)],
        after=[adj["local"]],
    )
    normed_parts, wide = mixer_backward(
        place, states[1:], later, fwd, out, adj, taps, rate,
        (w_query, w_key, w_value, w_small, w_outgate), gain, grad_mlp_gain, grad_blocks,
        after=[feed_kept[-1]],
    )
    feed_grads = [feed_kept[0]] + [
        lax.ppermute(
            feed_kept[shift], HEAD, [(i, (i + 2 * shift) % head_n) for i in range(head_n)]
        )
        for shift in range(1, pairs)
    ]
    block_given = crossed(tied(feed_kept[0], block_given)[1], HEAD)
    block_out = (middle + add_up([fed[4], block_own, block_given])).astype(bf16)
    normed_parts = spread(normed_parts, HEAD)

    columns = wide[0].shape[1]
    wide_blocks = kernel_call(
        mixer_blocks_kernel, "mixer_blocks",
        (place, wide[0], crossed(tied(wide[1], block_given, *feed_grads[1:])[0], "batch")),
        late(*[low(seq_rows + 16, columns)] * seq_n),
    )
    wide_parts = spread(wide_blocks, "seq")
    extra, gains = kernel_call(
        functools.partial(extra_rows_kernel, head_n), "extra_rows", normed_parts,
        [low(RIM, model), sds(8, model)],
        after=wide_parts[1:2],
    )
    gains = add_up([gains, crossed(gains, "batch")])
    gain_parts = ring(gains, "seq")
    rim_part = lax.ppermute(
        extra,
        ("seq", *HEAD),
        [(s * head_n + head_last, (s - 1) * head_n + head_last) for s in range(1, seq_n)],
    )
    group_own, group_sent = kernel_call(
        functools.partial(feed_pair_kernel, pairs), "feed_pair", (place, *feed_grads),
        [low(6 * own_rows, window)] * 2,
        scratch=[pltpu.VMEM((12 * own_rows, window), f32)],
        after=[extra],
    )
    group_got = crossed(group_sent, HEAD)
    group = [group_own, crossed(group_own, "batch"), group_got, crossed(group_got, "batch")]
    grad_gate, grad_up, grad_down = kernel_call(
        functools.partial(feed_out_kernel, hidden), "feed_out", (place, *group),
        [sds(own_rows, ways * hidden)] * 3,
    )
    (grad_tokens,) = kernel_call(
        functools.partial(tokens_back_kernel, head_n), "tokens_back",
        (*normed_parts, rim_part, tokens, gain, grad_middle),
        [sds(each, model)],
    )
    *sums, grad_decay, grad_out_gain = kernel_call(
        functools.partial(mixer_sum_kernel, seq_n, nh), "mixer_sum", wide_parts,
        [sds(seq_rows, w) for w in (nq, 2 * nq, 2 * nq)] + [sds(w, seq_rows) for w in (2 * nh, nh)]
        + [sds(seq_rows, nq), sds(nq, seq_rows)]
        + [sds(4, w) for w in (nq, 2 * nq, 2 * nq)] + [sds(1, nh), sds(1, nq)],
    )
    grad_q, grad_k, grad_v, grad_b, grad_d, grad_g, grad_out, *grad_convs = sums
    gains = add_up(gain_parts)
    index = (core * seq_n + seq_place) * head_n + me
    gains = lax.dynamic_slice_in_dim(gains, index * own_rows, own_rows, 1)
    return (
        block_out, grad_tokens, gains[0], grad_q, grad_k, grad_v, grad_b.T, grad_d.T, grad_g,
        *grad_convs, grad_decay[0], grad_out_gain[0], grad_out, gains[1], grad_gate, grad_up,
        grad_down.T,
    )


def solution(mesh):
    batch, seq, head = mesh.devices.shape
    split_mesh = Mesh(mesh.devices.reshape(batch, seq, head // 2, 2), ("batch", "seq", *HEAD))
    return jax.shard_map(
        on_device,
        mesh=split_mesh,
        in_specs=(
            P(("batch", "seq", *HEAD), None),
            P(("batch", "seq")),
            P(),
            P(None, HEAD),
            P(None, HEAD),
            P(None, HEAD),
            P(None, HEAD),
            P(None, HEAD),
            P(None, HEAD),
            P(None, HEAD),
            P(None, HEAD),
            P(None, HEAD),
            P(HEAD),
            P(HEAD),
            P(HEAD, None),
            P(),
            P(),
            P(),
            P(),
            P(("batch", "seq", *HEAD), None),
        ),
        out_specs=(
            P(("batch", "seq", *HEAD), None),
            P(("batch", "seq", *HEAD), None),
            P(("batch", "seq", *HEAD)),
            P(("batch", "seq"), HEAD),
            P(("batch", "seq"), HEAD),
            P(("batch", "seq"), HEAD),
            P(("batch", "seq"), HEAD),
            P(("batch", "seq"), HEAD),
            P(("batch", "seq"), HEAD),
            P(None, HEAD),
            P(None, HEAD),
            P(None, HEAD),
            P(HEAD),
            P(HEAD),
            P(HEAD, ("batch", "seq")),
            P(("batch", "seq", *HEAD)),
            P(("batch", "seq", *HEAD), None),
            P(("batch", "seq", *HEAD), None),
            P(None, ("batch", "seq", *HEAD)),
        ),
        check_vma=False,
    )
```
